32 devices in a mesh: dp: 2 (over core), seq: 4 (over y, x), tensor: 4 (over z).
Axes of the slice: x: 2, y: 2, z: 4, core: 2. Of those that a mesh axis runs over, the one named last changes fastest.
Arguments:
- hidden: bfloat16 [2, 2112, 2048], P('dp', 'seq'), may hold values from -6 to 6
- teacher: bfloat16 [2, 2112, 2048], P('dp', 'seq'), may hold values from -6 to 6
- valid_length: int32 [2], replicated, may hold values from 1585 to 2112, as said below
- mamba_norm: bfloat16 [2048], P(('dp', 'seq')), may hold values from 0.5 to 1.5
- mamba_in: bfloat16 [2048, 2, 4096], P(('dp', 'seq'), None, 'tensor'), may hold values from -0.125 to 0.125
- conv_kernel: float32 [4, 4096], P(None, 'tensor'), may hold values from -3 to 3
- conv_bias: float32 [4096], P('tensor'), may hold values from -3 to 3
- select_weight: bfloat16 [4096, 160], P('tensor'), may hold values from -0.09375 to 0.09375
- step_weight: bfloat16 [128, 4096], P(None, 'tensor'), may hold values from -0.5 to 0.5
- step_bias: float32 [4096], P('tensor'), may hold values from -7 to -2.5
- decay_log: float32 [16, 4096], P(None, 'tensor'), may hold values from 0 to 2.77
- skip_gain: float32 [4096], P('tensor'), may hold values from 0.5 to 1.5
- mamba_out: bfloat16 [2048, 4096], P(('dp', 'seq'), 'tensor'), may hold values from -0.1875 to 0.1875
- attn_norm: bfloat16 [2048], P(('dp', 'seq')), may hold values from 0.5 to 1.5
- attn_qkv: bfloat16 [2048, 3, 2048], P(('dp', 'seq'), None, 'tensor'), may hold values from -0.125 to 0.125
- attn_out: bfloat16 [2048, 2048], P(('dp', 'seq'), 'tensor'), may hold values from -2 to 2
- first_norm: bfloat16 [2048], P(('dp', 'seq')), may hold values from 0.5 to 1.5
- first_gate_up: bfloat16 [2048, 2, 8192], P(('dp', 'seq'), None, 'tensor'), may hold values from -0.125 to 0.125
- first_down: bfloat16 [2048, 8192], P(('dp', 'seq'), 'tensor'), may hold values from -0.125 to 0.125
- second_norm: bfloat16 [2048], P(('dp', 'seq')), may hold values from 0.5 to 1.5
- second_gate_up: bfloat16 [2048, 2, 8192], P(('dp', 'seq'), None, 'tensor'), may hold values from -0.125 to 0.125
- second_down: bfloat16 [2048, 8192], P(('dp', 'seq'), 'tensor'), may hold values from -0.125 to 0.125
Outputs:
- loss: float32 [], replicated
- output: bfloat16 [2, 2112, 2048], P('dp', 'seq')
- input_grad: float32 [2, 2112, 2048], P('dp', 'seq')
- grad_mamba_norm: float32 [2048], P(('dp', 'seq'))
- grad_mamba_in: float32 [2048, 2, 4096], P(('dp', 'seq'), None, 'tensor')
- grad_conv_kernel: float32 [4, 4096], P(None, 'tensor')
- grad_conv_bias: float32 [4096], P('tensor')
- grad_select_weight: float32 [4096, 160], P('tensor')
- grad_step_weight: float32 [128, 4096], P(None, 'tensor')
- grad_step_bias: float32 [4096], P('tensor')
- grad_decay_log: float32 [16, 4096], P(None, 'tensor')
- grad_skip_gain: float32 [4096], P('tensor')
- grad_mamba_out: float32 [2048, 4096], P(('dp', 'seq'), 'tensor')
- grad_attn_norm: float32 [2048], P(('dp', 'seq'))
- grad_attn_qkv: float32 [2048, 3, 2048], P(('dp', 'seq'), None, 'tensor')
- grad_attn_out: float32 [2048, 2048], P(('dp', 'seq'), 'tensor')
- grad_first_norm: float32 [2048], P(('dp', 'seq'))
- grad_first_gate_up: float32 [2048, 2, 8192], P(('dp', 'seq'), None, 'tensor')
- grad_first_down: float32 [2048, 8192], P(('dp', 'seq'), 'tensor')
- grad_second_norm: float32 [2048], P(('dp', 'seq'))
- grad_second_gate_up: float32 [2048, 2, 8192], P(('dp', 'seq'), None, 'tensor')
- grad_second_down: float32 [2048, 8192], P(('dp', 'seq'), 'tensor')
The draws below stay inside these ranges and needn't reach their ends.
Inputs may be any that keep to these rules, and one draw needn't show every extreme that they name: valid_length[s] counts the leading valid positions of sequence s; in every draw some sequence is valid over all 2112 positions.
All inputs are finite; a program needn't handle non-finite values.
Results may differ from the reference program's by a relative error of at most 0.024.
Values may be sent and summed in bfloat16 or wider, within the bound.
A program may use at most 384 MiB of HBM per device.

```python
import jax
import jax.numpy as jnp
from jax import lax

D = 2048
E = 4096
N = 16
KC = 4
R = 128
H = 32
HD = 64
FF = 8192
WINDOW = 2048
SPAN = 528
SEQS = 2
LEN = 2112
LOSS_SCALE = 4325376
N_SEQ = 4


def draw_valid_length(key, part):
    key = jax.random.fold_in(key, 11)
    length_key, chosen_key = jax.random.split(key)
    counts = jax.random.randint(length_key, (SEQS,), LEN - SPAN + 1, LEN + 1)
    chosen = jax.random.randint(chosen_key, (), 0, SEQS)
    return jnp.where(jnp.arange(SEQS) == chosen, LEN, counts).astype(jnp.int32)


def levels(own_key, dims, cuts, least, largest):
    factor_of, own = 1.0, jax.random.fold_in(own_key, 6)
    for dim, shards_of in cuts:
        draws = jnp.exp(jax.random.uniform(jax.random.fold_in(own, dim), (shards_of,), jnp.float32, least / len(cuts), largest / len(cuts)))
        factor_of = factor_of * jnp.repeat(draws, dims[dim] // shards_of).reshape([-1 if axis == dim else 1 for axis in range(len(dims))])
    return factor_of


def bell_draw(key, extent, deviation, most, shards=(), held_as=jnp.bfloat16):
    values = deviation * jax.random.normal(key, extent, jnp.float32)
    if shards:
        values = values * levels(key, extent, shards, -0.22, 0.18)
    return jnp.clip(values, -most, most).astype(held_as)


def setup_inputs(seed: int = 0) -> dict:
    arg_keys = jax.random.split(jax.random.key(seed), 23)
    hidden = bell_draw(arg_keys[0], (SEQS, LEN, D), 1.0, 6.0, ((0, 2), (1, 4)))
    teacher = bell_draw(arg_keys[1], (SEQS, LEN, D), 1.0, 6.0, ((0, 2), (1, 4)))
    valid_length = draw_valid_length(jax.random.fold_in(arg_keys[22], 71), 0)
    mamba_norm = jnp.clip(1.0 + 0.1 * jax.random.normal(arg_keys[3], (D,), jnp.float32), 0.5, 1.5).astype(jnp.bfloat16)
    mamba_in = bell_draw(arg_keys[4], (D, 2, E), D ** -0.5, 0.125, ((0, 8), (2, 4)))
    conv_kernel = bell_draw(arg_keys[5], (KC, E), KC ** -0.5, 3.0, ((1, 4),), jnp.float32)
    conv_bias = bell_draw(arg_keys[6], (E,), 0.5, 3.0, ((0, 4),), jnp.float32)
    select_weight = bell_draw(arg_keys[7], (E, R + 2 * N), E ** -0.5, 0.09375, ((0, 4),))
    step_weight = bell_draw(arg_keys[8], (R, E), R ** -0.5, 0.5, ((1, 4),))
    step_bias = jnp.clip(-7.0 + 4.5 * jax.random.uniform(arg_keys[9], (E,), jnp.float32) ** levels(arg_keys[9], (E,), ((0, 4),), -0.2, 0.2), -7.0, -2.5)
    decay_log = jnp.clip(2.77 * jax.random.uniform(arg_keys[10], (N, E), jnp.float32) ** levels(arg_keys[10], (N, E), ((1, 4),), -0.2, 0.2), 0.0, 2.77)
    skip_gain = jnp.clip(0.5 + 1.0 * jax.random.uniform(arg_keys[11], (E,), jnp.float32) ** levels(arg_keys[11], (E,), ((0, 4),), -0.2, 0.2), 0.5, 1.5)
    mamba_out = bell_draw(arg_keys[12], (D, E), (E // 4) ** -0.5, 0.1875, ((0, 8), (1, 4)))
    attn_norm = jnp.clip(1.0 + 0.1 * jax.random.normal(arg_keys[13], (D,), jnp.float32), 0.5, 1.5).astype(jnp.bfloat16)
    attn_qkv = bell_draw(arg_keys[14], (D, 3, H * HD), D ** -0.5, 0.125, ((0, 8), (2, 4)))
    attn_out = bell_draw(arg_keys[15], (D, H * HD), (max(1, H * HD // 256)) ** -0.5, 2.0, ((0, 8), (1, 4)))
    first_norm = jnp.clip(1.0 + 0.1 * jax.random.normal(arg_keys[16], (D,), jnp.float32), 0.5, 1.5).astype(jnp.bfloat16)
    first_gate_up = bell_draw(arg_keys[17], (D, 2, FF), D ** -0.5, 0.125, ((0, 8), (2, 4)))
    first_down = bell_draw(arg_keys[18], (D, FF), (FF // 4) ** -0.5, 0.125, ((0, 8), (1, 4)))
    second_norm = jnp.clip(1.0 + 0.1 * jax.random.normal(arg_keys[19], (D,), jnp.float32), 0.5, 1.5).astype(jnp.bfloat16)
    second_gate_up = bell_draw(arg_keys[20], (D, 2, FF), D ** -0.5, 0.125, ((0, 8), (2, 4)))
    second_down = bell_draw(arg_keys[21], (D, FF), (FF // 4) ** -0.5, 0.125, ((0, 8), (1, 4)))
    return {"hidden": hidden, "teacher": teacher, "valid_length": valid_length, "mamba_norm": mamba_norm, "mamba_in": mamba_in, "conv_kernel": conv_kernel, "conv_bias": conv_bias, "select_weight": select_weight, "step_weight": step_weight, "step_bias": step_bias, "decay_log": decay_log, "skip_gain": skip_gain, "mamba_out": mamba_out, "attn_norm": attn_norm, "attn_qkv": attn_qkv, "attn_out": attn_out, "first_norm": first_norm, "first_gate_up": first_gate_up, "first_down": first_down, "second_norm": second_norm, "second_gate_up": second_gate_up, "second_down": second_down}


highest = lax.Precision.HIGHEST
epsilon = 1e-05

@jax.custom_vjp
def low(v):
    return lax.optimization_barrier(v.astype(jnp.bfloat16)).astype(jnp.float32)

@jax.custom_vjp
def low_back(v):
    return v

def low_keep(v):
    return (low(v), None)

def low_pass(kept, grad):
    return (grad,)

def back_keep(v):
    return (v, None)

def back_low(kept, grad):
    return (low(grad),)
low.defvjp(low_keep, low_pass)
low_back.defvjp(back_keep, back_low)

def product(left, right):
    return jnp.dot(left, right, precision=highest)

def product_t(left, right):
    return lax.dot_general(left, right, (((1,), (1,)), ((), ())), precision=highest)

def expand(acting, weight):
    return jnp.einsum('td,dge->tge', acting, weight, precision=highest)

def norm_apply(values, gain_vec):
    return values * lax.rsqrt(lax.optimization_barrier(jnp.mean(values * values, axis=-1, keepdims=True)) + epsilon) * gain_vec

def rotate(values, positions):
    half_dim = values.shape[-1] // 2
    frequency = 10000.0 ** (-jnp.arange(half_dim, dtype=jnp.float32) / half_dim)
    angles = positions.astype(jnp.float32)[:, None] * frequency[None, :]
    cosine = jnp.cos(angles)[:, None, :]
    sine_table = jnp.sin(angles)[:, None, :]
    front_half = values[..., :half_dim]
    back_half = values[..., half_dim:]
    return jnp.concatenate([front_half * cosine - back_half * sine_table, back_half * cosine + front_half * sine_table], axis=-1)

def selective_scan(inputs, step_size, input_map, output_map, decay_rate):
    groups = LEN // 16

    def advance_group(carried, pieces):

        def advance(current, row_items):
            value_row, size_row, in_row, out_row = row_items
            current = jnp.exp(size_row[None, :] * decay_rate) * current + in_row[:, None] * (size_row * value_row)[None, :]
            return (current, lax.optimization_barrier(jnp.sum(out_row[:, None] * current, axis=0)))
        return lax.scan(advance, carried, pieces)
    shaped = tuple((piece.reshape(groups, 16, piece.shape[-1]) for piece in (inputs, step_size, input_map, output_map)))
    final_state, outputs = lax.scan(jax.checkpoint(advance_group), jnp.zeros(decay_rate.shape, jnp.float32), shaped)
    return outputs.reshape(LEN, decay_rate.shape[1])

def mamba_branch(stream, mamba_norm, mamba_in, conv_kernel, conv_bias, select_weight, step_weight, step_bias, decay_log, skip_gain, mamba_out):
    acting = low(norm_apply(stream, mamba_norm))
    projected = low_back(low(expand(acting, mamba_in)))
    conv_input = projected[:, 0]
    gate_input = projected[:, 1]
    padded = jnp.concatenate([jnp.zeros((KC - 1, E), jnp.float32), conv_input], axis=0)
    conv_pre = conv_bias
    for tap_index in range(KC):
        conv_pre = conv_pre + conv_kernel[tap_index] * padded[tap_index:tap_index + LEN]
    inputs = low(jax.nn.silu(conv_pre))
    selected = low_back(product(inputs, select_weight))
    step_in = low(selected[:, :R])
    input_map = selected[:, R:R + N]
    output_map = selected[:, R + N:]
    step_size = jax.nn.softplus(low_back(product(step_in, step_weight)) + step_bias)
    decay_rate = -jnp.exp(decay_log)
    scanned = selective_scan(inputs, step_size, input_map, output_map, decay_rate) + skip_gain * inputs
    gated_low = low(scanned * jax.nn.silu(gate_input))
    return low_back(product_t(gated_low, mamba_out))

def attention_branch(stream, attn_norm, attn_qkv, attn_out):
    acting = low(norm_apply(stream, attn_norm))
    projected = low_back(expand(acting, attn_qkv))
    positions = jnp.arange(LEN, dtype=jnp.int32)
    queries = low_back(low(rotate(projected[:, 0].reshape(LEN, H, HD), positions)))
    key_rows = low_back(low(rotate(projected[:, 1].reshape(LEN, H, HD), positions)))
    values = low_back(low(projected[:, 2].reshape(LEN, H, HD)))
    scaling = HD ** (-0.5)

    def attend_block(row_start):
        query_rows = lax.dynamic_slice_in_dim(queries, row_start, SPAN, 0)
        scores = low_back(jnp.einsum('qhd,khd->hqk', query_rows, key_rows, precision=highest) * scaling)
        distance = (row_start + jnp.arange(SPAN, dtype=jnp.int32))[:, None] - positions[None, :]
        visible = (distance >= 0) & (distance < WINDOW)
        scores = jnp.where(visible[None], scores, -1e+30)
        row_top = lax.optimization_barrier(jnp.max(scores, axis=-1, keepdims=True))
        exponent = jnp.exp(scores - row_top)
        soft_weights = low(exponent / lax.optimization_barrier(jnp.sum(exponent, axis=-1, keepdims=True)))
        return jnp.einsum('hqk,khd->qhd', soft_weights, values, precision=highest)
    starts = (jnp.arange(N_SEQ) * SPAN).astype(jnp.int32)
    attended = lax.map(jax.checkpoint(attend_block), starts).reshape(LEN, H * HD)
    return low_back(product_t(low_back(low(attended)), attn_out))

def ffn_branch(stream, gain_vec, gate_up, down_weight):
    acting = low(norm_apply(stream, gain_vec))
    projected = low_back(expand(acting, gate_up))
    hidden_units = low(jax.nn.silu(projected[:, 0]) * projected[:, 1])
    return low_back(product_t(hidden_units, down_weight))

def reference(hidden, teacher, valid_length, mamba_norm, mamba_in, conv_kernel, conv_bias, select_weight, step_weight, step_bias, decay_log, skip_gain, mamba_out, attn_norm, attn_qkv, attn_out, first_norm, first_gate_up, first_down, second_norm, second_gate_up, second_down):
    params = tuple((weight.astype(jnp.float32) for weight in (mamba_norm, mamba_in, conv_kernel, conv_bias, select_weight, step_weight, step_bias, decay_log, skip_gain, mamba_out, attn_norm, attn_qkv, attn_out, first_norm, first_gate_up, first_down, second_norm, second_gate_up, second_down)))
    streams = hidden.astype(jnp.float32)
    targets = teacher.astype(jnp.float32)
    valid_total = jnp.sum(valid_length).astype(jnp.float32)
    positions = jnp.arange(LEN, dtype=jnp.int32)

    def objective(weights, inputs_all):
        mamba_weights = weights[:10]
        attn_weights = weights[10:13]
        first_weights = weights[13:16]
        second_weights = weights[16:19]

        def one_sequence(running, pieces):
            stream, target, length = pieces
            stream = stream + mamba_branch(stream, *mamba_weights)
            stream = stream + attention_branch(stream, *attn_weights)
            stream = stream + ffn_branch(stream, *first_weights)
            stream = stream + ffn_branch(stream, *second_weights)
            residue = jnp.where((positions < length)[:, None], stream - target, 0.0)
            return (running + jnp.sum(residue * residue), stream)
        running, outputs = lax.scan(one_sequence, jnp.zeros((), jnp.float32), (inputs_all, targets, valid_length))
        return (outputs, running / (D * valid_total))
    (outputs, loss_value), pullback = jax.vjp(objective, params, streams)
    weight_grads, input_grad = pullback((jnp.zeros_like(outputs), jnp.asarray(LOSS_SCALE, jnp.float32)))
    grad_mamba_norm, grad_mamba_in, grad_conv_kernel, grad_conv_bias, grad_select_weight, grad_step_weight, grad_step_bias, grad_decay_log, grad_skip_gain, grad_mamba_out, grad_attn_norm, grad_attn_qkv, grad_attn_out, grad_first_norm, grad_first_gate_up, grad_first_down, grad_second_norm, grad_second_gate_up, grad_second_down = weight_grads
    return (loss_value, outputs.astype(jnp.bfloat16), input_grad, grad_mamba_norm, grad_mamba_in, grad_conv_kernel, grad_conv_bias, grad_select_weight, grad_step_weight, grad_step_bias, grad_decay_log, grad_skip_gain, grad_mamba_out, grad_attn_norm, grad_attn_qkv, grad_attn_out, grad_first_norm, grad_first_gate_up, grad_first_down, grad_second_norm, grad_second_gate_up, grad_second_down)
```

```python
import functools

import jax
import jax.numpy as jnp
from jax import lax
from jax.experimental import pallas as pl
from jax.experimental.pallas import tpu as pltpu
from jax.sharding import PartitionSpec as P

HD = 64
WINDOW = 2048
F32 = jnp.float32
BF16 = jnp.bfloat16
MESH = pl.DeviceIdType.MESH
LOG2E = 1.4426950408889634
LN2 = 0.6931471805599453

epsilon = 1e-05


def lasting(microseconds):
    return pl.CostEstimate(flops=int(microseconds * 1e7), bytes_accessed=0, transcendentals=0)

head_groups = 2


def state_kernel(dt_ref, dtx_ref, b_ref, rate_ref, out_ref, *, wide, chunk):
    @pl.when(pl.program_id(0) == 0)
    def _():
        out_ref[...] = jnp.zeros_like(out_ref)
    for j in range(out_ref.shape[1] // wide):
        cols = pl.ds(j * wide, wide)
        rate = rate_ref[:, cols]
        def group(g, h):
            base = pl.multiple_of(g * 8, 8)
            dts = dt_ref[pl.ds(base, 8), cols]
            dtxs = dtx_ref[pl.ds(base, 8), cols]
            for r in range(8):
                b = b_ref[base + r]
                b = jnp.concatenate([b] * (wide // 128), axis=1)
                h = jnp.exp2(dts[r:r+1] * rate) * h + b * dtxs[r:r+1]
            return h
        out_ref[:, cols] = lax.fori_loop(0, chunk // 8, group, out_ref[:, cols])

def scan_kernel(dt_ref, dtx_ref, b_ref, c_ref, rate_ref, h0_ref, y_ref, hp_ref, h_ref, *, wide, chunk):
    @pl.when(pl.program_id(0) == 0)
    def _():
        h_ref[...] = h0_ref[...]
    for j in range(h_ref.shape[1] // wide):
        cols = pl.ds(j * wide, wide)
        rate = rate_ref[:, cols]
        def group(g, h):
            base = pl.multiple_of(g * 8, 8)
            dts = dt_ref[pl.ds(base, 8), cols]
            dtxs = dtx_ref[pl.ds(base, 8), cols]
            ys = []
            for r in range(8):
                b = jnp.concatenate([b_ref[base + r]] * (wide // 128), axis=1)
                c = jnp.concatenate([c_ref[base + r]] * (wide // 128), axis=1)
                hp_ref[base + r, :, cols] = h
                h = jnp.exp2(dts[r:r+1] * rate) * h + b * dtxs[r:r+1]
                ys.append(jnp.sum(c * h, axis=0, keepdims=True))
            y_ref[pl.ds(base, 8), cols] = jnp.concatenate(ys, axis=0)
            return h
        h_ref[:, cols] = lax.fori_loop(0, chunk // 8, group, h_ref[:, cols])

def back_state_kernel(dt_ref, g_ref, c_ref, rate_ref, out_ref, *, wide, chunk):
    @pl.when(pl.program_id(0) == 0)
    def _():
        out_ref[...] = jnp.zeros_like(out_ref)
    for j in range(out_ref.shape[1] // wide):
        cols = pl.ds(j * wide, wide)
        rate = rate_ref[:, cols]
        def group(g, carry):
            base = pl.multiple_of(chunk - 8 - g * 8, 8)
            dts = dt_ref[pl.ds(base, 8), cols]
            gs = g_ref[pl.ds(base, 8), cols]
            for r in reversed(range(8)):
                c = jnp.concatenate([c_ref[base + r]] * (wide // 128), axis=1)
                carry = jnp.exp2(dts[r:r+1] * rate) * (carry + c * gs[r:r+1])
            return carry
        out_ref[:, cols] = lax.fori_loop(0, chunk // 8, group, out_ref[:, cols])

def back_kernel(dt_ref, x_ref, g_ref, b_ref, c_ref, rate_ref, hp_ref, l0_ref,
                gdt_ref, gx_ref, gb_out, gc_out, grate_ref, l_ref, gb_ref, gc_ref, *, wide, chunk):
    @pl.when(pl.program_id(0) == 0)
    def _():
        l_ref[...] = l0_ref[...]
        grate_ref[...] = jnp.zeros_like(grate_ref)
    for j in range(l_ref.shape[1] // wide):
        cols = pl.ds(j * wide, wide)
        rate = rate_ref[:, cols]
        def fold(v):
            out = v[:, :128]
            for i in range(1, wide // 128):
                out = out + v[:, i * 128:(i + 1) * 128]
            return out
        def group(g, state):
            carry, grate = state
            base = pl.multiple_of(chunk - 8 - g * 8, 8)
            dts = dt_ref[pl.ds(base, 8), cols]
            xs = x_ref[pl.ds(base, 8), cols].astype(F32)
            gs = g_ref[pl.ds(base, 8), cols]
            dtxs = dts * xs
            sw = [None] * 8
            sb = [None] * 8
            for r in reversed(range(8)):
                b = jnp.concatenate([b_ref[base + r]] * (wide // 128), axis=1)
                c = jnp.concatenate([c_ref[base + r]] * (wide // 128), axis=1)
                dt = dts[r:r+1]
                dtx = dtxs[r:r+1]
                gr = gs[r:r+1]
                da = jnp.exp2(dt * rate)
                q = da * hp_ref[base + r, :, cols]
                h = q + b * dtx
                lam = c * gr + carry
                w = lam * q
                carry = lam * da
                gb = fold(lam * dtx)
                gc = fold(h * gr)
                if j == 0:
                    gb_ref[base + r] = gb
                    gc_ref[base + r] = gc
                else:
                    gb_ref[base + r] += gb
                    gc_ref[base + r] += gc
                grate = grate + w * dt
                sw[r] = jnp.sum(w * rate, axis=0, keepdims=True)
                sb[r] = jnp.sum(lam * b, axis=0, keepdims=True)
            sbs = jnp.concatenate(sb, axis=0)
            sws = jnp.concatenate(sw, axis=0)
            gdt_ref[pl.ds(base, 8), cols] = sws * LN2 + xs * sbs
            gx_ref[pl.ds(base, 8), cols] = dts * sbs
            return carry, grate
        carry, grate = lax.fori_loop(0, chunk // 8, group, (l_ref[:, cols], grate_ref[:, cols]))
        l_ref[:, cols] = carry
        grate_ref[:, cols] = grate
    gb_out[...] = jnp.sum(gb_ref[...], axis=2)
    gc_out[...] = jnp.sum(gc_ref[...], axis=2)


SCAN_WIDE = 512


def scan_calls(rows, width, states):
    chunk = max(c for c in range(8, 57, 8) if rows % c == 0)
    steps = rows // chunk
    lanes = 128
    row = pl.BlockSpec((chunk, width), lambda i: (i, 0))
    maps = pl.BlockSpec((chunk, states, lanes), lambda i: (i, 0, 0))
    whole = pl.BlockSpec((states, width), lambda i: (0, 0))
    kept = pl.BlockSpec((chunk, states, width), lambda i: (i, 0, 0))
    row_back = pl.BlockSpec((chunk, width), lambda i: (steps - 1 - i, 0))
    maps_back = pl.BlockSpec((chunk, states, lanes), lambda i: (steps - 1 - i, 0, 0))
    narrow_back = pl.BlockSpec((chunk, states), lambda i: (steps - 1 - i, 0))
    kept_back = pl.BlockSpec((chunk, states, width), lambda i: (steps - 1 - i, 0, 0))

    def shape(*sizes):
        return jax.ShapeDtypeStruct(sizes, F32)

    params = pltpu.CompilerParams(vmem_limit_bytes=40 * 2**20)
    sizes = dict(wide=min(SCAN_WIDE, width), chunk=chunk)
    carried = [pltpu.VMEM((states, width), F32)]
    cells = rows * width * states
    state = pl.pallas_call(
        functools.partial(state_kernel, **sizes),
        grid=(steps,),
        in_specs=[row, row, maps, whole],
        out_specs=whole,
        out_shape=shape(states, width),
        compiler_params=params,
        cost_estimate=lasting(7),
        name="scan_state",
    )
    scan = pl.pallas_call(
        functools.partial(scan_kernel, **sizes),
        grid=(steps,),
        in_specs=[row, row, maps, maps, whole, whole],
        out_specs=[row, kept],
        out_shape=[shape(rows, width), shape(rows, states, width)],
        scratch_shapes=carried,
        compiler_params=params,
        cost_estimate=lasting(18),
        name="scan_rows",
    )
    back_state = pl.pallas_call(
        functools.partial(back_state_kernel, **sizes),
        grid=(steps,),
        in_specs=[row_back, row_back, maps_back, whole],
        out_specs=whole,
        out_shape=shape(states, width),
        compiler_params=params,
        cost_estimate=lasting(7),
        name="scan_back_state",
    )
    back = pl.pallas_call(
        functools.partial(back_kernel, **sizes),
        grid=(steps,),
        in_specs=[row_back, row_back, row_back, maps_back, maps_back, whole, kept_back, whole],
        out_specs=[row_back, row_back, narrow_back, narrow_back, whole],
        out_shape=[
            shape(rows, width),
            shape(rows, width),
            shape(rows, states),
            shape(rows, states),
            shape(states, width),
        ],
        scratch_shapes=carried + [pltpu.VMEM((chunk, states, lanes), F32)] * 2,
        compiler_params=params,
        cost_estimate=lasting(36),
        name="scan_back",
    )
    return state, scan, back_state, back


def gather_kernel(block_ref, out_ref, send, recv, own, *, axes):
    sizes = [lax.axis_size(a) for a in axes]
    total = 1
    for size in sizes:
        total *= size
    me = lax.axis_index(axes[0])
    for a in axes[1:]:
        me = me * lax.axis_size(a) + lax.axis_index(a)

    def coordinates(index):
        found = {}
        for a, size in zip(reversed(axes), reversed(sizes)):
            found[a] = lax.rem(index, size)
            index = index // size
        return found

    barrier = pltpu.get_barrier_semaphore()
    for step in range(1, total):
        pl.semaphore_signal(
            barrier, inc=1, device_id=coordinates(lax.rem(me + step, total)), device_id_type=MESH
        )
    pl.semaphore_wait(barrier, total - 1)
    mine = pltpu.make_async_copy(block_ref, out_ref.at[me], own)
    mine.start()
    copies = []
    for step in range(1, total):
        copy = pltpu.make_async_remote_copy(
            block_ref,
            out_ref.at[me],
            send.at[step],
            recv.at[step],
            device_id=coordinates(lax.rem(me + step, total)),
            device_id_type=MESH,
        )
        copy.start()
        copies.append(copy)
    mine.wait()
    for step in range(1, total):
        source = lax.rem(me - step + total, total)
        pltpu.make_async_remote_copy(
            block_ref,
            out_ref.at[source],
            send.at[step],
            recv.at[step],
            device_id=coordinates(source),
            device_id_type=MESH,
        ).wait_recv()
    for copy in copies:
        copy.wait_send()


def direct_gather(block, axes, identifier):
    total = 1
    for a in axes:
        total *= lax.axis_size(a)
    whole = pl.BlockSpec(memory_space=pltpu.VMEM)
    return pl.pallas_call(
        functools.partial(gather_kernel, axes=axes),
        out_shape=jax.ShapeDtypeStruct((total,) + block.shape, block.dtype),
        in_specs=[whole],
        out_specs=whole,
        scratch_shapes=[
            pltpu.SemaphoreType.DMA((total,)),
            pltpu.SemaphoreType.DMA((total,)),
            pltpu.SemaphoreType.DMA,
        ],
        compiler_params=pltpu.CompilerParams(
            collective_id=identifier, has_side_effects=True, vmem_limit_bytes=24 * 2**20
        ),
        name="gather_" + "_".join(axes),
        cost_estimate=lasting(6),
    )(block)


def ar_kernel(x_ref, out_ref, a_buf, b_buf, s_buf, a_send, a_recv, b_send, b_recv, c_send, c_recv, *, pieces, rows, lag):
    z = lax.axis_index("tensor")
    size = lax.axis_size("tensor")
    half = size // 2
    inner = (z == half - 1) | (z == half)
    low = z < half
    outer_dev = jnp.where(low, half - 2, half + 1)
    inner_dev = jnp.where(low, half - 1, half)
    other = jnp.where(low, half, half - 1)
    barrier = pltpu.get_barrier_semaphore()

    def at(ref, k):
        return ref.at[pl.ds(k * rows, rows)]

    def send_a(k):
        return pltpu.make_async_remote_copy(at(x_ref, k), at(a_buf, k), a_send.at[k], a_recv.at[k], device_id={"tensor": inner_dev}, device_id_type=MESH)
    def send_b(k):
        return pltpu.make_async_remote_copy(at(s_buf, k), at(b_buf, k), b_send.at[k], b_recv.at[k], device_id={"tensor": other}, device_id_type=MESH)
    def send_c(k):
        return pltpu.make_async_remote_copy(at(out_ref, k), at(out_ref, k), c_send.at[k], c_recv.at[k], device_id={"tensor": outer_dev}, device_id_type=MESH)

    @pl.when(jnp.logical_not(inner))
    def _():
        pl.semaphore_signal(barrier, inc=1, device_id={"tensor": inner_dev}, device_id_type=MESH)
        pl.semaphore_wait(barrier, 1)
        for k in range(pieces):
            send_a(k).start()
        for k in range(pieces):
            send_c(k).wait_recv()
        for k in range(pieces):
            send_a(k).wait_send()

    @pl.when(inner)
    def _():
        pl.semaphore_signal(barrier, inc=1, device_id={"tensor": outer_dev}, device_id_type=MESH)
        pl.semaphore_signal(barrier, inc=1, device_id={"tensor": other}, device_id_type=MESH)
        pl.semaphore_wait(barrier, 2)
        for t in range(pieces + lag):
            if t < pieces:
                send_a(t).wait_recv()
                part = pl.ds(t * rows, rows)
                s_buf[part] = (x_ref[part].astype(F32) + a_buf[part].astype(F32)).astype(BF16)
                send_b(t).start()
            if t >= lag:
                k = t - lag
                send_b(k).wait_recv()
                part = pl.ds(k * rows, rows)
                out_ref[part] = (s_buf[part].astype(F32) + b_buf[part].astype(F32)).astype(BF16)
                send_c(k).start()
        for k in range(pieces):
            send_b(k).wait_send()
            send_c(k).wait_send()


def tensor_sum(partial_sum, pieces, identifier):
    rows, width = partial_sum.shape
    lag = min(3, pieces)
    whole = pl.BlockSpec(memory_space=pltpu.VMEM)
    return pl.pallas_call(
        functools.partial(ar_kernel, pieces=pieces, rows=rows // pieces, lag=lag),
        out_shape=jax.ShapeDtypeStruct((rows, width), BF16),
        in_specs=[whole],
        out_specs=whole,
        scratch_shapes=[pltpu.VMEM((rows, width), BF16)] * 3
        + [pltpu.SemaphoreType.DMA((pieces,))] * 6,
        compiler_params=pltpu.CompilerParams(
            collective_id=identifier, has_side_effects=True, vmem_limit_bytes=24 * 2**20
        ),
        name="tensor_sum",
        cost_estimate=lasting(16),
    )(partial_sum)


def shifted(block, axis, distance):
    devices = range(lax.axis_size(axis))
    route = [(i - distance, i) for i in devices if i - distance in devices]
    return lax.ppermute(block, axis, route)


def product(left, right):
    return jnp.dot(left, right, preferred_element_type=F32)


def product_t(left, right):
    return lax.dot_general(
        left, right, (((1,), (1,)), ((), ())), preferred_element_type=F32
    )


def product_tl(left, right):
    return lax.dot_general(
        left, right, (((0,), (0,)), ((), ())), preferred_element_type=F32
    )


def norm_forward(values, gain_vec):
    inv_rms = lax.rsqrt(jnp.mean(values * values, axis=-1, keepdims=True) + epsilon)
    return values * inv_rms * gain_vec


def silu_slope(values):
    sigmoid_val = jax.nn.sigmoid(values)
    return sigmoid_val * (1.0 + values * (1.0 - sigmoid_val))


def join(*matrices):
    rows = matrices[0].shape[0]
    return jnp.concatenate([matrix.reshape(rows, -1) for matrix in matrices], axis=1)


def gather_joined(joined):
    return lax.all_gather(joined, ("dp", "seq"), axis=0, tiled=True)


def tensor_forward_sum(partial_sum):
    rows, width = partial_sum.shape
    low = partial_sum.astype(BF16)
    if width % 128:
        padded = jnp.pad(low, ((0, 0), (0, -width % 128)))
        return tensor_sum(padded, 11, 1)[:, :width].astype(F32)
    return tensor_sum(low, 33, 0).astype(F32)


tensor_backward_sum = tensor_forward_sum


def nt(a, b):
    return lax.dot_general(a, b, (((1,), (1,)), ((), ())), preferred_element_type=F32)

def nn(a, b):
    return lax.dot_general(a, b, (((1,), (0,)), ((), ())), preferred_element_type=F32)

def tn(a, b):
    return lax.dot_general(a, b, (((0,), (0,)), ((), ())), preferred_element_type=F32)

def head_lanes(shape, head):
    lane = lax.broadcasted_iota(jnp.int32, shape, 1)
    return (lane >= HD) if head else (lane < HD)

def seen(shape, hop, rows, query_axis):
    if hop * rows - (rows - 1) >= 0 and hop * rows + rows - 1 < WINDOW:
        return None
    distance = hop * rows + lax.broadcasted_iota(jnp.int32, shape, query_axis) - lax.broadcasted_iota(jnp.int32, shape, 1 - query_axis)
    return (distance >= 0) & (distance < WINDOW)

def seq_greet(place, count):
    barrier = pltpu.get_barrier_semaphore()
    for step in range(1, count):
        pl.semaphore_signal(
            barrier, inc=1, device_id={"seq": lax.rem(place + step, count)}, device_id_type=MESH
        )
    pl.semaphore_wait(barrier, count - 1)


def attend_kernel(
    q_ref, kv_ref, acc_ref, low_ref, top_ref, far_ref, total_ref, send, recv, *, count, hop_count
):
    rows = q_ref.shape[0]
    pairs = top_ref.shape[0]
    place = lax.axis_index("seq")
    scale = LOG2E * HD**-0.5
    seq_greet(place, count)

    def move(hop, device):
        return pltpu.make_async_remote_copy(
            kv_ref,
            far_ref.at[hop - 1],
            send.at[hop - 1],
            recv.at[hop - 1],
            device_id={"seq": device},
            device_id_type=MESH,
        )

    for hop in range(1, hop_count + 1):

        @pl.when(place + hop < count)
        def _(hop=hop):
            move(hop, place + hop).start()

    low = head_lanes((rows, 128), 0)

    def one_block(hop, pair):
        cols = pl.ds(pl.multiple_of(pair * 128, 128), 128)
        q = q_ref[:, cols]
        keys = kv_ref[0, :, cols] if hop == 0 else far_ref[hop - 1, 0, :, cols]
        values = kv_ref[1, :, cols] if hop == 0 else far_ref[hop - 1, 1, :, cols]
        mask = seen((rows, rows), hop, rows, 0)
        outs = []
        tops = []
        for head in range(2):
            mine = low if head == 0 else jnp.logical_not(low)
            s = nt(jnp.where(mine, q, jnp.zeros_like(q)), keys)
            if mask is not None:
                s = jnp.where(mask, s, -1e30)
            top = jnp.max(s, axis=1, keepdims=True)
            if hop > 0:
                top = jnp.maximum(top, top_ref[pair, :, pl.ds(head * HD, 1)])
            p = jnp.exp2((s - top) * scale).astype(BF16)
            outs.append(nn(p, jnp.where(mine, values, jnp.ones_like(values))))
            tops.append(top)
        top = jnp.where(low, tops[0], tops[1])
        acc = jnp.where(low, outs[0], outs[1])
        total = pltpu.roll(jnp.where(low, outs[1], outs[0]), HD, 1)
        if hop > 0:
            fade = jnp.exp2((top_ref[pair] - top) * scale)
            acc = acc + acc_ref[:, cols] * fade
            total = total + total_ref[pair] * fade
        acc_ref[:, cols] = acc
        top_ref[pair] = top
        total_ref[pair] = total

    def all_pairs(hop):
        def one(pair, carry):
            one_block(hop, pair)
            return carry

        lax.fori_loop(0, pairs, one, 0)

    all_pairs(0)
    for hop in range(1, hop_count + 1):

        @pl.when(place >= hop)
        def _(hop=hop):
            move(hop, place - hop).wait_recv()
            all_pairs(hop)

    def finish(pair, carry):
        cols = pl.ds(pl.multiple_of(pair * 128, 128), 128)
        total = total_ref[pair]
        acc = acc_ref[:, cols] / total
        acc_ref[:, cols] = acc
        low_ref[:, cols] = acc.astype(BF16)
        top_ref[pair] = top_ref[pair] * scale + jnp.log2(total)
        return carry

    lax.fori_loop(0, pairs, finish, 0)
    for hop in range(1, hop_count + 1):

        @pl.when(place + hop < count)
        def _(hop=hop):
            move(hop, place + hop).wait_send()


def attend(q, kv, hop_count, identifier):
    rows, width = q.shape
    pairs = width // 128
    whole = pl.BlockSpec(memory_space=pltpu.VMEM)
    return pl.pallas_call(
        functools.partial(attend_kernel, count=lax.axis_size("seq"), hop_count=hop_count),
        in_specs=[whole] * 2,
        out_specs=[whole] * 4,
        out_shape=[
            jax.ShapeDtypeStruct((rows, width), F32),
            jax.ShapeDtypeStruct((rows, width), BF16),
            jax.ShapeDtypeStruct((pairs, rows, 128), F32),
            jax.ShapeDtypeStruct((hop_count, 2, rows, width), BF16),
        ],
        scratch_shapes=[
            pltpu.VMEM((pairs, rows, 128), F32),
            pltpu.SemaphoreType.DMA((hop_count,)),
            pltpu.SemaphoreType.DMA((hop_count,)),
        ],
        compiler_params=pltpu.CompilerParams(
            collective_id=identifier, has_side_effects=True, vmem_limit_bytes=48 * 2**20
        ),
        cost_estimate=lasting(55),
        name="attend",
    )(q, kv)


def attend_back_kernel(
    q_ref,
    g_ref,
    o_ref,
    lse_ref,
    kv_ref,
    far_ref,
    cosine_ref,
    sine_ref,
    out_ref,
    lines,
    dq_ref,
    dkv_ref,
    leaving,
    landed,
    send,
    recv,
    *,
    count,
    hop_count,
):
    rows, width = q_ref.shape
    pairs = width // 128
    place = lax.axis_index("seq")
    scale = HD**-0.5
    seq_greet(place, count)

    def columns(pair):
        return pl.ds(pl.multiple_of(pair * 128, 128), 128)

    def move(hop, pair, device):
        return pltpu.make_async_remote_copy(
            leaving.at[hop - 1, :, :, columns(pair)],
            landed.at[hop - 1, :, :, columns(pair)],
            send.at[hop - 1, pair],
            recv.at[hop - 1, pair],
            device_id={"seq": device},
            device_id_type=MESH,
        )

    def prepare(pair, carry):
        cols = columns(pair)
        turned = jnp.transpose(lse_ref[pair])
        dots = jnp.transpose(o_ref[:, cols] * g_ref[:, cols].astype(F32))
        lines[pair, 0:1] = turned[0:1]
        lines[pair, 1:2] = turned[HD : HD + 1]
        lines[pair, 2:3] = jnp.sum(dots[:HD], axis=0, keepdims=True)
        lines[pair, 3:4] = jnp.sum(dots[HD:], axis=0, keepdims=True)
        dq_ref[:, cols] = jnp.zeros((rows, 128), F32)
        return carry

    lax.fori_loop(0, pairs, prepare, 0)

    def one_block(hop, pair):
        cols = columns(pair)
        q = q_ref[:, cols]
        g = g_ref[:, cols]
        k = kv_ref[0, :, cols] if hop == 0 else far_ref[hop - 1, 0, :, cols]
        v = kv_ref[1, :, cols] if hop == 0 else far_ref[hop - 1, 1, :, cols]
        mask = seen((rows, rows), hop, rows, 1)
        dk = jnp.zeros((rows, 128), F32)
        dv = jnp.zeros((rows, 128), F32)
        dq = dq_ref[:, cols]
        for head in range(2):
            mine = head_lanes((rows, 128), head)
            qm = jnp.where(mine, q, jnp.zeros_like(q))
            gm = jnp.where(mine, g, jnp.zeros_like(g))
            km = jnp.where(mine, k, jnp.zeros_like(k))
            s = nt(k, qm) * (LOG2E * scale)
            p = jnp.exp2(s - lines[pair, head : head + 1])
            if mask is not None:
                p = jnp.where(mask, p, 0.0)
            dv = dv + nn(p.astype(BF16), gm)
            dp = nt(v, gm)
            ds = (p * (dp - lines[pair, head + 2 : head + 3])).astype(BF16)
            dk = dk + nn(ds, qm)
            dq = dq + tn(ds, km) * scale
        dq_ref[:, cols] = dq
        return dk * scale, dv

    for hop in reversed(range(1, hop_count + 1)):

        @pl.when(place >= hop)
        def _(hop=hop):
            def one(pair, carry):
                dk, dv = one_block(hop, pair)
                leaving[hop - 1, 0, :, columns(pair)] = dk.astype(BF16)
                leaving[hop - 1, 1, :, columns(pair)] = dv.astype(BF16)
                move(hop, pair, place - hop).start()
                return carry

            lax.fori_loop(0, pairs, one, 0)

    def own(pair, carry):
        dk, dv = one_block(0, pair)
        dkv_ref[0, :, columns(pair)] = dk
        dkv_ref[1, :, columns(pair)] = dv
        return carry

    lax.fori_loop(0, pairs, own, 0)

    for hop in range(1, hop_count + 1):

        @pl.when(place + hop < count)
        def _(hop=hop):
            def one(pair, carry):
                cols = columns(pair)
                move(hop, pair, place + hop).wait_recv()
                for which in range(2):
                    dkv_ref[which, :, cols] += landed[hop - 1, which, :, cols].astype(F32)
                return carry

            lax.fori_loop(0, pairs, one, 0)

    def finish(pair, carry):
        cols = columns(pair)
        cosine, sine = cosine_ref[...], sine_ref[...]

        def turned(values):
            return turn(values.astype(BF16).astype(F32), cosine, sine, -1.0).astype(BF16)

        def later(part):
            return pl.ds(pl.multiple_of(part * width + pair * 128, 128), 128)

        out_ref[:, cols] = turned(dq_ref[:, cols])
        out_ref[:, later(1)] = turned(dkv_ref[0, :, cols])
        out_ref[:, later(2)] = dkv_ref[1, :, cols].astype(BF16)
        return carry

    lax.fori_loop(0, pairs, finish, 0)
    for hop in range(1, hop_count + 1):

        @pl.when(place >= hop)
        def _(hop=hop):
            def one(pair, carry):
                move(hop, pair, place - hop).wait_send()
                return carry

            lax.fori_loop(0, pairs, one, 0)


def attend_back(q, g, o, lse, kv, far, cosine, sine, identifier):
    rows, width = q.shape
    pairs = width // 128
    hop_count = far.shape[0]
    whole = pl.BlockSpec(memory_space=pltpu.VMEM)
    return pl.pallas_call(
        functools.partial(attend_back_kernel, count=lax.axis_size("seq"), hop_count=hop_count),
        in_specs=[whole] * 8,
        out_specs=whole,
        out_shape=jax.ShapeDtypeStruct((rows, 3 * width), BF16),
        scratch_shapes=[
            pltpu.VMEM((pairs, 8, rows), F32),
            pltpu.VMEM((rows, width), F32),
            pltpu.VMEM((2, rows, width), F32),
            pltpu.VMEM((hop_count, 2, rows, width), BF16),
            pltpu.VMEM((hop_count, 2, rows, width), BF16),
            pltpu.SemaphoreType.DMA((hop_count, pairs)),
            pltpu.SemaphoreType.DMA((hop_count, pairs)),
        ],
        compiler_params=pltpu.CompilerParams(
            collective_id=identifier, has_side_effects=True, vmem_limit_bytes=48 * 2**20
        ),
        cost_estimate=lasting(55),
        name="attend_back",
    )(q, g, o, lse, kv, far, cosine, sine)


def partners(values):
    lane = lax.broadcasted_iota(jnp.int32, values.shape, 1)
    half = HD // 2
    return jnp.where(
        lax.rem(lane, HD) < half, pltpu.roll(values, 128 - half, 1), pltpu.roll(values, half, 1)
    )


def turn(values, cosine, sine, sign):
    parts = []
    for first in range(0, values.shape[1], 128):
        piece = values[:, first : first + 128]
        parts.append(piece * cosine + partners(piece) * (sine * sign))
    return jnp.concatenate(parts, axis=1) if len(parts) > 1 else parts[0]


def rope_tables(positions):
    half = HD // 2
    frequency = 10000.0 ** (-jnp.arange(half, dtype=F32) / half)
    angles = positions.astype(F32)[:, None] * frequency[None, :]
    cosine, sine = jnp.cos(angles), jnp.sin(angles)
    return jnp.tile(cosine, (1, 4)), jnp.tile(jnp.concatenate([-sine, sine], axis=1), (1, 2))


def qkv_kernel(x_ref, w_ref, cosine_ref, sine_ref, q_ref, kv_ref, *, tiles):
    step = pl.program_id(0)
    result = nn(x_ref[...], w_ref[...])
    turned = turn(result, cosine_ref[...], sine_ref[...], 1.0)

    @pl.when(step < tiles)
    def _():
        q_ref[...] = turned.astype(BF16)

    @pl.when(step >= tiles)
    def _():
        kv_ref[0] = jnp.where(step < 2 * tiles, turned, result).astype(BF16)


def qkv_rows(x, w, first_column, width, cosine, sine):
    rows, depth = x.shape
    tile = 256
    tiles = width // tile
    skip = first_column // tile
    table = pl.BlockSpec((rows, 128), lambda j: (0, 0))

    def kv_at(j):
        later = jnp.maximum(j - tiles, 0)
        return later // tiles, 0, lax.rem(later, tiles)

    return pl.pallas_call(
        functools.partial(qkv_kernel, tiles=tiles),
        grid=(3 * tiles,),
        in_specs=[
            pl.BlockSpec((rows, depth), lambda j: (0, 0)),
            pl.BlockSpec((depth, tile), lambda j: (0, j + skip)),
            table,
            table,
        ],
        out_specs=[
            pl.BlockSpec((rows, tile), lambda j: (0, jnp.minimum(j, tiles - 1))),
            pl.BlockSpec((1, rows, tile), kv_at),
        ],
        out_shape=[
            jax.ShapeDtypeStruct((rows, width), BF16),
            jax.ShapeDtypeStruct((2, rows, width), BF16),
        ],
        compiler_params=pltpu.CompilerParams(vmem_limit_bytes=32 * 2**20),
        cost_estimate=lasting(8),
        name="qkv_rows",
    )(x, w, cosine, sine)


def sigmoid(v):
    return 1.0 / (1.0 + jnp.exp(-v))

def gate_up_kernel(x_ref, wg_ref, wu_ref, gate_ref, up_ref, hid_ref):
    x = x_ref[...]
    gate = nn(x, wg_ref[...])
    up = nn(x, wu_ref[...])
    gate_ref[...] = gate.astype(BF16)
    up_ref[...] = up.astype(BF16)
    hid_ref[...] = (gate * sigmoid(gate) * up).astype(BF16)

def gate_up(x, w, tile):
    rows, depth = x.shape
    units = w.shape[1] // 3
    steps = units // tile
    col = pl.BlockSpec((rows, tile), lambda j: (0, j))
    out = jax.ShapeDtypeStruct((rows, units), BF16)
    return pl.pallas_call(gate_up_kernel, grid=(steps,),
        in_specs=[pl.BlockSpec((rows, depth), lambda j: (0, 0)), pl.BlockSpec((depth, tile), lambda j: (0, j)), pl.BlockSpec((depth, tile), lambda j: (0, j + steps))],
        out_specs=[col] * 3, out_shape=[out] * 3, compiler_params=pltpu.CompilerParams(vmem_limit_bytes=40 * 2**20),
        cost_estimate=lasting(14), name="gate_up")(x, w, w)

def hidden_back_kernel(g_ref, w_ref, gate_ref, up_ref, gg_ref, gu_ref):
    gh = nn(g_ref[...], w_ref[...])
    gate = gate_ref[...].astype(F32)
    up = up_ref[...].astype(F32)
    sig = sigmoid(gate)
    gg_ref[...] = (gh * up * (sig * (1.0 + gate * (1.0 - sig)))).astype(BF16)
    gu_ref[...] = (gh * (gate * sig)).astype(BF16)

def hidden_back(g, w, gate, up, tile):
    rows, depth = g.shape
    units = w.shape[1] // 3
    steps = units // tile
    col = pl.BlockSpec((rows, tile), lambda j: (0, j))
    out = jax.ShapeDtypeStruct((rows, units), BF16)
    return pl.pallas_call(hidden_back_kernel, grid=(steps,),
        in_specs=[pl.BlockSpec((rows, depth), lambda j: (0, 0)), pl.BlockSpec((depth, tile), lambda j: (0, j + 2 * steps)), col, col],
        out_specs=[col] * 2, out_shape=[out] * 2, compiler_params=pltpu.CompilerParams(vmem_limit_bytes=40 * 2**20),
        cost_estimate=lasting(10), name="hidden_back")(g, w, gate, up)

def weight_grads_kernel(*refs, counts):
    n = len(counts)
    lhs, rhs, out_ref, turned = refs[:n], refs[n:2 * n], refs[2 * n], refs[2 * n + 1]
    step = pl.program_id(0)
    first = 0
    for which in range(n):
        @pl.when(step == first)
        def _():
            turned[...] = jnp.transpose(lhs[which][...])
        @pl.when((step >= first) & (step < first + counts[which]))
        def _():
            out_ref[...] = nn(turned[...], rhs[which][...]).astype(BF16)
        first += counts[which]

def weight_grads(pairs, tile):
    rows, depth = pairs[0][0].shape
    counts = [right.shape[1] // tile for _, right in pairs]
    total = sum(counts)
    starts = [sum(counts[:i]) for i in range(len(counts))]
    whole = pl.BlockSpec((rows, depth), lambda j: (0, 0))
    def spec(start, count):
        return pl.BlockSpec((rows, tile), lambda j: (0, jnp.clip(j - start, 0, count - 1)))
    return pl.pallas_call(functools.partial(weight_grads_kernel, counts=counts), grid=(total,),
        in_specs=[whole] * len(pairs) + [spec(s, c) for s, c in zip(starts, counts)],
        out_specs=pl.BlockSpec((depth, tile), lambda j: (0, j)),
        out_shape=jax.ShapeDtypeStruct((depth, total * tile), BF16),
        scratch_shapes=[pltpu.VMEM((depth, rows), BF16)],
        compiler_params=pltpu.CompilerParams(vmem_limit_bytes=40 * 2**20),
        cost_estimate=lasting(1.25 * total), name="weight_grads")(
        *[left for left, _ in pairs], *[right for _, right in pairs])

def group_place(axes):
    me = lax.axis_index(axes[0])
    for a in axes[1:]:
        me = me * lax.axis_size(a) + lax.axis_index(a)
    return me


def group_device(axes, index):
    found = {}
    for a in reversed(axes):
        found[a] = lax.rem(index, lax.axis_size(a))
        index = index // lax.axis_size(a)
    return found


class SmallSum:
    axes = ("dp", "seq")

    def __init__(self, x_ref, out_ref, arrived, total, send, recv, send_out, recv_out):
        self.x_ref, self.out_ref, self.arrived, self.total = x_ref, out_ref, arrived, total
        self.sems = (send, recv, send_out, recv_out)
        self.count = x_ref.shape[0]
        self.me = group_place(self.axes)

    def to(self, step):
        return lax.rem(self.me + step, self.count)

    def back(self, step):
        return lax.rem(self.me - step + self.count, self.count)

    def greet(self, barrier):
        for step in range(1, self.count):
            pl.semaphore_signal(
                barrier,
                inc=1,
                device_id=group_device(self.axes, self.to(step)),
                device_id_type=MESH,
            )
        return self.count - 1

    def part(self, step, device):
        return pltpu.make_async_remote_copy(
            self.x_ref.at[device],
            self.arrived.at[step],
            self.sems[0].at[step],
            self.sems[1].at[step],
            device_id=group_device(self.axes, device),
            device_id_type=MESH,
        )

    def whole(self, step, slot, device):
        return pltpu.make_async_remote_copy(
            self.total,
            self.out_ref.at[slot],
            self.sems[2].at[step],
            self.sems[3].at[step],
            device_id=group_device(self.axes, device),
            device_id_type=MESH,
        )

    def begin(self):
        for step in range(1, self.count):
            self.part(step, self.to(step)).start()

    def middle(self):
        result = self.x_ref[self.me].astype(F32)
        for step in range(1, self.count):
            self.part(step, self.back(step)).wait_recv()
            result = result + self.arrived[step].astype(F32)
        self.total[...] = result.astype(BF16)
        self.out_ref[self.me] = result.astype(BF16)
        for step in range(1, self.count):
            self.whole(step, self.me, self.to(step)).start()

    def end(self):
        for step in range(1, self.count):
            self.whole(step, self.back(step), self.back(step)).wait_recv()
        for step in range(1, self.count):
            self.part(step, self.to(step)).wait_send()
            self.whole(step, self.me, self.to(step)).wait_send()


class OwnGrads:
    lag = 0

    def __init__(self, lefts, rights, uses, counts, tile, out_ref, scratch):
        self.lefts, self.rights, self.uses, self.counts, self.tile = lefts, rights, uses, counts, tile
        self.out_ref = out_ref
        self.turned, self.staged, self.out_sem = scratch
        self.total = sum(counts)

    @staticmethod
    def scratch(rows, depth, total, tile):
        return [
            pltpu.VMEM((depth, rows), BF16),
            pltpu.VMEM((2, depth, tile), BF16),
            pltpu.SemaphoreType.DMA((2,)),
        ]

    def put(self, t):
        slot = lax.rem(t, 2)
        return pltpu.make_async_copy(
            self.staged.at[slot],
            self.out_ref.at[:, pl.ds(pl.multiple_of(t * self.tile, self.tile), self.tile)],
            self.out_sem.at[slot],
        )

    def turn(self, which):
        self.turned[...] = jnp.transpose(self.lefts[self.uses[which]][...])

    def step(self, t):
        first = 0
        for which, count in enumerate(self.counts):
            if which == 0 or self.uses[which] != self.uses[which - 1]:

                @pl.when(t == first)
                def _(which=which):
                    self.turn(which)

            @pl.when((t >= first) & (t < first + count))
            def _(which=which, first=first):
                self.multiply(which, t - first, t)

            first += count

    def greet(self, barrier):
        return 0

    def multiply(self, which, index, t):
        slot = lax.rem(t, 2)
        block = self.rights[which][:, pl.ds(pl.multiple_of(index * self.tile, self.tile), self.tile)]

        @pl.when(t >= 2)
        def _():
            self.put(t - 2).wait()

        self.staged[slot] = nn(self.turned[...], block).astype(BF16)
        self.put(t).start()

    def end(self):
        for t in (self.total - 2, self.total - 1):
            self.put(t).wait()


class ScatterGrads(OwnGrads):
    lags = (1, 3, 4)
    lag = 4

    def __init__(self, lefts, rights, uses, counts, tile, out_ref, scratch):
        self.lefts, self.rights, self.uses, self.counts, self.tile = lefts, rights, uses, counts, tile
        self.out_ref = out_ref
        self.turned, self.sent, self.kept, self.landed, self.crossed, self.last = scratch[:6]
        self.sems = scratch[6:]
        self.total = sum(counts)
        self.dp = lax.axis_index("dp")
        place = lax.axis_index("seq")
        self.low, self.high = lax.rem(place, 2), place // 2
        self.beside = self.high * 2 + 1 - self.low
        self.across = (1 - self.high) * 2 + self.low
        self.half = self.turned.shape[0] // 2
        self.block = self.half // 4

    @staticmethod
    def scratch(rows, depth, total, tile):
        half = depth // 2
        return [
            pltpu.VMEM((depth, rows), BF16),
            pltpu.VMEM((2, half, tile), BF16),
            pltpu.VMEM((3, half, tile), F32),
            pltpu.VMEM((total, half, tile), BF16),
            pltpu.VMEM((total, 2, half // 4, tile), BF16),
            pltpu.VMEM((total, half // 4, tile), BF16),
            pltpu.SemaphoreType.DMA((2, total)),
            pltpu.SemaphoreType.DMA((total, 2)),
            pltpu.SemaphoreType.DMA((total, 2)),
            pltpu.SemaphoreType.DMA((total,)),
            pltpu.SemaphoreType.DMA((total,)),
        ]

    def greet(self, barrier):
        for device in ({"dp": 1 - self.dp}, {"seq": self.beside}, {"seq": self.across}):
            pl.semaphore_signal(barrier, inc=1, device_id=device, device_id_type=MESH)
        return 3

    def part(self, which):
        return self.turned[pl.ds(pl.multiple_of(which * self.half, self.half), self.half)]

    def to_core(self, t):
        return pltpu.make_async_remote_copy(
            self.sent.at[lax.rem(t, 2)],
            self.landed.at[t],
            self.sems[0].at[0, t],
            self.sems[0].at[1, t],
            device_id={"dp": 1 - self.dp},
            device_id_type=MESH,
        )

    def rows(self, index):
        return pl.ds(pl.multiple_of(index * self.block, self.block), self.block)

    def even(self, t, if_even, if_odd):
        return jnp.where(lax.rem(t, 2) == 0, if_even, if_odd)

    def to_first(self, t, k):
        index = self.even(t, 2 * k + 1 - self.low, (1 - self.high) * 2 + k)
        return pltpu.make_async_remote_copy(
            self.landed.at[t, self.rows(index)],
            self.crossed.at[t, k],
            self.sems[1].at[t, k],
            self.sems[2].at[t, k],
            device_id={"seq": self.even(t, self.beside, self.across)},
            device_id_type=MESH,
        )

    def to_second(self, t):
        return pltpu.make_async_remote_copy(
            self.crossed.at[t, self.even(t, 1 - self.high, 1 - self.low)],
            self.last.at[t],
            self.sems[3].at[t],
            self.sems[4].at[t],
            device_id={"seq": self.even(t, self.across, self.beside)},
            device_id_type=MESH,
        )

    def multiply(self, which, index, t):
        slot = lax.rem(t, 2)
        block = self.rights[which][:, pl.ds(pl.multiple_of(index * self.tile, self.tile), self.tile)]

        @pl.when(t >= 2)
        def _():
            self.to_core(t - 2).wait_send()

        self.sent[slot] = nn(self.part(1 - self.dp), block).astype(BF16)
        self.to_core(t).start()
        self.kept[lax.rem(t, 3)] = nn(self.part(self.dp), block)

    def core_sum(self, t):
        self.to_core(t).wait_recv()
        self.landed[t] = (self.kept[lax.rem(t, 3)] + self.landed[t].astype(F32)).astype(BF16)
        for k in range(2):
            self.to_first(t, k).start()

    def first_chip_sum(self, t):
        for k in range(2):
            self.to_first(t, k).wait_recv()
            index = self.even(t, 2 * k + self.low, self.high * 2 + k)
            own = self.landed[t, self.rows(index)].astype(F32)
            self.crossed[t, k] = (own + self.crossed[t, k].astype(F32)).astype(BF16)
        self.to_second(t).start()

    def second_chip_sum(self, t):
        self.to_second(t).wait_recv()
        own = self.crossed[t, self.even(t, self.high, self.low)].astype(F32)
        self.out_ref[:, pl.ds(pl.multiple_of(t * self.tile, self.tile), self.tile)] = (
            own + self.last[t].astype(F32)
        ).astype(BF16)

    def step(self, t):
        super().step(t)
        works = (self.core_sum, self.first_chip_sum, self.second_chip_sum)
        for late, work in zip(self.lags, works):

            @pl.when((t >= late) & (t < self.total + late))
            def _(late=late, work=work):
                work(t - late)

    def end(self):
        for t in (self.total - 2, self.total - 1):
            self.to_core(t).wait_send()

        def finish(t, carry):
            for k in range(2):
                self.to_first(t, k).wait_send()
            self.to_second(t).wait_send()
            return carry

        lax.fori_loop(0, self.total, finish, 0)


def grad_operands(pairs, xs):
    lefts, uses = [], []
    for left, _ in pairs:
        known = [i for i, other in enumerate(lefts) if other is left]
        uses.append(known[0] if known else len(lefts))
        if not known:
            lefts.append(left)
    shared = []
    rights = []
    for _, right in pairs:
        same = [i for i, x in enumerate(xs) if x is right]
        shared.append(same[0] if same else -1)
        if not same:
            rights.append(right)
    return lefts, rights, uses, shared


def matmul_sum_kernel(
    *refs, columns, first_column, tile, splits, with_small, uses, shared, counts, job_kind
):
    refs = list(refs)

    def take(count):
        taken = refs[:count]
        del refs[:count]
        return taken

    xs = take(len(columns))
    (w_ref,) = take(1)
    small_in = take(1 if with_small else 0)
    lefts = take(max(uses) + 1 if uses else 0)
    others = take(sum(which < 0 for which in shared))
    rights = [xs[which] if which >= 0 else others.pop(0) for which in shared]
    (out_ref,) = take(1)
    small_out = take(1 if with_small else 0)
    grads_out = take(1 if uses else 0)
    w_buf, part, a_buf, b_buf, w_sem, a_send, a_recv, b_send, b_recv, c_send, c_recv = take(11)
    small = SmallSum(*small_in, *small_out, *take(6)) if with_small else None
    job = None
    if uses:
        job = job_kind(lefts, rights, uses, counts, tile, *grads_out, refs)
    rows, depth = out_ref.shape
    tiles = depth // tile
    short = rows // splits
    wide = sum(columns)
    z = lax.axis_index("tensor")
    half = lax.axis_size("tensor") // 2
    inner = (z == half - 1) | (z == half)
    low = z < half
    outer_dev = jnp.where(low, half - 2, half + 1)
    inner_dev = jnp.where(low, half - 1, half)
    other = jnp.where(low, half, half - 1)
    barrier = pltpu.get_barrier_semaphore()

    def weights(j, slot):
        return pltpu.make_async_copy(
            w_ref.at[pl.ds(pl.multiple_of(j * tile, tile), tile), pl.ds(first_column, wide)],
            w_buf.at[slot],
            w_sem.at[slot],
        )

    def cells(ref, j, r):
        return ref.at[pl.ds(r * short, short), pl.ds(pl.multiple_of(j * tile, tile), tile)]

    def send(src, dst, sems, j, r, device):
        return pltpu.make_async_remote_copy(
            cells(src, j, r),
            cells(dst, j, r),
            sems[0].at[j, r],
            sems[1].at[j, r],
            device_id={"tensor": device},
            device_id_type=MESH,
        )

    def send_a(j, r):
        return send(part, a_buf, (a_send, a_recv), j, r, inner_dev)

    def send_b(j, r):
        return send(part, b_buf, (b_send, b_recv), j, r, other)

    def send_c(j, r):
        return send(out_ref, out_ref, (c_send, c_recv), j, r, outer_dev)

    weights(0, 0).start()
    greeted = (small.greet(barrier) if with_small else 0) + (job.greet(barrier) if uses else 0)

    @pl.when(jnp.logical_not(inner))
    def _():
        pl.semaphore_signal(barrier, inc=1, device_id={"tensor": inner_dev}, device_id_type=MESH)
        pl.semaphore_wait(barrier, 1 + greeted)

    @pl.when(inner)
    def _():
        pl.semaphore_signal(barrier, inc=1, device_id={"tensor": outer_dev}, device_id_type=MESH)
        pl.semaphore_signal(barrier, inc=1, device_id={"tensor": other}, device_id_type=MESH)
        pl.semaphore_wait(barrier, 2 + greeted)

    if with_small:
        small.begin()

    def first_sum(j, r):
        send_a(j, r).wait_recv()
        mine = cells(part, j, r)
        mine[...] = (mine[...].astype(F32) + cells(a_buf, j, r)[...].astype(F32)).astype(BF16)
        send_b(j, r).start()

    def second_sum(j, r):
        send_b(j, r).wait_recv()
        cells(out_ref, j, r)[...] = (
            cells(part, j, r)[...].astype(F32) + cells(b_buf, j, r)[...].astype(F32)
        ).astype(BF16)
        send_c(j, r).start()

    lag = splits - 1

    def one_tile(j, carry):
        slot = lax.rem(j, 2)
        weights(j, slot).wait()

        @pl.when(j + 1 < tiles)
        def _():
            weights(j + 1, 1 - slot).start()

        total = None
        first = 0
        for x_ref, count in zip(xs, columns):
            term = nt(x_ref[...], w_buf[slot, :, pl.ds(first, count)])
            total = term if total is None else total + term
            first += count
        part[:, pl.ds(pl.multiple_of(j * tile, tile), tile)] = total.astype(BF16)

        @pl.when(jnp.logical_not(inner))
        def _():
            for r in range(splits):
                send_a(j, r).start()

        each = -(-(job.total + job.lag) // tiles) if uses else 0
        for r in range(max(splits, each)):
            if r < splits:

                @pl.when(inner)
                def _(r=r):
                    first_sum(j, r)
                    if r >= lag:
                        second_sum(j, r - lag)
                    else:

                        @pl.when(j > 0)
                        def _():
                            second_sum(j - 1, r + splits - lag)

            if r < each:
                job.step(j * each + r)

        return carry

    if with_small:
        lax.fori_loop(0, tiles // 2, one_tile, 0)
        small.middle()
        lax.fori_loop(tiles // 2, tiles, one_tile, 0)
    else:
        lax.fori_loop(0, tiles, one_tile, 0)

    @pl.when(inner)
    def _():
        for r in range(splits - lag, splits):
            second_sum(tiles - 1, r)

        def finish(j, carry):
            for r in range(splits):
                send_b(j, r).wait_send()
                send_c(j, r).wait_send()
            return carry

        lax.fori_loop(0, tiles, finish, 0)

    @pl.when(jnp.logical_not(inner))
    def _():
        def finish(j, carry):
            for r in range(splits):
                send_c(j, r).wait_recv()
                send_a(j, r).wait_send()
            return carry

        lax.fori_loop(0, tiles, finish, 0)

    if with_small:
        small.end()
    if uses:
        job.end()


def matmul_sum(
    xs, w, first_column, identifier, small=None, pairs=None, scatter=False, tile=256, splits=3
):
    rows = xs[0].shape[0]
    depth = w.shape[0]
    columns = [x.shape[1] for x in xs]
    wide = sum(columns)
    whole = pl.BlockSpec(memory_space=pltpu.VMEM)
    far = pl.BlockSpec(memory_space=pltpu.HBM)
    tiles = depth // tile
    out_shape = [jax.ShapeDtypeStruct((rows, depth), BF16)]
    out_specs = [whole]
    scratch = (
        [pltpu.VMEM((2, tile, wide), BF16)]
        + [pltpu.VMEM((rows, depth), BF16)] * 3
        + [pltpu.SemaphoreType.DMA((2,))]
        + [pltpu.SemaphoreType.DMA((tiles, splits))] * 6
    )
    extra = ()
    if small is not None:
        extra = (small,)
        out_shape.append(jax.ShapeDtypeStruct(small.shape, BF16))
        out_specs.append(whole)
        scratch += [pltpu.VMEM(small.shape, BF16), pltpu.VMEM(small.shape[1:], BF16)]
        scratch += [pltpu.SemaphoreType.DMA((small.shape[0],))] * 4
    uses, shared, counts, job_kind = (), (), (), None
    if pairs is not None:
        job_kind = ScatterGrads if scatter else OwnGrads
        lefts, rights, uses, shared = grad_operands(pairs, xs)
        counts = [right.shape[1] // tile for _, right in pairs]
        extra = (*extra, *lefts, *rights)
        height = depth // 8 if scatter else depth
        out_shape.append(jax.ShapeDtypeStruct((height, sum(counts) * tile), BF16))
        out_specs.append(whole if scatter else far)
        scratch += job_kind.scratch(rows, depth, sum(counts), tile)
    results = pl.pallas_call(
        functools.partial(
            matmul_sum_kernel,
            columns=columns,
            first_column=first_column,
            tile=tile,
            splits=splits,
            with_small=small is not None,
            uses=uses,
            shared=shared,
            counts=counts,
            job_kind=job_kind,
        ),
        out_shape=out_shape,
        in_specs=[whole] * len(xs) + [far] + [whole] * len(extra),
        out_specs=out_specs,
        scratch_shapes=scratch,
        compiler_params=pltpu.CompilerParams(
            collective_id=identifier, has_side_effects=True, vmem_limit_bytes=(40 if pairs is None else 44) * 2**20
        ),
        cost_estimate=lasting(58 if pairs is None else 67),
        name="matmul_sum" + ("_small" if small is not None else "_grads" if uses else ""),
    )(*xs, w, *extra)
    return results if extra else results[0]


def norm_back_kernel(v_ref, gain_ref, normed_ref, out_ref, total_ref, low_ref, gain_out):
    @pl.when(pl.program_id(0) == 0)
    def _():
        gain_out[...] = jnp.zeros_like(gain_out)

    v = v_ref[...].astype(F32)
    grad = normed_ref[...].astype(F32)
    inv_rms = lax.rsqrt(jnp.mean(v * v, axis=1, keepdims=True) + epsilon)
    weighted = grad * gain_ref[...]
    mean_term = jnp.mean(weighted * v, axis=1, keepdims=True)
    total = out_ref[...] + inv_rms * weighted - v * (inv_rms * inv_rms * inv_rms * mean_term)
    total_ref[...] = total
    low_ref[...] = total.astype(BF16)
    gain_out[...] += jnp.sum(grad * (v * inv_rms), axis=0, keepdims=True)


def norm_back(v, gain, grad_normed, grad_out):
    rows, depth = v.shape
    chunk = rows // 11 if rows % 176 == 0 else rows
    block = pl.BlockSpec((chunk, depth), lambda i: (i, 0))
    line = pl.BlockSpec((1, depth), lambda i: (0, 0))
    return pl.pallas_call(
        norm_back_kernel,
        grid=(rows // chunk,),
        in_specs=[block, line, block, block],
        out_specs=[block, block, line],
        out_shape=[
            jax.ShapeDtypeStruct((rows, depth), F32),
            jax.ShapeDtypeStruct((rows, depth), BF16),
            jax.ShapeDtypeStruct((1, depth), F32),
        ],
        compiler_params=pltpu.CompilerParams(vmem_limit_bytes=24 * 2**20),
        cost_estimate=lasting(4),
        name="norm_back",
    )(v, gain.reshape(1, depth), grad_normed, grad_out)


def scattered(grads, axes):
    return lax.optimization_barrier(
        lax.psum_scatter(grads, axes, scatter_dimension=0, tiled=True)
    )


def first_gather_kernel(
    rows_ref, gains_ref, w_ref, full_ref, gains_out, acting_ref, own_sem, gain_sems, sems
):
    dp = lax.axis_index("dp")
    seq = lax.axis_index("seq")
    low, high = lax.rem(seq, 2), seq // 2
    beside = high * 2 + 1 - low
    across = (1 - high) * 2 + low
    far = (1 - high) * 2 + 1 - low
    count = 8
    me = dp * 4 + seq
    height = w_ref.shape[0]
    pieces = 4
    wide = w_ref.shape[1] // pieces
    axes = ("dp", "seq")
    barrier = pltpu.get_barrier_semaphore()
    for step in range(1, count):
        pl.semaphore_signal(
            barrier,
            inc=1,
            device_id=group_device(axes, lax.rem(me + step, count)),
            device_id_type=MESH,
        )
    pl.semaphore_wait(barrier, count - 1)

    def cells(ref, owner_dp, owner_seq, p):
        first = pl.multiple_of((owner_dp * 4 + owner_seq) * height, height)
        return ref.at[pl.ds(first, height), pl.ds(p * wide, wide)]

    def copy(kind, p, owner_dp, owner_seq, device, own=False):
        here = w_ref.at[:, pl.ds(p * wide, wide)] if own else cells(full_ref, owner_dp, owner_seq, p)
        return pltpu.make_async_remote_copy(
            here,
            cells(full_ref, owner_dp, owner_seq, p),
            sems.at[0, kind, p],
            sems.at[1, kind, p],
            device_id=device,
            device_id_type=MESH,
        )

    to_beside, to_across, to_core = {"seq": beside}, {"seq": across}, {"dp": 1 - dp}
    keep = pltpu.make_async_copy(
        w_ref, full_ref.at[pl.ds(pl.multiple_of(me * height, height), height)], own_sem
    )

    def gain_copy(step, slot, device):
        return pltpu.make_async_remote_copy(
            gains_ref,
            gains_out.at[slot],
            gain_sems.at[0, step],
            gain_sems.at[1, step],
            device_id=group_device(axes, device),
            device_id_type=MESH,
        )

    for step in range(1, count):
        gain_copy(step, me, lax.rem(me + step, count)).start()
    for p in range(pieces):
        copy(0, p, dp, seq, to_beside, True).start()
        copy(1, (p + 2) % pieces, dp, seq, to_across, True).start()
    keep.start()
    for p in range(pieces):
        copy(3, p, dp, seq, to_core, True).start()
    gains_out[me] = gains_ref[...]
    for step in range(1, count):
        source = lax.rem(me - step + count, count)
        gain_copy(step, source, source).wait_recv()
    values = rows_ref[...].astype(F32)
    inv_rms = lax.rsqrt(jnp.mean(values * values, axis=1, keepdims=True) + epsilon)
    part = values.shape[1] // count
    for i in range(count):
        at = pl.ds(i * part, part)
        acting_ref[:, at] = (
            values[:, i * part : (i + 1) * part] * inv_rms * gains_out[i, 0:1, :]
        ).astype(BF16)
    for turn_index in range(pieces):
        p = turn_index
        copy(0, p, dp, beside, to_beside).wait_recv()
        if p < pieces // 2:
            copy(2, p, dp, beside, to_across).start()
        copy(4, p, dp, beside, to_core).start()
        p = (turn_index + 2) % pieces
        copy(1, p, dp, across, to_across).wait_recv()
        if p >= pieces // 2:
            copy(2, p, dp, across, to_beside).start()
        copy(5, p, dp, across, to_core).start()
    for p in (0, 2, 1, 3):
        copy(2, p, dp, far, to_across).wait_recv()
        copy(6, p, dp, far, to_core).start()
    for p in range(pieces):
        for kind, owner in ((3, seq), (4, beside), (5, across), (6, far)):
            copy(kind, p, 1 - dp, owner, to_core).wait_recv()
    keep.wait()
    for step in range(1, count):
        gain_copy(step, me, lax.rem(me + step, count)).wait_send()
    for p in range(pieces):
        copy(0, p, dp, seq, to_beside, True).wait_send()
        copy(1, p, dp, seq, to_across, True).wait_send()
        copy(3, p, dp, seq, to_core, True).wait_send()
        if p < pieces // 2:
            copy(2, p, dp, beside, to_across).wait_send()
        else:
            copy(2, p, dp, across, to_beside).wait_send()
        copy(4, p, dp, beside, to_core).wait_send()
        copy(5, p, dp, across, to_core).wait_send()
        copy(6, p, dp, far, to_core).wait_send()


def first_gather(rows, gains, w, identifier):
    whole = pl.BlockSpec(memory_space=pltpu.VMEM)
    far = pl.BlockSpec(memory_space=pltpu.HBM)
    return pl.pallas_call(
        first_gather_kernel,
        in_specs=[whole, whole, far],
        out_specs=[far, whole, whole],
        out_shape=[
            jax.ShapeDtypeStruct((8 * w.shape[0], w.shape[1]), BF16),
            jax.ShapeDtypeStruct((8,) + gains.shape, F32),
            jax.ShapeDtypeStruct(rows.shape, BF16),
        ],
        scratch_shapes=[
            pltpu.SemaphoreType.DMA,
            pltpu.SemaphoreType.DMA((2, 8)),
            pltpu.SemaphoreType.DMA((2, 7, 4)),
        ],
        compiler_params=pltpu.CompilerParams(
            collective_id=identifier, has_side_effects=True, vmem_limit_bytes=32 * 2**20
        ),
        name="first_gather",
        cost_estimate=lasting(42),
    )(rows, gains, w)


def gate_back_kernel(g_ref, w_ref, gate_ref, scanned_ref, input_ref, scan_ref, gate_out, skip_ref):
    grad = nn(g_ref[...], w_ref[...])
    gate = gate_ref[...].astype(F32)
    sig = sigmoid(gate)
    scan = grad * (gate * sig)
    scan_ref[...] = scan
    gate_out[...] = (grad * scanned_ref[...] * (sig * (1.0 + gate * (1.0 - sig)))).astype(BF16)
    skip_ref[...] = jnp.sum(scan * input_ref[...].astype(F32), axis=0, keepdims=True)


def gate_back(g, w, gate, gate_column, scanned, inputs, tile=256):
    rows, depth = g.shape
    width = scanned.shape[1]
    skip = gate_column // tile
    column = pl.BlockSpec((rows, tile), lambda j: (0, j))
    return pl.pallas_call(
        gate_back_kernel,
        grid=(width // tile,),
        in_specs=[
            pl.BlockSpec((rows, depth), lambda j: (0, 0)),
            pl.BlockSpec((depth, tile), lambda j: (0, j)),
            pl.BlockSpec((rows, tile), lambda j: (0, j + skip)),
            column,
            column,
        ],
        out_specs=[column, column, pl.BlockSpec((1, tile), lambda j: (0, j))],
        out_shape=[
            jax.ShapeDtypeStruct((rows, width), F32),
            jax.ShapeDtypeStruct((rows, width), BF16),
            jax.ShapeDtypeStruct((1, width), F32),
        ],
        compiler_params=pltpu.CompilerParams(vmem_limit_bytes=32 * 2**20),
        cost_estimate=lasting(6),
        name="gate_back",
    )(g, w, gate, scanned, inputs)


def ffn_forward(stream, gain, weights, identifier):
    acting = norm_forward(stream, gain).astype(BF16)
    gate, up, hidden_low = gate_up(acting, weights, 256)
    branch = matmul_sum([hidden_low], weights, 2 * hidden_low.shape[1], identifier)
    return (stream + branch.astype(F32), (acting, gate, up, hidden_low))


def shards(
    hidden,
    teacher,
    valid_length,
    mamba_norm,
    mamba_in,
    conv_kernel,
    conv_bias,
    select_weight,
    step_weight,
    step_bias,
    decay_log,
    skip_gain,
    mamba_out,
    attn_norm,
    attn_qkv,
    attn_out,
    first_norm,
    first_gate_up,
    first_down,
    second_norm,
    second_gate_up,
    second_down,
):
    def split(rows, *like):
        parts = []
        first = 0
        for shard in like:
            if len(shard.shape) == 3:
                height, groups, columns = shard.shape
                pieces = [
                    rows[:, first + columns * g : first + columns * (g + 1)] for g in range(groups)
                ]
                parts.append(jnp.stack(pieces).transpose(1, 0, 2).astype(F32))
                columns = columns * groups
            else:
                columns = shard.shape[1]
                parts.append(rows[:, first : first + columns].astype(F32))
            first += columns
        return parts

    rows_here = hidden.shape[1]
    model_width = hidden.shape[2]
    seq_count = lax.axis_size("seq")
    seq_place = lax.axis_index("seq")
    my_length = valid_length[lax.axis_index("dp")]
    positions = seq_place * rows_here + jnp.arange(rows_here, dtype=jnp.int32)
    valid_rows = (positions < my_length).astype(F32)[:, None]
    total_valid = jnp.sum(valid_length).astype(F32)
    total_slots = valid_length.shape[0] * rows_here * seq_count
    stream_zero = hidden[0].astype(F32)
    gains = jnp.stack([mamba_norm, attn_norm, first_norm, second_norm]).astype(F32)
    gains = jnp.pad(gains, ((0, 4), (0, 0)))
    split_four = lax.axis_size("dp") == 2 and seq_count == 4
    mixed = join(mamba_out, attn_qkv, attn_out)
    if split_four:
        gains, mixed = lax.optimization_barrier((gains, mixed))
        in_full, gains, acting_mamba = first_gather(hidden[0], gains, join(mamba_in), 2)
    else:
        gains = direct_gather(gains, ("dp", "seq"), 2)
        in_full = gather_joined(join(mamba_in))
    gain_mamba, gain_attn, gain_first, gain_second = (
        gains[:, which].reshape(model_width) for which in range(4)
    )
    mixed, in_full = lax.optimization_barrier((mixed, in_full))
    mixed_full = gather_joined(mixed)
    channels = mamba_out.shape[1]
    heads_width = attn_out.shape[1]
    qkv_column = channels
    attn_column = channels + 3 * heads_width
    if not split_four:
        acting_mamba = norm_forward(stream_zero, gain_mamba).astype(BF16)
    projected = product(acting_mamba, in_full).astype(BF16)
    ffn_shards = (first_gate_up, first_down, second_gate_up, second_down)
    ffn_shards, projected = lax.optimization_barrier((ffn_shards, projected))
    first_weights = gather_joined(join(*ffn_shards[:2]))
    second_weights = gather_joined(join(*ffn_shards[2:]))
    conv_input = projected[:, :channels]
    gate_input = projected[:, channels:].astype(F32)
    tap_count = conv_kernel.shape[0]
    edge_rows = shifted(conv_input[rows_here - (tap_count - 1) :], "seq", 1)
    padded = jnp.concatenate([edge_rows, conv_input], axis=0).astype(F32)
    conv_pre = conv_bias
    for tap_index in range(tap_count):
        conv_pre = conv_pre + conv_kernel[tap_index] * padded[tap_index : tap_index + rows_here]
    inputs_low = jax.nn.silu(conv_pre).astype(BF16)
    inputs = inputs_low.astype(F32)
    selected = tensor_forward_sum(product(inputs_low, select_weight))
    step_rank = step_weight.shape[0]
    states = decay_log.shape[0]
    step_in = selected[:, :step_rank].astype(BF16)
    input_map = selected[:, step_rank : step_rank + states]
    output_map = selected[:, step_rank + states :]
    step_pre = product(step_in, step_weight) + step_bias
    step_size = jax.nn.softplus(step_pre)
    decay_rate = -jnp.exp(decay_log)
    width = inputs.shape[1]
    run_state, run_scan, run_back_state, run_back = scan_calls(rows_here, width, states)
    rate_two = decay_rate * LOG2E
    in_wide = jnp.broadcast_to(input_map[:, :, None], (rows_here, states, 128))
    out_wide = jnp.broadcast_to(output_map[:, :, None], (rows_here, states, 128))
    moved = step_size * inputs
    end_state = run_state(step_size, moved, in_wide, rate_two)
    step_total = jnp.sum(step_size, axis=0, keepdims=True)
    ends = direct_gather(
        jnp.concatenate([end_state, step_total, jnp.zeros((7, width), F32)], axis=0), ("seq",), 3
    )
    decays = [jnp.exp2(rate_two * ends[place, states][None]) for place in range(seq_count)]
    start_state = jnp.zeros_like(end_state)
    for place in range(seq_count - 1):
        start_state = jnp.where(
            place < seq_place, decays[place] * start_state + ends[place, :states], start_state
        )
    scanned, kept_states = run_scan(step_size, moved, in_wide, out_wide, rate_two, start_state)
    scanned = scanned + skip_gain * inputs
    gate_silu = jax.nn.silu(gate_input)
    gated_low = (scanned * gate_silu).astype(BF16)
    stream_one = stream_zero + matmul_sum([gated_low], mixed_full, 0, 6).astype(F32)
    normed_attn = norm_forward(stream_one, gain_attn)
    acting_attn = normed_attn.astype(BF16)
    cosine, sine = rope_tables(positions)
    queries, own_kv = qkv_rows(acting_attn, mixed_full, qkv_column, heads_width, cosine, sine)
    hop_count = min(seq_count - 1, (WINDOW - 2) // rows_here + 1)
    attended, attended_low, log_sums, far_kv = attend(queries, own_kv, hop_count, 13)
    stream_two = stream_one + matmul_sum([attended_low], mixed_full, attn_column, 7).astype(F32)
    stream_three, first_saved = ffn_forward(stream_two, gain_first, first_weights, 8)
    stream_four, second_saved = ffn_forward(stream_three, gain_second, second_weights, 8)
    residue = (stream_four - teacher[0].astype(F32)) * valid_rows
    local_loss = jnp.sum(residue * residue) / (model_width * total_valid)
    grad_four = residue * (total_slots / total_valid)
    acting, gate, up, hidden_low = second_saved
    grad_low = grad_four.astype(BF16)
    grad_gate, grad_up = hidden_back(grad_low, second_weights, gate, up, 256)
    second_parts = [(acting, grad_gate), (acting, grad_up), (grad_low, hidden_low)]
    grad_normed, second_grads = matmul_sum(
        [grad_gate, grad_up], second_weights, 0, 16, pairs=second_parts
    )
    second_grads = scattered(second_grads, ("dp", "seq"))
    grad_three, grad_low, grad_gain_second = norm_back(
        stream_three, gain_second, grad_normed, grad_four
    )
    acting, gate, up, hidden_low = first_saved
    grad_gate, grad_up = hidden_back(grad_low, first_weights, gate, up, 256)
    first_parts = [(acting, grad_gate), (acting, grad_up), (grad_low, hidden_low)]
    grad_normed, first_grads = matmul_sum(
        [grad_gate, grad_up], first_weights, 0, 16, pairs=first_parts
    )
    grad_two, grad_low_attn, grad_gain_first = norm_back(
        stream_two, gain_first, grad_normed, grad_three
    )
    grad_attended = product(grad_low_attn, mixed_full[:, attn_column:]).astype(BF16)
    grad_projected_attn = attend_back(
        queries, grad_attended, attended, log_sums, own_kv, far_kv, cosine, sine, 14
    )
    grad_projected_attn, second_grads = lax.optimization_barrier(
        (grad_projected_attn, second_grads)
    )
    first_grads = scattered(first_grads, ("dp", "seq"))
    attn_pairs = [(acting_attn, grad_projected_attn), (grad_low_attn, attended_low)]
    grad_normed_attn, attn_grads = matmul_sum(
        [grad_projected_attn], mixed_full, qkv_column, 10, pairs=attn_pairs
    )
    attn_grads = scattered(attn_grads, ("dp", "seq"))
    grad_one, grad_low_mamba, grad_gain_attn = norm_back(
        stream_one, gain_attn, grad_normed_attn, grad_two
    )
    second_both, second_down_grad = split(second_grads, second_gate_up, second_down)
    grad_scanned, grad_gate_low, grad_skip = gate_back(
        grad_low_mamba, mixed_full, projected, channels, scanned, inputs_low
    )
    incoming = run_back_state(step_size, grad_scanned, out_wide, rate_two)
    incomings = direct_gather(incoming, ("seq",), 4)
    arriving_grad = jnp.zeros_like(incoming)
    for place in reversed(range(1, seq_count)):
        arriving_grad = jnp.where(
            place > seq_place, incomings[place] + decays[place] * arriving_grad, arriving_grad
        )
    grad_sizes, grad_inputs_scan, grad_in_map, grad_out_map, grad_rates = run_back(
        step_size, inputs, grad_scanned, in_wide, out_wide, rate_two, kept_states, arriving_grad
    )
    grad_decay_log = grad_rates * decay_rate
    grad_inputs = grad_inputs_scan + grad_scanned * skip_gain
    grad_step_pre = grad_sizes * jax.nn.sigmoid(step_pre)
    grad_step_bias = jnp.sum(grad_step_pre, axis=0)
    grad_step_low = grad_step_pre.astype(BF16)
    grad_step_weight = product_tl(step_in, grad_step_low)
    grad_step_in = product_t(grad_step_low, step_weight)
    grad_selected = tensor_backward_sum(
        jnp.concatenate([grad_step_in, grad_in_map, grad_out_map], axis=1)
    ).astype(BF16)
    grad_selected, first_grads = lax.optimization_barrier((grad_selected, first_grads))
    grad_select = product_tl(grad_selected, inputs_low)
    grad_inputs = grad_inputs + product_t(grad_selected, select_weight)
    grad_conv_pre = grad_inputs * silu_slope(conv_pre)
    grad_conv_bias = jnp.sum(grad_conv_pre, axis=0)
    grad_kernel = jnp.stack(
        [
            jnp.sum(padded[tap_index : tap_index + rows_here] * grad_conv_pre, axis=0)
            for tap_index in range(tap_count)
        ]
    )
    grad_padded = sum(
        (
            jnp.pad(
                conv_kernel[tap_index] * grad_conv_pre,
                ((tap_index, tap_count - 1 - tap_index), (0, 0)),
            )
            for tap_index in range(tap_count)
        )
    )
    back_edge = shifted(grad_padded[: tap_count - 1], "seq", -1)
    grad_conv_input = grad_padded[tap_count - 1 :] + jnp.pad(
        back_edge, ((rows_here - (tap_count - 1), 0), (0, 0))
    )
    grad_conv_low = grad_conv_input.astype(BF16)
    mamba_pairs = [
        (grad_low_mamba, gated_low),
        (acting_mamba, grad_gate_low),
        (acting_mamba, grad_conv_low),
    ]
    loose = (
        grad_kernel,
        grad_conv_bias[None],
        grad_step_bias[None],
        grad_skip,
        jnp.broadcast_to(local_loss, (1, width)),
        grad_gain_attn.reshape(-1, width),
        grad_gain_first.reshape(-1, width),
        grad_gain_second.reshape(-1, width),
    )
    loose_rows = sum(part.shape[0] for part in loose)
    loose_block = jnp.concatenate(
        loose + (jnp.zeros((-loose_rows % 16, width), F32),), axis=0
    ).astype(BF16)
    packed = (grad_select, grad_step_weight, grad_decay_log, loose_block)
    devices = lax.axis_size("dp") * seq_count
    packed_rows = sum(part.shape[0] for part in packed)
    each = -(-packed_rows // (16 * devices)) * 16
    blocks = jnp.concatenate(
        [part.astype(BF16) for part in packed]
        + [jnp.zeros((each * devices - packed_rows, width), BF16)],
        axis=0,
    ).reshape(devices, each, width)
    if split_four:
        grad_normed_mamba, summed, mamba_grads = matmul_sum(
            [grad_conv_low, grad_gate_low],
            in_full,
            0,
            11,
            small=blocks,
            pairs=mamba_pairs,
            scatter=True,
        )
    else:
        grad_normed_mamba, summed = matmul_sum(
            [grad_conv_low, grad_gate_low], in_full, 0, 11, small=blocks
        )
        mamba_grads = scattered(weight_grads(mamba_pairs, 256), ("dp", "seq"))
    input_grad, _, grad_gain_mamba = norm_back(stream_zero, gain_mamba, grad_normed_mamba, grad_one)
    summed = summed.reshape(devices * each, width).astype(F32)

    def unpack(rows, shapes):
        parts = []
        first = 0
        for part in shapes:
            parts.append(rows[first : first + part.shape[0]])
            first += part.shape[0]
        return parts

    sum_select, sum_step_weight, sum_decay_log, loose_sums = unpack(summed, packed)
    (
        sum_kernel,
        sum_conv_bias,
        sum_step_bias,
        sum_skip,
        sum_loss,
        sum_attn,
        sum_first,
        sum_second,
    ) = unpack(loose_sums, loose)
    loss_total = sum_loss[0, 0]
    sum_mamba = jnp.sum(direct_gather(grad_gain_mamba.reshape(8, -1), ("dp", "seq"), 5), axis=0)
    gain_rows = mamba_norm.shape[0]
    place = lax.axis_index("dp") * seq_count + seq_place
    grad_qkv, grad_attn_out = split(attn_grads, attn_qkv, attn_out)
    grad_out, gate_half, conv_half = split(
        mamba_grads, mamba_out, mamba_in[:, 1], mamba_in[:, 0]
    )
    grad_in = jnp.stack([conv_half, gate_half], axis=1)
    grad_first_both, grad_first_down = split(first_grads, first_gate_up, first_down)

    def own(whole_gain):
        return lax.dynamic_slice_in_dim(whole_gain.reshape(-1), place * gain_rows, gain_rows)

    return (
        loss_total,
        stream_four.astype(BF16)[None],
        input_grad[None],
        own(sum_mamba),
        grad_in,
        sum_kernel,
        sum_conv_bias[0],
        sum_select.T,
        sum_step_weight,
        sum_step_bias[0],
        sum_decay_log,
        sum_skip[0],
        grad_out,
        own(sum_attn),
        grad_qkv,
        grad_attn_out,
        own(sum_first),
        grad_first_both,
        grad_first_down,
        own(sum_second),
        second_both,
        second_down_grad,
    )


def solution(mesh):
    placed = (
        P("dp", "seq", None),
        P("dp", "seq", None),
        P(),
        P(("dp", "seq")),
        P(("dp", "seq"), None, "tensor"),
        P(None, "tensor"),
        P("tensor"),
        P("tensor", None),
        P(None, "tensor"),
        P("tensor"),
        P(None, "tensor"),
        P("tensor"),
        P(("dp", "seq"), "tensor"),
        P(("dp", "seq")),
        P(("dp", "seq"), None, "tensor"),
        P(("dp", "seq"), "tensor"),
        P(("dp", "seq")),
        P(("dp", "seq"), None, "tensor"),
        P(("dp", "seq"), "tensor"),
        P(("dp", "seq")),
        P(("dp", "seq"), None, "tensor"),
        P(("dp", "seq"), "tensor"),
    )
    return jax.shard_map(
        shards,
        mesh=mesh,
        in_specs=placed,
        out_specs=(
            P(),
            P("dp", "seq", None),
            P("dp", "seq", None),
            P(("dp", "seq")),
            P(("dp", "seq"), None, "tensor"),
            P(None, "tensor"),
            P("tensor"),
            P("tensor", None),
            P(None, "tensor"),
            P("tensor"),
            P(None, "tensor"),
            P("tensor"),
            P(("dp", "seq"), "tensor"),
            P(("dp", "seq")),
            P(("dp", "seq"), None, "tensor"),
            P(("dp", "seq"), "tensor"),
            P(("dp", "seq")),
            P(("dp", "seq"), None, "tensor"),
            P(("dp", "seq"), "tensor"),
            P(("dp", "seq")),
            P(("dp", "seq"), None, "tensor"),
            P(("dp", "seq"), "tensor"),
        ),
        check_vma=False,
    )
```

```python
import functools

import jax
import jax.numpy as jnp
from jax import lax
from jax.experimental import pallas as pl
from jax.experimental.pallas import tpu as pltpu
from jax.sharding import PartitionSpec as P

HD = 64
WINDOW = 2048
F32 = jnp.float32
BF16 = jnp.bfloat16
MESH = pl.DeviceIdType.MESH
LOG2E = 1.4426950408889634
LN2 = 0.6931471805599453

epsilon = 1e-05


def lasting(microseconds):
    return pl.CostEstimate(flops=int(microseconds * 1e7), bytes_accessed=0, transcendentals=0)

head_groups = 2


def state_kernel(dt_ref, dtx_ref, b_ref, rate_ref, out_ref, *, wide, chunk):
    @pl.when(pl.program_id(0) == 0)
    def _():
        out_ref[...] = jnp.zeros_like(out_ref)
    for j in range(out_ref.shape[1] // wide):
        cols = pl.ds(j * wide, wide)
        rate = rate_ref[:, cols]
        def group(g, h):
            base = pl.multiple_of(g * 8, 8)
            dts = dt_ref[pl.ds(base, 8), cols]
            dtxs = dtx_ref[pl.ds(base, 8), cols]
            for r in range(8):
                b = b_ref[base + r]
                b = jnp.concatenate([b] * (wide // 128), axis=1)
                h = jnp.exp2(dts[r:r+1] * rate) * h + b * dtxs[r:r+1]
            return h
        out_ref[:, cols] = lax.fori_loop(0, chunk // 8, group, out_ref[:, cols])

def scan_kernel(dt_ref, dtx_ref, b_ref, c_ref, rate_ref, h0_ref, y_ref, hp_ref, h_ref, *, wide, chunk):
    @pl.when(pl.program_id(0) == 0)
    def _():
        h_ref[...] = h0_ref[...]
    for j in range(h_ref.shape[1] // wide):
        cols = pl.ds(j * wide, wide)
        rate = rate_ref[:, cols]
        def group(g, h):
            base = pl.multiple_of(g * 8, 8)
            dts = dt_ref[pl.ds(base, 8), cols]
            dtxs = dtx_ref[pl.ds(base, 8), cols]
            ys = []
            for r in range(8):
                b = jnp.concatenate([b_ref[base + r]] * (wide // 128), axis=1)
                c = jnp.concatenate([c_ref[base + r]] * (wide // 128), axis=1)
                hp_ref[base + r, :, cols] = h
                h = jnp.exp2(dts[r:r+1] * rate) * h + b * dtxs[r:r+1]
                ys.append(jnp.sum(c * h, axis=0, keepdims=True))
            y_ref[pl.ds(base, 8), cols] = jnp.concatenate(ys, axis=0)
            return h
        h_ref[:, cols] = lax.fori_loop(0, chunk // 8, group, h_ref[:, cols])

def back_state_kernel(dt_ref, g_ref, c_ref, rate_ref, out_ref, *, wide, chunk):
    @pl.when(pl.program_id(0) == 0)
    def _():
        out_ref[...] = jnp.zeros_like(out_ref)
    for j in range(out_ref.shape[1] // wide):
        cols = pl.ds(j * wide, wide)
        rate = rate_ref[:, cols]
        def group(g, carry):
            base = pl.multiple_of(chunk - 8 - g * 8, 8)
            dts = dt_ref[pl.ds(base, 8), cols]
            gs = g_ref[pl.ds(base, 8), cols]
            for r in reversed(range(8)):
                c = jnp.concatenate([c_ref[base + r]] * (wide // 128), axis=1)
                carry = jnp.exp2(dts[r:r+1] * rate) * (carry + c * gs[r:r+1])
            return carry
        out_ref[:, cols] = lax.fori_loop(0, chunk // 8, group, out_ref[:, cols])

def back_kernel(dt_ref, x_ref, g_ref, b_ref, c_ref, rate_ref, hp_ref, l0_ref,
                gdt_ref, gx_ref, gb_out, gc_out, grate_ref, l_ref, gb_ref, gc_ref, *, wide, chunk):
    @pl.when(pl.program_id(0) == 0)
    def _():
        l_ref[...] = l0_ref[...]
        grate_ref[...] = jnp.zeros_like(grate_ref)
    for j in range(l_ref.shape[1] // wide):
        cols = pl.ds(j * wide, wide)
        rate = rate_ref[:, cols]
        def fold(v):
            out = v[:, :128]
            for i in range(1, wide // 128):
                out = out + v[:, i * 128:(i + 1) * 128]
            return out
        def group(g, state):
            carry, grate = state
            base = pl.multiple_of(chunk - 8 - g * 8, 8)
            dts = dt_ref[pl.ds(base, 8), cols]
            xs = x_ref[pl.ds(base, 8), cols].astype(F32)
            gs = g_ref[pl.ds(base, 8), cols]
            dtxs = dts * xs
            sw = [None] * 8
            sb = [None] * 8
            for r in reversed(range(8)):
                b = jnp.concatenate([b_ref[base + r]] * (wide // 128), axis=1)
                c = jnp.concatenate([c_ref[base + r]] * (wide // 128), axis=1)
                dt = dts[r:r+1]
                dtx = dtxs[r:r+1]
                gr = gs[r:r+1]
                da = jnp.exp2(dt * rate)
                q = da * hp_ref[base + r, :, cols]
                h = q + b * dtx
                lam = c * gr + carry
                w = lam * q
                carry = lam * da
                gb = fold(lam * dtx)
                gc = fold(h * gr)
                if j == 0:
                    gb_ref[base + r] = gb
                    gc_ref[base + r] = gc
                else:
                    gb_ref[base + r] += gb
                    gc_ref[base + r] += gc
                grate = grate + w * dt
                sw[r] = jnp.sum(w * rate, axis=0, keepdims=True)
                sb[r] = jnp.sum(lam * b, axis=0, keepdims=True)
            sbs = jnp.concatenate(sb, axis=0)
            sws = jnp.concatenate(sw, axis=0)
            gdt_ref[pl.ds(base, 8), cols] = sws * LN2 + xs * sbs
            gx_ref[pl.ds(base, 8), cols] = dts * sbs
            return carry, grate
        carry, grate = lax.fori_loop(0, chunk // 8, group, (l_ref[:, cols], grate_ref[:, cols]))
        l_ref[:, cols] = carry
        grate_ref[:, cols] = grate
    gb_out[...] = jnp.sum(gb_ref[...], axis=2)
    gc_out[...] = jnp.sum(gc_ref[...], axis=2)


SCAN_WIDE = 512


def scan_calls(rows, width, states):
    chunk = max(c for c in range(8, 57, 8) if rows % c == 0)
    steps = rows // chunk
    lanes = 128
    row = pl.BlockSpec((chunk, width), lambda i: (i, 0))
    maps = pl.BlockSpec((chunk, states, lanes), lambda i: (i, 0, 0))
    whole = pl.BlockSpec((states, width), lambda i: (0, 0))
    kept = pl.BlockSpec((chunk, states, width), lambda i: (i, 0, 0))
    row_back = pl.BlockSpec((chunk, width), lambda i: (steps - 1 - i, 0))
    maps_back = pl.BlockSpec((chunk, states, lanes), lambda i: (steps - 1 - i, 0, 0))
    narrow_back = pl.BlockSpec((chunk, states), lambda i: (steps - 1 - i, 0))
    kept_back = pl.BlockSpec((chunk, states, width), lambda i: (steps - 1 - i, 0, 0))

    def shape(*sizes):
        return jax.ShapeDtypeStruct(sizes, F32)

    params = pltpu.CompilerParams(vmem_limit_bytes=40 * 2**20)
    sizes = dict(wide=min(SCAN_WIDE, width), chunk=chunk)
    carried = [pltpu.VMEM((states, width), F32)]
    cells = rows * width * states
    state = pl.pallas_call(
        functools.partial(state_kernel, **sizes),
        grid=(steps,),
        in_specs=[row, row, maps, whole],
        out_specs=whole,
        out_shape=shape(states, width),
        compiler_params=params,
        cost_estimate=lasting(7),
        name="scan_state",
    )
    scan = pl.pallas_call(
        functools.partial(scan_kernel, **sizes),
        grid=(steps,),
        in_specs=[row, row, maps, maps, whole, whole],
        out_specs=[row, kept],
        out_shape=[shape(rows, width), shape(rows, states, width)],
        scratch_shapes=carried,
        compiler_params=params,
        cost_estimate=lasting(18),
        name="scan_rows",
    )
    back_state = pl.pallas_call(
        functools.partial(back_state_kernel, **sizes),
        grid=(steps,),
        in_specs=[row_back, row_back, maps_back, whole],
        out_specs=whole,
        out_shape=shape(states, width),
        compiler_params=params,
        cost_estimate=lasting(7),
        name="scan_back_state",
    )
    back = pl.pallas_call(
        functools.partial(back_kernel, **sizes),
        grid=(steps,),
        in_specs=[row_back, row_back, row_back, maps_back, maps_back, whole, kept_back, whole],
        out_specs=[row_back, row_back, narrow_back, narrow_back, whole],
        out_shape=[
            shape(rows, width),
            shape(rows, width),
            shape(rows, states),
            shape(rows, states),
            shape(states, width),
        ],
        scratch_shapes=carried + [pltpu.VMEM((chunk, states, lanes), F32)] * 2,
        compiler_params=params,
        cost_estimate=lasting(36),
        name="scan_back",
    )
    return state, scan, back_state, back


def gather_kernel(block_ref, out_ref, send, recv, own, *, axes):
    sizes = [lax.axis_size(a) for a in axes]
    total = 1
    for size in sizes:
        total *= size
    me = lax.axis_index(axes[0])
    for a in axes[1:]:
        me = me * lax.axis_size(a) + lax.axis_index(a)

    def coordinates(index):
        found = {}
        for a, size in zip(reversed(axes), reversed(sizes)):
            found[a] = lax.rem(index, size)
            index = index // size
        return found

    barrier = pltpu.get_barrier_semaphore()
    for step in range(1, total):
        pl.semaphore_signal(
            barrier, inc=1, device_id=coordinates(lax.rem(me + step, total)), device_id_type=MESH
        )
    pl.semaphore_wait(barrier, total - 1)
    mine = pltpu.make_async_copy(block_ref, out_ref.at[me], own)
    mine.start()
    copies = []
    for step in range(1, total):
        copy = pltpu.make_async_remote_copy(
            block_ref,
            out_ref.at[me],
            send.at[step],
            recv.at[step],
            device_id=coordinates(lax.rem(me + step, total)),
            device_id_type=MESH,
        )
        copy.start()
        copies.append(copy)
    mine.wait()
    for step in range(1, total):
        source = lax.rem(me - step + total, total)
        pltpu.make_async_remote_copy(
            block_ref,
            out_ref.at[source],
            send.at[step],
            recv.at[step],
            device_id=coordinates(source),
            device_id_type=MESH,
        ).wait_recv()
    for copy in copies:
        copy.wait_send()


def direct_gather(block, axes, identifier):
    total = 1
    for a in axes:
        total *= lax.axis_size(a)
    whole = pl.BlockSpec(memory_space=pltpu.VMEM)
    return pl.pallas_call(
        functools.partial(gather_kernel, axes=axes),
        out_shape=jax.ShapeDtypeStruct((total,) + block.shape, block.dtype),
        in_specs=[whole],
        out_specs=whole,
        scratch_shapes=[
            pltpu.SemaphoreType.DMA((total,)),
            pltpu.SemaphoreType.DMA((total,)),
            pltpu.SemaphoreType.DMA,
        ],
        compiler_params=pltpu.CompilerParams(
            collective_id=identifier, has_side_effects=True, vmem_limit_bytes=24 * 2**20
        ),
        name="gather_" + "_".join(axes),
        cost_estimate=lasting(6),
    )(block)


def ar_kernel(x_ref, out_ref, a_buf, b_buf, s_buf, a_send, a_recv, b_send, b_recv, c_send, c_recv, *, pieces, rows, lag):
    z = lax.axis_index("tensor")
    size = lax.axis_size("tensor")
    half = size // 2
    inner = (z == half - 1) | (z == half)
    low = z < half
    outer_dev = jnp.where(low, half - 2, half + 1)
    inner_dev = jnp.where(low, half - 1, half)
    other = jnp.where(low, half, half - 1)
    barrier = pltpu.get_barrier_semaphore()

    def at(ref, k):
        return ref.at[pl.ds(k * rows, rows)]

    def send_a(k):
        return pltpu.make_async_remote_copy(at(x_ref, k), at(a_buf, k), a_send.at[k], a_recv.at[k], device_id={"tensor": inner_dev}, device_id_type=MESH)
    def send_b(k):
        return pltpu.make_async_remote_copy(at(s_buf, k), at(b_buf, k), b_send.at[k], b_recv.at[k], device_id={"tensor": other}, device_id_type=MESH)
    def send_c(k):
        return pltpu.make_async_remote_copy(at(out_ref, k), at(out_ref, k), c_send.at[k], c_recv.at[k], device_id={"tensor": outer_dev}, device_id_type=MESH)

    @pl.when(jnp.logical_not(inner))
    def _():
        pl.semaphore_signal(barrier, inc=1, device_id={"tensor": inner_dev}, device_id_type=MESH)
        pl.semaphore_wait(barrier, 1)
        for k in range(pieces):
            send_a(k).start()
        for k in range(pieces):
            send_c(k).wait_recv()
        for k in range(pieces):
            send_a(k).wait_send()

    @pl.when(inner)
    def _():
        pl.semaphore_signal(barrier, inc=1, device_id={"tensor": outer_dev}, device_id_type=MESH)
        pl.semaphore_signal(barrier, inc=1, device_id={"tensor": other}, device_id_type=MESH)
        pl.semaphore_wait(barrier, 2)
        for t in range(pieces + lag):
            if t < pieces:
                send_a(t).wait_recv()
                part = pl.ds(t * rows, rows)
                s_buf[part] = (x_ref[part].astype(F32) + a_buf[part].astype(F32)).astype(BF16)
                send_b(t).start()
            if t >= lag:
                k = t - lag
                send_b(k).wait_recv()
                part = pl.ds(k * rows, rows)
                out_ref[part] = (s_buf[part].astype(F32) + b_buf[part].astype(F32)).astype(BF16)
                send_c(k).start()
        for k in range(pieces):
            send_b(k).wait_send()
            send_c(k).wait_send()


def tensor_sum(partial_sum, pieces, identifier):
    rows, width = partial_sum.shape
    lag = min(3, pieces)
    whole = pl.BlockSpec(memory_space=pltpu.VMEM)
    return pl.pallas_call(
        functools.partial(ar_kernel, pieces=pieces, rows=rows // pieces, lag=lag),
        out_shape=jax.ShapeDtypeStruct((rows, width), BF16),
        in_specs=[whole],
        out_specs=whole,
        scratch_shapes=[pltpu.VMEM((rows, width), BF16)] * 3
        + [pltpu.SemaphoreType.DMA((pieces,))] * 6,
        compiler_params=pltpu.CompilerParams(
            collective_id=identifier, has_side_effects=True, vmem_limit_bytes=24 * 2**20
        ),
        name="tensor_sum",
        cost_estimate=lasting(16),
    )(partial_sum)


def shifted(block, axis, distance):
    devices = range(lax.axis_size(axis))
    route = [(i - distance, i) for i in devices if i - distance in devices]
    return lax.ppermute(block, axis, route)


def product(left, right):
    return jnp.dot(left, right, preferred_element_type=F32)


def product_t(left, right):
    return lax.dot_general(
        left, right, (((1,), (1,)), ((), ())), preferred_element_type=F32
    )


def product_tl(left, right):
    return lax.dot_general(
        left, right, (((0,), (0,)), ((), ())), preferred_element_type=F32
    )


def norm_forward(values, gain_vec):
    inv_rms = lax.rsqrt(jnp.mean(values * values, axis=-1, keepdims=True) + epsilon)
    return values * inv_rms * gain_vec


def silu_slope(values):
    sigmoid_val = jax.nn.sigmoid(values)
    return sigmoid_val * (1.0 + values * (1.0 - sigmoid_val))


def join(*matrices):
    rows = matrices[0].shape[0]
    return jnp.concatenate([matrix.reshape(rows, -1) for matrix in matrices], axis=1)


def gather_joined(joined):
    return lax.all_gather(joined, ("dp", "seq"), axis=0, tiled=True)


def tensor_forward_sum(partial_sum):
    rows, width = partial_sum.shape
    low = partial_sum.astype(BF16)
    if width % 128:
        padded = jnp.pad(low, ((0, 0), (0, -width % 128)))
        return tensor_sum(padded, 11, 1)[:, :width].astype(F32)
    return tensor_sum(low, 33, 0).astype(F32)


tensor_backward_sum = tensor_forward_sum


def nt(a, b):
    return lax.dot_general(a, b, (((1,), (1,)), ((), ())), preferred_element_type=F32)

def nn(a, b):
    return lax.dot_general(a, b, (((1,), (0,)), ((), ())), preferred_element_type=F32)

def tn(a, b):
    return lax.dot_general(a, b, (((0,), (0,)), ((), ())), preferred_element_type=F32)

def head_lanes(shape, head):
    lane = lax.broadcasted_iota(jnp.int32, shape, 1)
    return (lane >= HD) if head else (lane < HD)

def seen(shape, hop, rows, query_axis):
    if hop * rows - (rows - 1) >= 0 and hop * rows + rows - 1 < WINDOW:
        return None
    distance = hop * rows + lax.broadcasted_iota(jnp.int32, shape, query_axis) - lax.broadcasted_iota(jnp.int32, shape, 1 - query_axis)
    return (distance >= 0) & (distance < WINDOW)

def seq_greet(place, count):
    barrier = pltpu.get_barrier_semaphore()
    for step in range(1, count):
        pl.semaphore_signal(
            barrier, inc=1, device_id={"seq": lax.rem(place + step, count)}, device_id_type=MESH
        )
    pl.semaphore_wait(barrier, count - 1)


def attend_kernel(
    q_ref, kv_ref, acc_ref, low_ref, top_ref, far_ref, total_ref, send, recv, *, count, hop_count
):
    rows = q_ref.shape[0]
    pairs = top_ref.shape[0]
    place = lax.axis_index("seq")
    scale = LOG2E * HD**-0.5
    seq_greet(place, count)

    def move(hop, device):
        return pltpu.make_async_remote_copy(
            kv_ref,
            far_ref.at[hop - 1],
            send.at[hop - 1],
            recv.at[hop - 1],
            device_id={"seq": device},
            device_id_type=MESH,
        )

    for hop in range(1, hop_count + 1):

        @pl.when(place + hop < count)
        def _(hop=hop):
            move(hop, place + hop).start()

    low = head_lanes((rows, 128), 0)

    def one_block(hop, pair):
        cols = pl.ds(pl.multiple_of(pair * 128, 128), 128)
        q = q_ref[:, cols]
        keys = kv_ref[0, :, cols] if hop == 0 else far_ref[hop - 1, 0, :, cols]
        values = kv_ref[1, :, cols] if hop == 0 else far_ref[hop - 1, 1, :, cols]
        mask = seen((rows, rows), hop, rows, 0)
        outs = []
        tops = []
        for head in range(2):
            mine = low if head == 0 else jnp.logical_not(low)
            s = nt(jnp.where(mine, q, jnp.zeros_like(q)), keys)
            if mask is not None:
                s = jnp.where(mask, s, -1e30)
            top = jnp.max(s, axis=1, keepdims=True)
            if hop > 0:
                top = jnp.maximum(top, top_ref[pair, :, pl.ds(head * HD, 1)])
            p = jnp.exp2((s - top) * scale).astype(BF16)
            outs.append(nn(p, jnp.where(mine, values, jnp.ones_like(values))))
            tops.append(top)
        top = jnp.where(low, tops[0], tops[1])
        acc = jnp.where(low, outs[0], outs[1])
        total = pltpu.roll(jnp.where(low, outs[1], outs[0]), HD, 1)
        if hop > 0:
            fade = jnp.exp2((top_ref[pair] - top) * scale)
            acc = acc + acc_ref[:, cols] * fade
            total = total + total_ref[pair] * fade
        acc_ref[:, cols] = acc
        top_ref[pair] = top
        total_ref[pair] = total

    def all_pairs(hop):
        def one(pair, carry):
            one_block(hop, pair)
            return carry

        lax.fori_loop(0, pairs, one, 0)

    all_pairs(0)
    for hop in range(1, hop_count + 1):

        @pl.when(place >= hop)
        def _(hop=hop):
            move(hop, place - hop).wait_recv()
            all_pairs(hop)

    def finish(pair, carry):
        cols = pl.ds(pl.multiple_of(pair * 128, 128), 128)
        total = total_ref[pair]
        acc = acc_ref[:, cols] / total
        acc_ref[:, cols] = acc
        low_ref[:, cols] = acc.astype(BF16)
        top_ref[pair] = top_ref[pair] * scale + jnp.log2(total)
        return carry

    lax.fori_loop(0, pairs, finish, 0)
    for hop in range(1, hop_count + 1):

        @pl.when(place + hop < count)
        def _(hop=hop):
            move(hop, place + hop).wait_send()


def attend(q, kv, hop_count, identifier):
    rows, width = q.shape
    pairs = width // 128
    whole = pl.BlockSpec(memory_space=pltpu.VMEM)
    return pl.pallas_call(
        functools.partial(attend_kernel, count=lax.axis_size("seq"), hop_count=hop_count),
        in_specs=[whole] * 2,
        out_specs=[whole] * 4,
        out_shape=[
            jax.ShapeDtypeStruct((rows, width), F32),
            jax.ShapeDtypeStruct((rows, width), BF16),
            jax.ShapeDtypeStruct((pairs, rows, 128), F32),
            jax.ShapeDtypeStruct((hop_count, 2, rows, width), BF16),
        ],
        scratch_shapes=[
            pltpu.VMEM((pairs, rows, 128), F32),
            pltpu.SemaphoreType.DMA((hop_count,)),
            pltpu.SemaphoreType.DMA((hop_count,)),
        ],
        compiler_params=pltpu.CompilerParams(
            collective_id=identifier, has_side_effects=True, vmem_limit_bytes=48 * 2**20
        ),
        cost_estimate=lasting(55),
        name="attend",
    )(q, kv)


def attend_back_kernel(
    q_ref,
    g_ref,
    o_ref,
    lse_ref,
    kv_ref,
    far_ref,
    cosine_ref,
    sine_ref,
    out_ref,
    lines,
    dq_ref,
    dkv_ref,
    leaving,
    landed,
    send,
    recv,
    *,
    count,
    hop_count,
):
    rows, width = q_ref.shape
    pairs = width // 128
    place = lax.axis_index("seq")
    scale = HD**-0.5
    seq_greet(place, count)

    def columns(pair):
        return pl.ds(pl.multiple_of(pair * 128, 128), 128)

    def move(hop, pair, device):
        return pltpu.make_async_remote_copy(
            leaving.at[hop - 1, :, :, columns(pair)],
            landed.at[hop - 1, :, :, columns(pair)],
            send.at[hop - 1, pair],
            recv.at[hop - 1, pair],
            device_id={"seq": device},
            device_id_type=MESH,
        )

    def prepare(pair, carry):
        cols = columns(pair)
        turned = jnp.transpose(lse_ref[pair])
        dots = jnp.transpose(o_ref[:, cols] * g_ref[:, cols].astype(F32))
        lines[pair, 0:1] = turned[0:1]
        lines[pair, 1:2] = turned[HD : HD + 1]
        lines[pair, 2:3] = jnp.sum(dots[:HD], axis=0, keepdims=True)
        lines[pair, 3:4] = jnp.sum(dots[HD:], axis=0, keepdims=True)
        dq_ref[:, cols] = jnp.zeros((rows, 128), F32)
        return carry

    lax.fori_loop(0, pairs, prepare, 0)

    def one_block(hop, pair):
        cols = columns(pair)
        q = q_ref[:, cols]
        g = g_ref[:, cols]
        k = kv_ref[0, :, cols] if hop == 0 else far_ref[hop - 1, 0, :, cols]
        v = kv_ref[1, :, cols] if hop == 0 else far_ref[hop - 1, 1, :, cols]
        mask = seen((rows, rows), hop, rows, 1)
        dk = jnp.zeros((rows, 128), F32)
        dv = jnp.zeros((rows, 128), F32)
        dq = dq_ref[:, cols]
        for head in range(2):
            mine = head_lanes((rows, 128), head)
            qm = jnp.where(mine, q, jnp.zeros_like(q))
            gm = jnp.where(mine, g, jnp.zeros_like(g))
            km = jnp.where(mine, k, jnp.zeros_like(k))
            s = nt(k, qm) * (LOG2E * scale)
            p = jnp.exp2(s - lines[pair, head : head + 1])
            if mask is not None:
                p = jnp.where(mask, p, 0.0)
            dv = dv + nn(p.astype(BF16), gm)
            dp = nt(v, gm)
            ds = (p * (dp - lines[pair, head + 2 : head + 3])).astype(BF16)
            dk = dk + nn(ds, qm)
            dq = dq + tn(ds, km) * scale
        dq_ref[:, cols] = dq
        return dk * scale, dv

    for hop in reversed(range(1, hop_count + 1)):

        @pl.when(place >= hop)
        def _(hop=hop):
            def one(pair, carry):
                dk, dv = one_block(hop, pair)
                leaving[hop - 1, 0, :, columns(pair)] = dk.astype(BF16)
                leaving[hop - 1, 1, :, columns(pair)] = dv.astype(BF16)
                move(hop, pair, place - hop).start()
                return carry

            lax.fori_loop(0, pairs, one, 0)

    def own(pair, carry):
        dk, dv = one_block(0, pair)
        dkv_ref[0, :, columns(pair)] = dk
        dkv_ref[1, :, columns(pair)] = dv
        return carry

    lax.fori_loop(0, pairs, own, 0)

    for hop in range(1, hop_count + 1):

        @pl.when(place + hop < count)
        def _(hop=hop):
            def one(pair, carry):
                cols = columns(pair)
                move(hop, pair, place + hop).wait_recv()
                for which in range(2):
                    dkv_ref[which, :, cols] += landed[hop - 1, which, :, cols].astype(F32)
                return carry

            lax.fori_loop(0, pairs, one, 0)

    def finish(pair, carry):
        cols = columns(pair)
        cosine, sine = cosine_ref[...], sine_ref[...]

        def turned(values):
            return turn(values.astype(BF16).astype(F32), cosine, sine, -1.0).astype(BF16)

        def later(part):
            return pl.ds(pl.multiple_of(part * width + pair * 128, 128), 128)

        out_ref[:, cols] = turned(dq_ref[:, cols])
        out_ref[:, later(1)] = turned(dkv_ref[0, :, cols])
        out_ref[:, later(2)] = dkv_ref[1, :, cols].astype(BF16)
        return carry

    lax.fori_loop(0, pairs, finish, 0)
    for hop in range(1, hop_count + 1):

        @pl.when(place >= hop)
        def _(hop=hop):
            def one(pair, carry):
                move(hop, pair, place - hop).wait_send()
                return carry

            lax.fori_loop(0, pairs, one, 0)


def attend_back(q, g, o, lse, kv, far, cosine, sine, identifier):
    rows, width = q.shape
    pairs = width // 128
    hop_count = far.shape[0]
    whole = pl.BlockSpec(memory_space=pltpu.VMEM)
    return pl.pallas_call(
        functools.partial(attend_back_kernel, count=lax.axis_size("seq"), hop_count=hop_count),
        in_specs=[whole] * 8,
        out_specs=whole,
        out_shape=jax.ShapeDtypeStruct((rows, 3 * width), BF16),
        scratch_shapes=[
            pltpu.VMEM((pairs, 8, rows), F32),
            pltpu.VMEM((rows, width), F32),
            pltpu.VMEM((2, rows, width), F32),
            pltpu.VMEM((hop_count, 2, rows, width), BF16),
            pltpu.VMEM((hop_count, 2, rows, width), BF16),
            pltpu.SemaphoreType.DMA((hop_count, pairs)),
            pltpu.SemaphoreType.DMA((hop_count, pairs)),
        ],
        compiler_params=pltpu.CompilerParams(
            collective_id=identifier, has_side_effects=True, vmem_limit_bytes=48 * 2**20
        ),
        cost_estimate=lasting(55),
        name="attend_back",
    )(q, g, o, lse, kv, far, cosine, sine)


def partners(values):
    lane = lax.broadcasted_iota(jnp.int32, values.shape, 1)
    half = HD // 2
    return jnp.where(
        lax.rem(lane, HD) < half, pltpu.roll(values, 128 - half, 1), pltpu.roll(values, half, 1)
    )


def turn(values, cosine, sine, sign):
    parts = []
    for first in range(0, values.shape[1], 128):
        piece = values[:, first : first + 128]
        parts.append(piece * cosine + partners(piece) * (sine * sign))
    return jnp.concatenate(parts, axis=1) if len(parts) > 1 else parts[0]


def rope_tables(positions):
    half = HD // 2
    frequency = 10000.0 ** (-jnp.arange(half, dtype=F32) / half)
    angles = positions.astype(F32)[:, None] * frequency[None, :]
    cosine, sine = jnp.cos(angles), jnp.sin(angles)
    return jnp.tile(cosine, (1, 4)), jnp.tile(jnp.concatenate([-sine, sine], axis=1), (1, 2))


def qkv_kernel(x_ref, w_ref, cosine_ref, sine_ref, q_ref, kv_ref, *, tiles):
    step = pl.program_id(0)
    result = nn(x_ref[...], w_ref[...])
    turned = turn(result, cosine_ref[...], sine_ref[...], 1.0)

    @pl.when(step < tiles)
    def _():
        q_ref[...] = turned.astype(BF16)

    @pl.when(step >= tiles)
    def _():
        kv_ref[0] = jnp.where(step < 2 * tiles, turned, result).astype(BF16)


def qkv_rows(x, w, first_column, width, cosine, sine):
    rows, depth = x.shape
    tile = 256
    tiles = width // tile
    skip = first_column // tile
    table = pl.BlockSpec((rows, 128), lambda j: (0, 0))

    def kv_at(j):
        later = jnp.maximum(j - tiles, 0)
        return later // tiles, 0, lax.rem(later, tiles)

    return pl.pallas_call(
        functools.partial(qkv_kernel, tiles=tiles),
        grid=(3 * tiles,),
        in_specs=[
            pl.BlockSpec((rows, depth), lambda j: (0, 0)),
            pl.BlockSpec((depth, tile), lambda j: (0, j + skip)),
            table,
            table,
        ],
        out_specs=[
            pl.BlockSpec((rows, tile), lambda j: (0, jnp.minimum(j, tiles - 1))),
            pl.BlockSpec((1, rows, tile), kv_at),
        ],
        out_shape=[
            jax.ShapeDtypeStruct((rows, width), BF16),
            jax.ShapeDtypeStruct((2, rows, width), BF16),
        ],
        compiler_params=pltpu.CompilerParams(vmem_limit_bytes=32 * 2**20),
        cost_estimate=lasting(8),
        name="qkv_rows",
    )(x, w, cosine, sine)


def sigmoid(v):
    return 1.0 / (1.0 + jnp.exp(-v))

def gate_up_kernel(x_ref, wg_ref, wu_ref, gate_ref, up_ref, hid_ref):
    x = x_ref[...]
    gate = nn(x, wg_ref[...])
    up = nn(x, wu_ref[...])
    gate_ref[...] = gate.astype(BF16)
    up_ref[...] = up.astype(BF16)
    hid_ref[...] = (gate * sigmoid(gate) * up).astype(BF16)

def gate_up(x, w, tile):
    rows, depth = x.shape
    units = w.shape[1] // 3
    steps = units // tile
    col = pl.BlockSpec((rows, tile), lambda j: (0, j))
    out = jax.ShapeDtypeStruct((rows, units), BF16)
    return pl.pallas_call(gate_up_kernel, grid=(steps,),
        in_specs=[pl.BlockSpec((rows, depth), lambda j: (0, 0)), pl.BlockSpec((depth, tile), lambda j: (0, j)), pl.BlockSpec((depth, tile), lambda j: (0, j + steps))],
        out_specs=[col] * 3, out_shape=[out] * 3, compiler_params=pltpu.CompilerParams(vmem_limit_bytes=40 * 2**20),
        cost_estimate=lasting(14), name="gate_up")(x, w, w)

def hidden_back_kernel(g_ref, w_ref, gate_ref, up_ref, gg_ref, gu_ref):
    gh = nn(g_ref[...], w_ref[...])
    gate = gate_ref[...].astype(F32)
    up = up_ref[...].astype(F32)
    sig = sigmoid(gate)
    gg_ref[...] = (gh * up * (sig * (1.0 + gate * (1.0 - sig)))).astype(BF16)
    gu_ref[...] = (gh * (gate * sig)).astype(BF16)

def hidden_back(g, w, gate, up, tile):
    rows, depth = g.shape
    units = w.shape[1] // 3
    steps = units // tile
    col = pl.BlockSpec((rows, tile), lambda j: (0, j))
    out = jax.ShapeDtypeStruct((rows, units), BF16)
    return pl.pallas_call(hidden_back_kernel, grid=(steps,),
        in_specs=[pl.BlockSpec((rows, depth), lambda j: (0, 0)), pl.BlockSpec((depth, tile), lambda j: (0, j + 2 * steps)), col, col],
        out_specs=[col] * 2, out_shape=[out] * 2, compiler_params=pltpu.CompilerParams(vmem_limit_bytes=40 * 2**20),
        cost_estimate=lasting(10), name="hidden_back")(g, w, gate, up)

def weight_grads_kernel(*refs, counts):
    n = len(counts)
    lhs, rhs, out_ref, turned = refs[:n], refs[n:2 * n], refs[2 * n], refs[2 * n + 1]
    step = pl.program_id(0)
    first = 0
    for which in range(n):
        @pl.when(step == first)
        def _():
            turned[...] = jnp.transpose(lhs[which][...])
        @pl.when((step >= first) & (step < first + counts[which]))
        def _():
            out_ref[...] = nn(turned[...], rhs[which][...]).astype(BF16)
        first += counts[which]

def weight_grads(pairs, tile):
    rows, depth = pairs[0][0].shape
    counts = [right.shape[1] // tile for _, right in pairs]
    total = sum(counts)
    starts = [sum(counts[:i]) for i in range(len(counts))]
    whole = pl.BlockSpec((rows, depth), lambda j: (0, 0))
    def spec(start, count):
        return pl.BlockSpec((rows, tile), lambda j: (0, jnp.clip(j - start, 0, count - 1)))
    return pl.pallas_call(functools.partial(weight_grads_kernel, counts=counts), grid=(total,),
        in_specs=[whole] * len(pairs) + [spec(s, c) for s, c in zip(starts, counts)],
        out_specs=pl.BlockSpec((depth, tile), lambda j: (0, j)),
        out_shape=jax.ShapeDtypeStruct((depth, total * tile), BF16),
        scratch_shapes=[pltpu.VMEM((depth, rows), BF16)],
        compiler_params=pltpu.CompilerParams(vmem_limit_bytes=40 * 2**20),
        cost_estimate=lasting(1.25 * total), name="weight_grads")(
        *[left for left, _ in pairs], *[right for _, right in pairs])

def group_place(axes):
    me = lax.axis_index(axes[0])
    for a in axes[1:]:
        me = me * lax.axis_size(a) + lax.axis_index(a)
    return me


def group_device(axes, index):
    found = {}
    for a in reversed(axes):
        found[a] = lax.rem(index, lax.axis_size(a))
        index = index // lax.axis_size(a)
    return found


class SmallSum:
    axes = ("dp", "seq")

    def __init__(self, x_ref, out_ref, arrived, total, send, recv, send_out, recv_out):
        self.x_ref, self.out_ref, self.arrived, self.total = x_ref, out_ref, arrived, total
        self.sems = (send, recv, send_out, recv_out)
        self.count = x_ref.shape[0]
        self.me = group_place(self.axes)

    def to(self, step):
        return lax.rem(self.me + step, self.count)

    def back(self, step):
        return lax.rem(self.me - step + self.count, self.count)

    def greet(self, barrier):
        for step in range(1, self.count):
            pl.semaphore_signal(
                barrier,
                inc=1,
                device_id=group_device(self.axes, self.to(step)),
                device_id_type=MESH,
            )
        return self.count - 1

    def part(self, step, device):
        return pltpu.make_async_remote_copy(
            self.x_ref.at[device],
            self.arrived.at[step],
            self.sems[0].at[step],
            self.sems[1].at[step],
            device_id=group_device(self.axes, device),
            device_id_type=MESH,
        )

    def whole(self, step, slot, device):
        return pltpu.make_async_remote_copy(
            self.total,
            self.out_ref.at[slot],
            self.sems[2].at[step],
            self.sems[3].at[step],
            device_id=group_device(self.axes, device),
            device_id_type=MESH,
        )

    def begin(self):
        for step in range(1, self.count):
            self.part(step, self.to(step)).start()

    def middle(self):
        result = self.x_ref[self.me].astype(F32)
        for step in range(1, self.count):
            self.part(step, self.back(step)).wait_recv()
            result = result + self.arrived[step].astype(F32)
        self.total[...] = result.astype(BF16)
        self.out_ref[self.me] = result.astype(BF16)
        for step in range(1, self.count):
            self.whole(step, self.me, self.to(step)).start()

    def end(self):
        for step in range(1, self.count):
            self.whole(step, self.back(step), self.back(step)).wait_recv()
        for step in range(1, self.count):
            self.part(step, self.to(step)).wait_send()
            self.whole(step, self.me, self.to(step)).wait_send()


class OwnGrads:
    lag = 0

    def __init__(self, lefts, rights, uses, counts, tile, out_ref, scratch):
        self.lefts, self.rights, self.uses, self.counts, self.tile = lefts, rights, uses, counts, tile
        self.out_ref = out_ref
        self.turned, self.staged, self.out_sem = scratch
        self.total = sum(counts)

    @staticmethod
    def scratch(rows, depth, total, tile):
        return [
            pltpu.VMEM((depth, rows), BF16),
            pltpu.VMEM((2, depth, tile), BF16),
            pltpu.SemaphoreType.DMA((2,)),
        ]

    def put(self, t):
        slot = lax.rem(t, 2)
        return pltpu.make_async_copy(
            self.staged.at[slot],
            self.out_ref.at[:, pl.ds(pl.multiple_of(t * self.tile, self.tile), self.tile)],
            self.out_sem.at[slot],
        )

    def turn(self, which):
        self.turned[...] = jnp.transpose(self.lefts[self.uses[which]][...])

    def step(self, t):
        first = 0
        for which, count in enumerate(self.counts):
            if which == 0 or self.uses[which] != self.uses[which - 1]:

                @pl.when(t == first)
                def _(which=which):
                    self.turn(which)

            @pl.when((t >= first) & (t < first + count))
            def _(which=which, first=first):
                self.multiply(which, t - first, t)

            first += count

    def greet(self, barrier):
        return 0

    def multiply(self, which, index, t):
        slot = lax.rem(t, 2)
        block = self.rights[which][:, pl.ds(pl.multiple_of(index * self.tile, self.tile), self.tile)]

        @pl.when(t >= 2)
        def _():
            self.put(t - 2).wait()

        self.staged[slot] = nn(self.turned[...], block).astype(BF16)
        self.put(t).start()

    def end(self):
        for t in (self.total - 2, self.total - 1):
            self.put(t).wait()


class ScatterGrads(OwnGrads):
    lags = (1, 3, 5)
    lag = 5

    def __init__(self, lefts, rights, uses, counts, tile, out_ref, scratch):
        self.lefts, self.rights, self.uses, self.counts, self.tile = lefts, rights, uses, counts, tile
        self.out_ref = out_ref
        self.turned, self.sent, self.kept, self.landed, self.crossed, self.last = scratch[:6]
        self.sems = scratch[6:]
        self.total = sum(counts)
        self.dp = lax.axis_index("dp")
        place = lax.axis_index("seq")
        self.low, self.high = lax.rem(place, 2), place // 2
        self.beside = self.high * 2 + 1 - self.low
        self.across = (1 - self.high) * 2 + self.low
        self.half = self.turned.shape[0] // 2
        self.block = self.half // 4

    @staticmethod
    def scratch(rows, depth, total, tile):
        half = depth // 2
        return [
            pltpu.VMEM((depth, rows), BF16),
            pltpu.VMEM((2, half, tile), BF16),
            pltpu.VMEM((3, half, tile), F32),
            pltpu.VMEM((total, half, tile), BF16),
            pltpu.VMEM((total, 2, half // 4, tile), BF16),
            pltpu.VMEM((total, half // 4, tile), BF16),
            pltpu.SemaphoreType.DMA((2, total)),
            pltpu.SemaphoreType.DMA((total, 2)),
            pltpu.SemaphoreType.DMA((total, 2)),
            pltpu.SemaphoreType.DMA((total,)),
            pltpu.SemaphoreType.DMA((total,)),
        ]

    def greet(self, barrier):
        for device in ({"dp": 1 - self.dp}, {"seq": self.beside}, {"seq": self.across}):
            pl.semaphore_signal(barrier, inc=1, device_id=device, device_id_type=MESH)
        return 3

    def part(self, which):
        return self.turned[pl.ds(pl.multiple_of(which * self.half, self.half), self.half)]

    def to_core(self, t):
        return pltpu.make_async_remote_copy(
            self.sent.at[lax.rem(t, 2)],
            self.landed.at[t],
            self.sems[0].at[0, t],
            self.sems[0].at[1, t],
            device_id={"dp": 1 - self.dp},
            device_id_type=MESH,
        )

    def rows(self, index):
        return pl.ds(pl.multiple_of(index * self.block, self.block), self.block)

    def even(self, t, if_even, if_odd):
        return jnp.where(lax.rem(t, 2) == 0, if_even, if_odd)

    def to_first(self, t, k):
        index = self.even(t, 2 * k + 1 - self.low, (1 - self.high) * 2 + k)
        return pltpu.make_async_remote_copy(
            self.landed.at[t, self.rows(index)],
            self.crossed.at[t, k],
            self.sems[1].at[t, k],
            self.sems[2].at[t, k],
            device_id={"seq": self.even(t, self.beside, self.across)},
            device_id_type=MESH,
        )

    def to_second(self, t):
        return pltpu.make_async_remote_copy(
            self.crossed.at[t, self.even(t, 1 - self.high, 1 - self.low)],
            self.last.at[t],
            self.sems[3].at[t],
            self.sems[4].at[t],
            device_id={"seq": self.even(t, self.across, self.beside)},
            device_id_type=MESH,
        )

    def multiply(self, which, index, t):
        slot = lax.rem(t, 2)
        block = self.rights[which][:, pl.ds(pl.multiple_of(index * self.tile, self.tile), self.tile)]

        @pl.when(t >= 2)
        def _():
            self.to_core(t - 2).wait_send()

        self.sent[slot] = nn(self.part(1 - self.dp), block).astype(BF16)
        self.to_core(t).start()
        self.kept[lax.rem(t, 3)] = nn(self.part(self.dp), block)

    def core_sum(self, t):
        self.to_core(t).wait_recv()
        self.landed[t] = (self.kept[lax.rem(t, 3)] + self.landed[t].astype(F32)).astype(BF16)
        for k in range(2):
            self.to_first(t, k).start()

    def first_chip_sum(self, t):
        for k in range(2):
            self.to_first(t, k).wait_recv()
            index = self.even(t, 2 * k + self.low, self.high * 2 + k)
            own = self.landed[t, self.rows(index)].astype(F32)
            self.crossed[t, k] = (own + self.crossed[t, k].astype(F32)).astype(BF16)
        self.to_second(t).start()

    def second_chip_sum(self, t):
        self.to_second(t).wait_recv()
        own = self.crossed[t, self.even(t, self.high, self.low)].astype(F32)
        self.out_ref[:, pl.ds(pl.multiple_of(t * self.tile, self.tile), self.tile)] = (
            own + self.last[t].astype(F32)
        ).astype(BF16)

    def step(self, t):
        super().step(t)
        works = (self.core_sum, self.first_chip_sum, self.second_chip_sum)
        for late, work in zip(self.lags, works):

            @pl.when((t >= late) & (t < self.total + late))
            def _(late=late, work=work):
                work(t - late)

    def end(self):
        for t in (self.total - 2, self.total - 1):
            self.to_core(t).wait_send()

        def finish(t, carry):
            for k in range(2):
                self.to_first(t, k).wait_send()
            self.to_second(t).wait_send()
            return carry

        lax.fori_loop(0, self.total, finish, 0)


def grad_operands(pairs, xs):
    lefts, uses = [], []
    for left, _ in pairs:
        known = [i for i, other in enumerate(lefts) if other is left]
        uses.append(known[0] if known else len(lefts))
        if not known:
            lefts.append(left)
    shared = []
    rights = []
    for _, right in pairs:
        same = [i for i, x in enumerate(xs) if x is right]
        shared.append(same[0] if same else -1)
        if not same:
            rights.append(right)
    return lefts, rights, uses, shared


def matmul_sum_kernel(
    *refs, columns, first_column, tile, splits, with_small, uses, shared, counts, job_kind
):
    refs = list(refs)

    def take(count):
        taken = refs[:count]
        del refs[:count]
        return taken

    xs = take(len(columns))
    (w_ref,) = take(1)
    small_in = take(1 if with_small else 0)
    lefts = take(max(uses) + 1 if uses else 0)
    others = take(sum(which < 0 for which in shared))
    rights = [xs[which] if which >= 0 else others.pop(0) for which in shared]
    (out_ref,) = take(1)
    small_out = take(1 if with_small else 0)
    grads_out = take(1 if uses else 0)
    w_buf, part, a_buf, b_buf, w_sem, a_send, a_recv, b_send, b_recv, c_send, c_recv = take(11)
    small = SmallSum(*small_in, *small_out, *take(6)) if with_small else None
    job = None
    if uses:
        job = job_kind(lefts, rights, uses, counts, tile, *grads_out, refs)
    rows, depth = out_ref.shape
    tiles = depth // tile
    short = rows // splits
    wide = sum(columns)
    z = lax.axis_index("tensor")
    half = lax.axis_size("tensor") // 2
    inner = (z == half - 1) | (z == half)
    low = z < half
    outer_dev = jnp.where(low, half - 2, half + 1)
    inner_dev = jnp.where(low, half - 1, half)
    other = jnp.where(low, half, half - 1)
    barrier = pltpu.get_barrier_semaphore()

    def weights(j, slot):
        return pltpu.make_async_copy(
            w_ref.at[pl.ds(pl.multiple_of(j * tile, tile), tile), pl.ds(first_column, wide)],
            w_buf.at[slot],
            w_sem.at[slot],
        )

    def cells(ref, j, r):
        return ref.at[pl.ds(r * short, short), pl.ds(pl.multiple_of(j * tile, tile), tile)]

    def send(src, dst, sems, j, r, device):
        return pltpu.make_async_remote_copy(
            cells(src, j, r),
            cells(dst, j, r),
            sems[0].at[j, r],
            sems[1].at[j, r],
            device_id={"tensor": device},
            device_id_type=MESH,
        )

    def send_a(j, r):
        return send(part, a_buf, (a_send, a_recv), j, r, inner_dev)

    def send_b(j, r):
        return send(part, b_buf, (b_send, b_recv), j, r, other)

    def send_c(j, r):
        return send(out_ref, out_ref, (c_send, c_recv), j, r, outer_dev)

    weights(0, 0).start()
    greeted = (small.greet(barrier) if with_small else 0) + (job.greet(barrier) if uses else 0)

    @pl.when(jnp.logical_not(inner))
    def _():
        pl.semaphore_signal(barrier, inc=1, device_id={"tensor": inner_dev}, device_id_type=MESH)
        pl.semaphore_wait(barrier, 1 + greeted)

    @pl.when(inner)
    def _():
        pl.semaphore_signal(barrier, inc=1, device_id={"tensor": outer_dev}, device_id_type=MESH)
        pl.semaphore_signal(barrier, inc=1, device_id={"tensor": other}, device_id_type=MESH)
        pl.semaphore_wait(barrier, 2 + greeted)

    if with_small:
        small.begin()

    def first_sum(j, r):
        send_a(j, r).wait_recv()
        mine = cells(part, j, r)
        mine[...] = (mine[...].astype(F32) + cells(a_buf, j, r)[...].astype(F32)).astype(BF16)
        send_b(j, r).start()

    def second_sum(j, r):
        send_b(j, r).wait_recv()
        cells(out_ref, j, r)[...] = (
            cells(part, j, r)[...].astype(F32) + cells(b_buf, j, r)[...].astype(F32)
        ).astype(BF16)
        send_c(j, r).start()

    lag = splits - 1

    def one_tile(j, carry):
        slot = lax.rem(j, 2)
        weights(j, slot).wait()

        @pl.when(j + 1 < tiles)
        def _():
            weights(j + 1, 1 - slot).start()

        total = None
        first = 0
        for x_ref, count in zip(xs, columns):
            term = nt(x_ref[...], w_buf[slot, :, pl.ds(first, count)])
            total = term if total is None else total + term
            first += count
        part[:, pl.ds(pl.multiple_of(j * tile, tile), tile)] = total.astype(BF16)

        @pl.when(jnp.logical_not(inner))
        def _():
            for r in range(splits):
                send_a(j, r).start()

        each = (job.total + job.lag) // tiles if uses else 0
        for r in range(max(splits, each)):
            if r < splits:

                @pl.when(inner)
                def _(r=r):
                    first_sum(j, r)
                    if r >= lag:
                        second_sum(j, r - lag)
                    else:

                        @pl.when(j > 0)
                        def _():
                            second_sum(j - 1, r + splits - lag)

            if r < each:
                job.step(j * each + r)

        return carry

    if with_small:
        lax.fori_loop(0, tiles // 2, one_tile, 0)
        small.middle()
        lax.fori_loop(tiles // 2, tiles, one_tile, 0)
    else:
        lax.fori_loop(0, tiles, one_tile, 0)

    @pl.when(inner)
    def _():
        for r in range(splits - lag, splits):
            second_sum(tiles - 1, r)

    if uses:
        for t in range((job.total + job.lag) // tiles * tiles, job.total + job.lag):
            job.step(t)

    @pl.when(inner)
    def _():

        def finish(j, carry):
            for r in range(splits):
                send_b(j, r).wait_send()
                send_c(j, r).wait_send()
            return carry

        lax.fori_loop(0, tiles, finish, 0)

    @pl.when(jnp.logical_not(inner))
    def _():
        def finish(j, carry):
            for r in range(splits):
                send_c(j, r).wait_recv()
                send_a(j, r).wait_send()
            return carry

        lax.fori_loop(0, tiles, finish, 0)

    if with_small:
        small.end()
    if uses:
        job.end()


def matmul_sum(
    xs, w, first_column, identifier, small=None, pairs=None, scatter=False, tile=256, splits=3
):
    rows = xs[0].shape[0]
    depth = w.shape[0]
    columns = [x.shape[1] for x in xs]
    wide = sum(columns)
    whole = pl.BlockSpec(memory_space=pltpu.VMEM)
    far = pl.BlockSpec(memory_space=pltpu.HBM)
    tiles = depth // tile
    out_shape = [jax.ShapeDtypeStruct((rows, depth), BF16)]
    out_specs = [whole]
    scratch = (
        [pltpu.VMEM((2, tile, wide), BF16)]
        + [pltpu.VMEM((rows, depth), BF16)] * 3
        + [pltpu.SemaphoreType.DMA((2,))]
        + [pltpu.SemaphoreType.DMA((tiles, splits))] * 6
    )
    extra = ()
    if small is not None:
        extra = (small,)
        out_shape.append(jax.ShapeDtypeStruct(small.shape, BF16))
        out_specs.append(whole)
        scratch += [pltpu.VMEM(small.shape, BF16), pltpu.VMEM(small.shape[1:], BF16)]
        scratch += [pltpu.SemaphoreType.DMA((small.shape[0],))] * 4
    uses, shared, counts, job_kind = (), (), (), None
    if pairs is not None:
        job_kind = ScatterGrads if scatter else OwnGrads
        lefts, rights, uses, shared = grad_operands(pairs, xs)
        counts = [right.shape[1] // tile for _, right in pairs]
        extra = (*extra, *lefts, *rights)
        height = depth // 8 if scatter else depth
        out_shape.append(jax.ShapeDtypeStruct((height, sum(counts) * tile), BF16))
        out_specs.append(whole if scatter else far)
        scratch += job_kind.scratch(rows, depth, sum(counts), tile)
    results = pl.pallas_call(
        functools.partial(
            matmul_sum_kernel,
            columns=columns,
            first_column=first_column,
            tile=tile,
            splits=splits,
            with_small=small is not None,
            uses=uses,
            shared=shared,
            counts=counts,
            job_kind=job_kind,
        ),
        out_shape=out_shape,
        in_specs=[whole] * len(xs) + [far] + [whole] * len(extra),
        out_specs=out_specs,
        scratch_shapes=scratch,
        compiler_params=pltpu.CompilerParams(
            collective_id=identifier, has_side_effects=True, vmem_limit_bytes=(40 if pairs is None else 44) * 2**20
        ),
        cost_estimate=lasting(58 if pairs is None else 67),
        name="matmul_sum" + ("_small" if small is not None else "_grads" if uses else ""),
    )(*xs, w, *extra)
    return results if extra else results[0]


def norm_back_kernel(v_ref, gain_ref, normed_ref, out_ref, total_ref, low_ref, gain_out):
    @pl.when(pl.program_id(0) == 0)
    def _():
        gain_out[...] = jnp.zeros_like(gain_out)

    v = v_ref[...].astype(F32)
    grad = normed_ref[...].astype(F32)
    inv_rms = lax.rsqrt(jnp.mean(v * v, axis=1, keepdims=True) + epsilon)
    weighted = grad * gain_ref[...]
    mean_term = jnp.mean(weighted * v, axis=1, keepdims=True)
    total = out_ref[...] + inv_rms * weighted - v * (inv_rms * inv_rms * inv_rms * mean_term)
    total_ref[...] = total
    low_ref[...] = total.astype(BF16)
    gain_out[...] += jnp.sum(grad * (v * inv_rms), axis=0, keepdims=True)


def norm_back(v, gain, grad_normed, grad_out):
    rows, depth = v.shape
    chunk = rows // 11 if rows % 176 == 0 else rows
    block = pl.BlockSpec((chunk, depth), lambda i: (i, 0))
    line = pl.BlockSpec((1, depth), lambda i: (0, 0))
    return pl.pallas_call(
        norm_back_kernel,
        grid=(rows // chunk,),
        in_specs=[block, line, block, block],
        out_specs=[block, block, line],
        out_shape=[
            jax.ShapeDtypeStruct((rows, depth), F32),
            jax.ShapeDtypeStruct((rows, depth), BF16),
            jax.ShapeDtypeStruct((1, depth), F32),
        ],
        compiler_params=pltpu.CompilerParams(vmem_limit_bytes=24 * 2**20),
        cost_estimate=lasting(4),
        name="norm_back",
    )(v, gain.reshape(1, depth), grad_normed, grad_out)


def scattered(grads, axes):
    return lax.optimization_barrier(
        lax.psum_scatter(grads, axes, scatter_dimension=0, tiled=True)
    )


def first_gather_kernel(
    rows_ref, gains_ref, w_ref, full_ref, gains_out, acting_ref, own_sem, gain_sems, sems
):
    dp = lax.axis_index("dp")
    seq = lax.axis_index("seq")
    low, high = lax.rem(seq, 2), seq // 2
    beside = high * 2 + 1 - low
    across = (1 - high) * 2 + low
    far = (1 - high) * 2 + 1 - low
    count = 8
    me = dp * 4 + seq
    height = w_ref.shape[0]
    pieces = 4
    wide = w_ref.shape[1] // pieces
    axes = ("dp", "seq")
    barrier = pltpu.get_barrier_semaphore()
    for step in range(1, count):
        pl.semaphore_signal(
            barrier,
            inc=1,
            device_id=group_device(axes, lax.rem(me + step, count)),
            device_id_type=MESH,
        )
    pl.semaphore_wait(barrier, count - 1)

    def cells(ref, owner_dp, owner_seq, p):
        first = pl.multiple_of((owner_dp * 4 + owner_seq) * height, height)
        return ref.at[pl.ds(first, height), pl.ds(p * wide, wide)]

    def copy(kind, p, owner_dp, owner_seq, device, own=False):
        here = w_ref.at[:, pl.ds(p * wide, wide)] if own else cells(full_ref, owner_dp, owner_seq, p)
        return pltpu.make_async_remote_copy(
            here,
            cells(full_ref, owner_dp, owner_seq, p),
            sems.at[0, kind, p],
            sems.at[1, kind, p],
            device_id=device,
            device_id_type=MESH,
        )

    to_beside, to_across, to_core = {"seq": beside}, {"seq": across}, {"dp": 1 - dp}
    keep = pltpu.make_async_copy(
        w_ref, full_ref.at[pl.ds(pl.multiple_of(me * height, height), height)], own_sem
    )

    def gain_copy(step, slot, device):
        return pltpu.make_async_remote_copy(
            gains_ref,
            gains_out.at[slot],
            gain_sems.at[0, step],
            gain_sems.at[1, step],
            device_id=group_device(axes, device),
            device_id_type=MESH,
        )

    for step in range(1, count):
        gain_copy(step, me, lax.rem(me + step, count)).start()
    for p in range(pieces):
        copy(0, p, dp, seq, to_beside, True).start()
        copy(1, (p + 2) % pieces, dp, seq, to_across, True).start()
    keep.start()
    for p in range(pieces):
        copy(3, p, dp, seq, to_core, True).start()
    gains_out[me] = gains_ref[...]
    for step in range(1, count):
        source = lax.rem(me - step + count, count)
        gain_copy(step, source, source).wait_recv()
    values = rows_ref[...].astype(F32)
    inv_rms = lax.rsqrt(jnp.mean(values * values, axis=1, keepdims=True) + epsilon)
    part = values.shape[1] // count
    for i in range(count):
        at = pl.ds(i * part, part)
        acting_ref[:, at] = (
            values[:, i * part : (i + 1) * part] * inv_rms * gains_out[i, 0:1, :]
        ).astype(BF16)
    for turn_index in range(pieces):
        p = turn_index
        copy(0, p, dp, beside, to_beside).wait_recv()
        if p < pieces // 2:
            copy(2, p, dp, beside, to_across).start()
        copy(4, p, dp, beside, to_core).start()
        p = (turn_index + 2) % pieces
        copy(1, p, dp, across, to_across).wait_recv()
        if p >= pieces // 2:
            copy(2, p, dp, across, to_beside).start()
        copy(5, p, dp, across, to_core).start()
    for p in (0, 2, 1, 3):
        copy(2, p, dp, far, to_across).wait_recv()
        copy(6, p, dp, far, to_core).start()
    for p in range(pieces):
        for kind, owner in ((3, seq), (4, beside), (5, across), (6, far)):
            copy(kind, p, 1 - dp, owner, to_core).wait_recv()
    keep.wait()
    for step in range(1, count):
        gain_copy(step, me, lax.rem(me + step, count)).wait_send()
    for p in range(pieces):
        copy(0, p, dp, seq, to_beside, True).wait_send()
        copy(1, p, dp, seq, to_across, True).wait_send()
        copy(3, p, dp, seq, to_core, True).wait_send()
        if p < pieces // 2:
            copy(2, p, dp, beside, to_across).wait_send()
        else:
            copy(2, p, dp, across, to_beside).wait_send()
        copy(4, p, dp, beside, to_core).wait_send()
        copy(5, p, dp, across, to_core).wait_send()
        copy(6, p, dp, far, to_core).wait_send()


def first_gather(rows, gains, w, identifier):
    whole = pl.BlockSpec(memory_space=pltpu.VMEM)
    far = pl.BlockSpec(memory_space=pltpu.HBM)
    return pl.pallas_call(
        first_gather_kernel,
        in_specs=[whole, whole, far],
        out_specs=[far, whole, whole],
        out_shape=[
            jax.ShapeDtypeStruct((8 * w.shape[0], w.shape[1]), BF16),
            jax.ShapeDtypeStruct((8,) + gains.shape, F32),
            jax.ShapeDtypeStruct(rows.shape, BF16),
        ],
        scratch_shapes=[
            pltpu.SemaphoreType.DMA,
            pltpu.SemaphoreType.DMA((2, 8)),
            pltpu.SemaphoreType.DMA((2, 7, 4)),
        ],
        compiler_params=pltpu.CompilerParams(
            collective_id=identifier, has_side_effects=True, vmem_limit_bytes=32 * 2**20
        ),
        name="first_gather",
        cost_estimate=lasting(42),
    )(rows, gains, w)


def gate_back_kernel(g_ref, w_ref, gate_ref, scanned_ref, input_ref, scan_ref, gate_out, skip_ref):
    grad = nn(g_ref[...], w_ref[...])
    gate = gate_ref[...].astype(F32)
    sig = sigmoid(gate)
    scan = grad * (gate * sig)
    scan_ref[...] = scan
    gate_out[...] = (grad * scanned_ref[...] * (sig * (1.0 + gate * (1.0 - sig)))).astype(BF16)
    skip_ref[...] = jnp.sum(scan * input_ref[...].astype(F32), axis=0, keepdims=True)


def gate_back(g, w, gate, gate_column, scanned, inputs, tile=256):
    rows, depth = g.shape
    width = scanned.shape[1]
    skip = gate_column // tile
    column = pl.BlockSpec((rows, tile), lambda j: (0, j))
    return pl.pallas_call(
        gate_back_kernel,
        grid=(width // tile,),
        in_specs=[
            pl.BlockSpec((rows, depth), lambda j: (0, 0)),
            pl.BlockSpec((depth, tile), lambda j: (0, j)),
            pl.BlockSpec((rows, tile), lambda j: (0, j + skip)),
            column,
            column,
        ],
        out_specs=[column, column, pl.BlockSpec((1, tile), lambda j: (0, j))],
        out_shape=[
            jax.ShapeDtypeStruct((rows, width), F32),
            jax.ShapeDtypeStruct((rows, width), BF16),
            jax.ShapeDtypeStruct((1, width), F32),
        ],
        compiler_params=pltpu.CompilerParams(vmem_limit_bytes=32 * 2**20),
        cost_estimate=lasting(6),
        name="gate_back",
    )(g, w, gate, scanned, inputs)


def ffn_forward(stream, gain, weights, identifier):
    acting = norm_forward(stream, gain).astype(BF16)
    gate, up, hidden_low = gate_up(acting, weights, 256)
    branch = matmul_sum([hidden_low], weights, 2 * hidden_low.shape[1], identifier)
    return (stream + branch.astype(F32), (acting, gate, up, hidden_low))


def shards(
    hidden,
    teacher,
    valid_length,
    mamba_norm,
    mamba_in,
    conv_kernel,
    conv_bias,
    select_weight,
    step_weight,
    step_bias,
    decay_log,
    skip_gain,
    mamba_out,
    attn_norm,
    attn_qkv,
    attn_out,
    first_norm,
    first_gate_up,
    first_down,
    second_norm,
    second_gate_up,
    second_down,
):
    def split(rows, *like):
        parts = []
        first = 0
        for shard in like:
            if len(shard.shape) == 3:
                height, groups, columns = shard.shape
                pieces = [
                    rows[:, first + columns * g : first + columns * (g + 1)] for g in range(groups)
                ]
                parts.append(jnp.stack(pieces).transpose(1, 0, 2).astype(F32))
                columns = columns * groups
            else:
                columns = shard.shape[1]
                parts.append(rows[:, first : first + columns].astype(F32))
            first += columns
        return parts

    rows_here = hidden.shape[1]
    model_width = hidden.shape[2]
    seq_count = lax.axis_size("seq")
    seq_place = lax.axis_index("seq")
    my_length = valid_length[lax.axis_index("dp")]
    positions = seq_place * rows_here + jnp.arange(rows_here, dtype=jnp.int32)
    valid_rows = (positions < my_length).astype(F32)[:, None]
    total_valid = jnp.sum(valid_length).astype(F32)
    total_slots = valid_length.shape[0] * rows_here * seq_count
    stream_zero = hidden[0].astype(F32)
    gains = jnp.stack([mamba_norm, attn_norm, first_norm, second_norm]).astype(F32)
    gains = jnp.pad(gains, ((0, 4), (0, 0)))
    split_four = lax.axis_size("dp") == 2 and seq_count == 4
    mixed = join(mamba_out, attn_qkv, attn_out)
    if split_four:
        gains, mixed = lax.optimization_barrier((gains, mixed))
        in_full, gains, acting_mamba = first_gather(hidden[0], gains, join(mamba_in), 2)
    else:
        gains = direct_gather(gains, ("dp", "seq"), 2)
        in_full = gather_joined(join(mamba_in))
    gain_mamba, gain_attn, gain_first, gain_second = (
        gains[:, which].reshape(model_width) for which in range(4)
    )
    mixed, in_full = lax.optimization_barrier((mixed, in_full))
    mixed_full = gather_joined(mixed)
    channels = mamba_out.shape[1]
    heads_width = attn_out.shape[1]
    qkv_column = channels
    attn_column = channels + 3 * heads_width
    if not split_four:
        acting_mamba = norm_forward(stream_zero, gain_mamba).astype(BF16)
    projected = product(acting_mamba, in_full).astype(BF16)
    ffn_shards = (first_gate_up, first_down, second_gate_up, second_down)
    ffn_shards, projected = lax.optimization_barrier((ffn_shards, projected))
    first_weights = gather_joined(join(*ffn_shards[:2]))
    second_weights = gather_joined(join(*ffn_shards[2:]))
    conv_input = projected[:, :channels]
    gate_input = projected[:, channels:].astype(F32)
    tap_count = conv_kernel.shape[0]
    edge_rows = shifted(conv_input[rows_here - (tap_count - 1) :], "seq", 1)
    padded = jnp.concatenate([edge_rows, conv_input], axis=0).astype(F32)
    conv_pre = conv_bias
    for tap_index in range(tap_count):
        conv_pre = conv_pre + conv_kernel[tap_index] * padded[tap_index : tap_index + rows_here]
    inputs_low = jax.nn.silu(conv_pre).astype(BF16)
    inputs = inputs_low.astype(F32)
    selected = tensor_forward_sum(product(inputs_low, select_weight))
    step_rank = step_weight.shape[0]
    states = decay_log.shape[0]
    step_in = selected[:, :step_rank].astype(BF16)
    input_map = selected[:, step_rank : step_rank + states]
    output_map = selected[:, step_rank + states :]
    step_pre = product(step_in, step_weight) + step_bias
    step_size = jax.nn.softplus(step_pre)
    decay_rate = -jnp.exp(decay_log)
    width = inputs.shape[1]
    run_state, run_scan, run_back_state, run_back = scan_calls(rows_here, width, states)
    rate_two = decay_rate * LOG2E
    in_wide = jnp.broadcast_to(input_map[:, :, None], (rows_here, states, 128))
    out_wide = jnp.broadcast_to(output_map[:, :, None], (rows_here, states, 128))
    moved = step_size * inputs
    end_state = run_state(step_size, moved, in_wide, rate_two)
    step_total = jnp.sum(step_size, axis=0, keepdims=True)
    ends = direct_gather(
        jnp.concatenate([end_state, step_total, jnp.zeros((7, width), F32)], axis=0), ("seq",), 3
    )
    decays = [jnp.exp2(rate_two * ends[place, states][None]) for place in range(seq_count)]
    start_state = jnp.zeros_like(end_state)
    for place in range(seq_count - 1):
        start_state = jnp.where(
            place < seq_place, decays[place] * start_state + ends[place, :states], start_state
        )
    scanned, kept_states = run_scan(step_size, moved, in_wide, out_wide, rate_two, start_state)
    scanned = scanned + skip_gain * inputs
    gate_silu = jax.nn.silu(gate_input)
    gated_low = (scanned * gate_silu).astype(BF16)
    stream_one = stream_zero + matmul_sum([gated_low], mixed_full, 0, 6).astype(F32)
    normed_attn = norm_forward(stream_one, gain_attn)
    acting_attn = normed_attn.astype(BF16)
    cosine, sine = rope_tables(positions)
    queries, own_kv = qkv_rows(acting_attn, mixed_full, qkv_column, heads_width, cosine, sine)
    hop_count = min(seq_count - 1, (WINDOW - 2) // rows_here + 1)
    attended, attended_low, log_sums, far_kv = attend(queries, own_kv, hop_count, 13)
    stream_two = stream_one + matmul_sum([attended_low], mixed_full, attn_column, 7).astype(F32)
    stream_three, first_saved = ffn_forward(stream_two, gain_first, first_weights, 8)
    stream_four, second_saved = ffn_forward(stream_three, gain_second, second_weights, 8)
    residue = (stream_four - teacher[0].astype(F32)) * valid_rows
    local_loss = jnp.sum(residue * residue) / (model_width * total_valid)
    grad_four = residue * (total_slots / total_valid)
    acting, gate, up, hidden_low = second_saved
    grad_low = grad_four.astype(BF16)
    grad_gate, grad_up = hidden_back(grad_low, second_weights, gate, up, 256)
    second_parts = [(acting, grad_gate), (acting, grad_up), (grad_low, hidden_low)]
    grad_normed, second_grads = matmul_sum(
        [grad_gate, grad_up], second_weights, 0, 16, pairs=second_parts
    )
    second_grads = scattered(second_grads, ("dp", "seq"))
    grad_three, grad_low, grad_gain_second = norm_back(
        stream_three, gain_second, grad_normed, grad_four
    )
    acting, gate, up, hidden_low = first_saved
    grad_gate, grad_up = hidden_back(grad_low, first_weights, gate, up, 256)
    first_parts = [(acting, grad_gate), (acting, grad_up), (grad_low, hidden_low)]
    grad_normed, first_grads = matmul_sum(
        [grad_gate, grad_up], first_weights, 0, 16, pairs=first_parts
    )
    grad_two, grad_low_attn, grad_gain_first = norm_back(
        stream_two, gain_first, grad_normed, grad_three
    )
    grad_attended = product(grad_low_attn, mixed_full[:, attn_column:]).astype(BF16)
    grad_projected_attn = attend_back(
        queries, grad_attended, attended, log_sums, own_kv, far_kv, cosine, sine, 14
    )
    grad_projected_attn, second_grads = lax.optimization_barrier(
        (grad_projected_attn, second_grads)
    )
    first_grads = scattered(first_grads, ("dp", "seq"))
    attn_pairs = [(acting_attn, grad_projected_attn), (grad_low_attn, attended_low)]
    grad_normed_attn, attn_grads = matmul_sum(
        [grad_projected_attn], mixed_full, qkv_column, 10, pairs=attn_pairs
    )
    attn_grads = scattered(attn_grads, ("dp", "seq"))
    grad_one, grad_low_mamba, grad_gain_attn = norm_back(
        stream_one, gain_attn, grad_normed_attn, grad_two
    )
    second_both, second_down_grad = split(second_grads, second_gate_up, second_down)
    grad_scanned, grad_gate_low, grad_skip = gate_back(
        grad_low_mamba, mixed_full, projected, channels, scanned, inputs_low
    )
    incoming = run_back_state(step_size, grad_scanned, out_wide, rate_two)
    incomings = direct_gather(incoming, ("seq",), 4)
    arriving_grad = jnp.zeros_like(incoming)
    for place in reversed(range(1, seq_count)):
        arriving_grad = jnp.where(
            place > seq_place, incomings[place] + decays[place] * arriving_grad, arriving_grad
        )
    grad_sizes, grad_inputs_scan, grad_in_map, grad_out_map, grad_rates = run_back(
        step_size, inputs, grad_scanned, in_wide, out_wide, rate_two, kept_states, arriving_grad
    )
    grad_decay_log = grad_rates * decay_rate
    grad_inputs = grad_inputs_scan + grad_scanned * skip_gain
    grad_step_pre = grad_sizes * jax.nn.sigmoid(step_pre)
    grad_step_bias = jnp.sum(grad_step_pre, axis=0)
    grad_step_low = grad_step_pre.astype(BF16)
    grad_step_weight = product_tl(step_in, grad_step_low)
    grad_step_in = product_t(grad_step_low, step_weight)
    grad_selected = tensor_backward_sum(
        jnp.concatenate([grad_step_in, grad_in_map, grad_out_map], axis=1)
    ).astype(BF16)
    early_grads = weight_grads(
        [(grad_low_mamba, gated_low), (acting_mamba, grad_gate_low)], 256
    )
    grad_selected, first_grads, early_grads, second_both, second_down_grad = (
        lax.optimization_barrier(
            (grad_selected, first_grads, early_grads, second_both, second_down_grad)
        )
    )
    early_grads = scattered(early_grads, ("dp", "seq"))
    grad_select = product_tl(grad_selected, inputs_low)
    grad_inputs = grad_inputs + product_t(grad_selected, select_weight)
    grad_conv_pre = grad_inputs * silu_slope(conv_pre)
    grad_conv_bias = jnp.sum(grad_conv_pre, axis=0)
    grad_kernel = jnp.stack(
        [
            jnp.sum(padded[tap_index : tap_index + rows_here] * grad_conv_pre, axis=0)
            for tap_index in range(tap_count)
        ]
    )
    grad_padded = sum(
        (
            jnp.pad(
                conv_kernel[tap_index] * grad_conv_pre,
                ((tap_index, tap_count - 1 - tap_index), (0, 0)),
            )
            for tap_index in range(tap_count)
        )
    )
    back_edge = shifted(grad_padded[: tap_count - 1], "seq", -1)
    grad_conv_input = grad_padded[tap_count - 1 :] + jnp.pad(
        back_edge, ((rows_here - (tap_count - 1), 0), (0, 0))
    )
    grad_conv_low = grad_conv_input.astype(BF16)
    late_pairs = [(acting_mamba, grad_conv_low)]
    loose = (
        grad_kernel,
        grad_conv_bias[None],
        grad_step_bias[None],
        grad_skip,
        jnp.broadcast_to(local_loss, (1, width)),
        grad_gain_attn.reshape(-1, width),
        grad_gain_first.reshape(-1, width),
        grad_gain_second.reshape(-1, width),
    )
    loose_rows = sum(part.shape[0] for part in loose)
    loose_block = jnp.concatenate(
        loose + (jnp.zeros((-loose_rows % 16, width), F32),), axis=0
    ).astype(BF16)
    packed = (grad_select, grad_step_weight, grad_decay_log, loose_block)
    devices = lax.axis_size("dp") * seq_count
    packed_rows = sum(part.shape[0] for part in packed)
    each = -(-packed_rows // (16 * devices)) * 16
    blocks = jnp.concatenate(
        [part.astype(BF16) for part in packed]
        + [jnp.zeros((each * devices - packed_rows, width), BF16)],
        axis=0,
    ).reshape(devices, each, width)
    if split_four:
        grad_normed_mamba, summed, late_grads = matmul_sum(
            [grad_conv_low, grad_gate_low],
            in_full,
            0,
            11,
            small=blocks,
            pairs=late_pairs,
            scatter=True,
        )
    else:
        grad_normed_mamba, summed = matmul_sum(
            [grad_conv_low, grad_gate_low], in_full, 0, 11, small=blocks
        )
        late_grads = scattered(weight_grads(late_pairs, 256), ("dp", "seq"))
    input_grad, _, grad_gain_mamba = norm_back(stream_zero, gain_mamba, grad_normed_mamba, grad_one)
    summed = summed.reshape(devices * each, width).astype(F32)

    def unpack(rows, shapes):
        parts = []
        first = 0
        for part in shapes:
            parts.append(rows[first : first + part.shape[0]])
            first += part.shape[0]
        return parts

    sum_select, sum_step_weight, sum_decay_log, loose_sums = unpack(summed, packed)
    (
        sum_kernel,
        sum_conv_bias,
        sum_step_bias,
        sum_skip,
        sum_loss,
        sum_attn,
        sum_first,
        sum_second,
    ) = unpack(loose_sums, loose)
    loss_total = sum_loss[0, 0]
    sum_mamba = jnp.sum(direct_gather(grad_gain_mamba.reshape(8, -1), ("dp", "seq"), 5), axis=0)
    gain_rows = mamba_norm.shape[0]
    place = lax.axis_index("dp") * seq_count + seq_place
    grad_qkv, grad_attn_out = split(attn_grads, attn_qkv, attn_out)
    grad_out, gate_half = split(early_grads, mamba_out, mamba_in[:, 1])
    (conv_half,) = split(late_grads, mamba_in[:, 0])
    grad_in = jnp.stack([conv_half, gate_half], axis=1)
    grad_first_both, grad_first_down = split(first_grads, first_gate_up, first_down)

    def own(whole_gain):
        return lax.dynamic_slice_in_dim(whole_gain.reshape(-1), place * gain_rows, gain_rows)

    return (
        loss_total,
        stream_four.astype(BF16)[None],
        input_grad[None],
        own(sum_mamba),
        grad_in,
        sum_kernel,
        sum_conv_bias[0],
        sum_select.T,
        sum_step_weight,
        sum_step_bias[0],
        sum_decay_log,
        sum_skip[0],
        grad_out,
        own(sum_attn),
        grad_qkv,
        grad_attn_out,
        own(sum_first),
        grad_first_both,
        grad_first_down,
        own(sum_second),
        second_both,
        second_down_grad,
    )


def solution(mesh):
    placed = (
        P("dp", "seq", None),
        P("dp", "seq", None),
        P(),
        P(("dp", "seq")),
        P(("dp", "seq"), None, "tensor"),
        P(None, "tensor"),
        P("tensor"),
        P("tensor", None),
        P(None, "tensor"),
        P("tensor"),
        P(None, "tensor"),
        P("tensor"),
        P(("dp", "seq"), "tensor"),
        P(("dp", "seq")),
        P(("dp", "seq"), None, "tensor"),
        P(("dp", "seq"), "tensor"),
        P(("dp", "seq")),
        P(("dp", "seq"), None, "tensor"),
        P(("dp", "seq"), "tensor"),
        P(("dp", "seq")),
        P(("dp", "seq"), None, "tensor"),
        P(("dp", "seq"), "tensor"),
    )
    return jax.shard_map(
        shards,
        mesh=mesh,
        in_specs=placed,
        out_specs=(
            P(),
            P("dp", "seq", None),
            P("dp", "seq", None),
            P(("dp", "seq")),
            P(("dp", "seq"), None, "tensor"),
            P(None, "tensor"),
            P("tensor"),
            P("tensor", None),
            P(None, "tensor"),
            P("tensor"),
            P(None, "tensor"),
            P("tensor"),
            P(("dp", "seq"), "tensor"),
            P(("dp", "seq")),
            P(("dp", "seq"), None, "tensor"),
            P(("dp", "seq"), "tensor"),
            P(("dp", "seq")),
            P(("dp", "seq"), None, "tensor"),
            P(("dp", "seq"), "tensor"),
            P(("dp", "seq")),
            P(("dp", "seq"), None, "tensor"),
            P(("dp", "seq"), "tensor"),
        ),
        check_vma=False,
    )
```

```python
import functools

import jax
import jax.numpy as jnp
from jax import lax
from jax.experimental import pallas as pl
from jax.experimental.pallas import tpu as pltpu
from jax.sharding import PartitionSpec as P

HD = 64
WINDOW = 2048
F32 = jnp.float32
BF16 = jnp.bfloat16
MESH = pl.DeviceIdType.MESH
LOG2E = 1.4426950408889634
LN2 = 0.6931471805599453

epsilon = 1e-05


def lasting(microseconds):
    return pl.CostEstimate(flops=int(microseconds * 1e7), bytes_accessed=0, transcendentals=0)

head_groups = 2


def state_kernel(dt_ref, dtx_ref, b_ref, rate_ref, out_ref, *, wide, chunk):
    @pl.when(pl.program_id(0) == 0)
    def _():
        out_ref[...] = jnp.zeros_like(out_ref)
    for j in range(out_ref.shape[1] // wide):
        cols = pl.ds(j * wide, wide)
        rate = rate_ref[:, cols]
        def group(g, h):
            base = pl.multiple_of(g * 8, 8)
            dts = dt_ref[pl.ds(base, 8), cols]
            dtxs = dtx_ref[pl.ds(base, 8), cols]
            for r in range(8):
                b = b_ref[base + r]
                b = jnp.concatenate([b] * (wide // 128), axis=1)
                h = jnp.exp2(dts[r:r+1] * rate) * h + b * dtxs[r:r+1]
            return h
        out_ref[:, cols] = lax.fori_loop(0, chunk // 8, group, out_ref[:, cols])

def scan_kernel(dt_ref, dtx_ref, b_ref, c_ref, rate_ref, h0_ref, y_ref, hp_ref, h_ref, *, wide, chunk):
    @pl.when(pl.program_id(0) == 0)
    def _():
        h_ref[...] = h0_ref[...]
    for j in range(h_ref.shape[1] // wide):
        cols = pl.ds(j * wide, wide)
        rate = rate_ref[:, cols]
        def group(g, h):
            base = pl.multiple_of(g * 8, 8)
            dts = dt_ref[pl.ds(base, 8), cols]
            dtxs = dtx_ref[pl.ds(base, 8), cols]
            ys = []
            for r in range(8):
                b = jnp.concatenate([b_ref[base + r]] * (wide // 128), axis=1)
                c = jnp.concatenate([c_ref[base + r]] * (wide // 128), axis=1)
                hp_ref[base + r, :, cols] = h
                h = jnp.exp2(dts[r:r+1] * rate) * h + b * dtxs[r:r+1]
                ys.append(jnp.sum(c * h, axis=0, keepdims=True))
            y_ref[pl.ds(base, 8), cols] = jnp.concatenate(ys, axis=0)
            return h
        h_ref[:, cols] = lax.fori_loop(0, chunk // 8, group, h_ref[:, cols])

def back_state_kernel(dt_ref, g_ref, c_ref, rate_ref, out_ref, *, wide, chunk):
    @pl.when(pl.program_id(0) == 0)
    def _():
        out_ref[...] = jnp.zeros_like(out_ref)
    for j in range(out_ref.shape[1] // wide):
        cols = pl.ds(j * wide, wide)
        rate = rate_ref[:, cols]
        def group(g, carry):
            base = pl.multiple_of(chunk - 8 - g * 8, 8)
            dts = dt_ref[pl.ds(base, 8), cols]
            gs = g_ref[pl.ds(base, 8), cols]
            for r in reversed(range(8)):
                c = jnp.concatenate([c_ref[base + r]] * (wide // 128), axis=1)
                carry = jnp.exp2(dts[r:r+1] * rate) * (carry + c * gs[r:r+1])
            return carry
        out_ref[:, cols] = lax.fori_loop(0, chunk // 8, group, out_ref[:, cols])

def back_kernel(dt_ref, x_ref, g_ref, b_ref, c_ref, rate_ref, hp_ref, l0_ref,
                gdt_ref, gx_ref, gb_out, gc_out, grate_ref, l_ref, gb_ref, gc_ref, *, wide, chunk):
    @pl.when(pl.program_id(0) == 0)
    def _():
        l_ref[...] = l0_ref[...]
        grate_ref[...] = jnp.zeros_like(grate_ref)
    for j in range(l_ref.shape[1] // wide):
        cols = pl.ds(j * wide, wide)
        rate = rate_ref[:, cols]
        def fold(v):
            out = v[:, :128]
            for i in range(1, wide // 128):
                out = out + v[:, i * 128:(i + 1) * 128]
            return out
        def group(g, state):
            carry, grate = state
            base = pl.multiple_of(chunk - 8 - g * 8, 8)
            dts = dt_ref[pl.ds(base, 8), cols]
            xs = x_ref[pl.ds(base, 8), cols].astype(F32)
            gs = g_ref[pl.ds(base, 8), cols]
            dtxs = dts * xs
            sw = [None] * 8
            sb = [None] * 8
            for r in reversed(range(8)):
                b = jnp.concatenate([b_ref[base + r]] * (wide // 128), axis=1)
                c = jnp.concatenate([c_ref[base + r]] * (wide // 128), axis=1)
                dt = dts[r:r+1]
                dtx = dtxs[r:r+1]
                gr = gs[r:r+1]
                da = jnp.exp2(dt * rate)
                q = da * hp_ref[base + r, :, cols]
                h = q + b * dtx
                lam = c * gr + carry
                w = lam * q
                carry = lam * da
                gb = fold(lam * dtx)
                gc = fold(h * gr)
                if j == 0:
                    gb_ref[base + r] = gb
                    gc_ref[base + r] = gc
                else:
                    gb_ref[base + r] += gb
                    gc_ref[base + r] += gc
                grate = grate + w * dt
                sw[r] = jnp.sum(w * rate, axis=0, keepdims=True)
                sb[r] = jnp.sum(lam * b, axis=0, keepdims=True)
            sbs = jnp.concatenate(sb, axis=0)
            sws = jnp.concatenate(sw, axis=0)
            gdt_ref[pl.ds(base, 8), cols] = sws * LN2 + xs * sbs
            gx_ref[pl.ds(base, 8), cols] = dts * sbs
            return carry, grate
        carry, grate = lax.fori_loop(0, chunk // 8, group, (l_ref[:, cols], grate_ref[:, cols]))
        l_ref[:, cols] = carry
        grate_ref[:, cols] = grate
    gb_out[...] = jnp.sum(gb_ref[...], axis=2)
    gc_out[...] = jnp.sum(gc_ref[...], axis=2)


SCAN_WIDE = 512


def scan_calls(rows, width, states):
    chunk = max(c for c in range(8, 57, 8) if rows % c == 0)
    steps = rows // chunk
    lanes = 128
    row = pl.BlockSpec((chunk, width), lambda i: (i, 0))
    maps = pl.BlockSpec((chunk, states, lanes), lambda i: (i, 0, 0))
    whole = pl.BlockSpec((states, width), lambda i: (0, 0))
    kept = pl.BlockSpec((chunk, states, width), lambda i: (i, 0, 0))
    row_back = pl.BlockSpec((chunk, width), lambda i: (steps - 1 - i, 0))
    maps_back = pl.BlockSpec((chunk, states, lanes), lambda i: (steps - 1 - i, 0, 0))
    narrow_back = pl.BlockSpec((chunk, states), lambda i: (steps - 1 - i, 0))
    kept_back = pl.BlockSpec((chunk, states, width), lambda i: (steps - 1 - i, 0, 0))

    def shape(*sizes):
        return jax.ShapeDtypeStruct(sizes, F32)

    params = pltpu.CompilerParams(vmem_limit_bytes=40 * 2**20)
    sizes = dict(wide=min(SCAN_WIDE, width), chunk=chunk)
    carried = [pltpu.VMEM((states, width), F32)]
    cells = rows * width * states
    state = pl.pallas_call(
        functools.partial(state_kernel, **sizes),
        grid=(steps,),
        in_specs=[row, row, maps, whole],
        out_specs=whole,
        out_shape=shape(states, width),
        compiler_params=params,
        cost_estimate=lasting(7),
        name="scan_state",
    )
    scan = pl.pallas_call(
        functools.partial(scan_kernel, **sizes),
        grid=(steps,),
        in_specs=[row, row, maps, maps, whole, whole],
        out_specs=[row, kept],
        out_shape=[shape(rows, width), shape(rows, states, width)],
        scratch_shapes=carried,
        compiler_params=params,
        cost_estimate=lasting(18),
        name="scan_rows",
    )
    back_state = pl.pallas_call(
        functools.partial(back_state_kernel, **sizes),
        grid=(steps,),
        in_specs=[row_back, row_back, maps_back, whole],
        out_specs=whole,
        out_shape=shape(states, width),
        compiler_params=params,
        cost_estimate=lasting(7),
        name="scan_back_state",
    )
    back = pl.pallas_call(
        functools.partial(back_kernel, **sizes),
        grid=(steps,),
        in_specs=[row_back, row_back, row_back, maps_back, maps_back, whole, kept_back, whole],
        out_specs=[row_back, row_back, narrow_back, narrow_back, whole],
        out_shape=[
            shape(rows, width),
            shape(rows, width),
            shape(rows, states),
            shape(rows, states),
            shape(states, width),
        ],
        scratch_shapes=carried + [pltpu.VMEM((chunk, states, lanes), F32)] * 2,
        compiler_params=params,
        cost_estimate=lasting(36),
        name="scan_back",
    )
    return state, scan, back_state, back


def gather_kernel(block_ref, out_ref, send, recv, own, *, axes):
    sizes = [lax.axis_size(a) for a in axes]
    total = 1
    for size in sizes:
        total *= size
    me = lax.axis_index(axes[0])
    for a in axes[1:]:
        me = me * lax.axis_size(a) + lax.axis_index(a)

    def coordinates(index):
        found = {}
        for a, size in zip(reversed(axes), reversed(sizes)):
            found[a] = lax.rem(index, size)
            index = index // size
        return found

    barrier = pltpu.get_barrier_semaphore()
    for step in range(1, total):
        pl.semaphore_signal(
            barrier, inc=1, device_id=coordinates(lax.rem(me + step, total)), device_id_type=MESH
        )
    pl.semaphore_wait(barrier, total - 1)
    mine = pltpu.make_async_copy(block_ref, out_ref.at[me], own)
    mine.start()
    copies = []
    for step in range(1, total):
        copy = pltpu.make_async_remote_copy(
            block_ref,
            out_ref.at[me],
            send.at[step],
            recv.at[step],
            device_id=coordinates(lax.rem(me + step, total)),
            device_id_type=MESH,
        )
        copy.start()
        copies.append(copy)
    mine.wait()
    for step in range(1, total):
        source = lax.rem(me - step + total, total)
        pltpu.make_async_remote_copy(
            block_ref,
            out_ref.at[source],
            send.at[step],
            recv.at[step],
            device_id=coordinates(source),
            device_id_type=MESH,
        ).wait_recv()
    for copy in copies:
        copy.wait_send()


def direct_gather(block, axes, identifier):
    total = 1
    for a in axes:
        total *= lax.axis_size(a)
    whole = pl.BlockSpec(memory_space=pltpu.VMEM)
    return pl.pallas_call(
        functools.partial(gather_kernel, axes=axes),
        out_shape=jax.ShapeDtypeStruct((total,) + block.shape, block.dtype),
        in_specs=[whole],
        out_specs=whole,
        scratch_shapes=[
            pltpu.SemaphoreType.DMA((total,)),
            pltpu.SemaphoreType.DMA((total,)),
            pltpu.SemaphoreType.DMA,
        ],
        compiler_params=pltpu.CompilerParams(
            collective_id=identifier, has_side_effects=True, vmem_limit_bytes=24 * 2**20
        ),
        name="gather_" + "_".join(axes),
        cost_estimate=lasting(6),
    )(block)


def ar_kernel(x_ref, out_ref, a_buf, b_buf, s_buf, a_send, a_recv, b_send, b_recv, c_send, c_recv, *, pieces, rows, lag):
    z = lax.axis_index("tensor")
    size = lax.axis_size("tensor")
    half = size // 2
    inner = (z == half - 1) | (z == half)
    low = z < half
    outer_dev = jnp.where(low, half - 2, half + 1)
    inner_dev = jnp.where(low, half - 1, half)
    other = jnp.where(low, half, half - 1)
    barrier = pltpu.get_barrier_semaphore()

    def at(ref, k):
        return ref.at[pl.ds(k * rows, rows)]

    def send_a(k):
        return pltpu.make_async_remote_copy(at(x_ref, k), at(a_buf, k), a_send.at[k], a_recv.at[k], device_id={"tensor": inner_dev}, device_id_type=MESH)
    def send_b(k):
        return pltpu.make_async_remote_copy(at(s_buf, k), at(b_buf, k), b_send.at[k], b_recv.at[k], device_id={"tensor": other}, device_id_type=MESH)
    def send_c(k):
        return pltpu.make_async_remote_copy(at(out_ref, k), at(out_ref, k), c_send.at[k], c_recv.at[k], device_id={"tensor": outer_dev}, device_id_type=MESH)

    @pl.when(jnp.logical_not(inner))
    def _():
        pl.semaphore_signal(barrier, inc=1, device_id={"tensor": inner_dev}, device_id_type=MESH)
        pl.semaphore_wait(barrier, 1)
        for k in range(pieces):
            send_a(k).start()
        for k in range(pieces):
            send_c(k).wait_recv()
        for k in range(pieces):
            send_a(k).wait_send()

    @pl.when(inner)
    def _():
        pl.semaphore_signal(barrier, inc=1, device_id={"tensor": outer_dev}, device_id_type=MESH)
        pl.semaphore_signal(barrier, inc=1, device_id={"tensor": other}, device_id_type=MESH)
        pl.semaphore_wait(barrier, 2)
        for t in range(pieces + lag):
            if t < pieces:
                send_a(t).wait_recv()
                part = pl.ds(t * rows, rows)
                s_buf[part] = (x_ref[part].astype(F32) + a_buf[part].astype(F32)).astype(BF16)
                send_b(t).start()
            if t >= lag:
                k = t - lag
                send_b(k).wait_recv()
                part = pl.ds(k * rows, rows)
                out_ref[part] = (s_buf[part].astype(F32) + b_buf[part].astype(F32)).astype(BF16)
                send_c(k).start()
        for k in range(pieces):
            send_b(k).wait_send()
            send_c(k).wait_send()


def tensor_sum(partial_sum, pieces, identifier):
    rows, width = partial_sum.shape
    lag = min(3, pieces)
    whole = pl.BlockSpec(memory_space=pltpu.VMEM)
    return pl.pallas_call(
        functools.partial(ar_kernel, pieces=pieces, rows=rows // pieces, lag=lag),
        out_shape=jax.ShapeDtypeStruct((rows, width), BF16),
        in_specs=[whole],
        out_specs=whole,
        scratch_shapes=[pltpu.VMEM((rows, width), BF16)] * 3
        + [pltpu.SemaphoreType.DMA((pieces,))] * 6,
        compiler_params=pltpu.CompilerParams(
            collective_id=identifier, has_side_effects=True, vmem_limit_bytes=24 * 2**20
        ),
        name="tensor_sum",
        cost_estimate=lasting(16),
    )(partial_sum)


def shifted(block, axis, distance):
    devices = range(lax.axis_size(axis))
    route = [(i - distance, i) for i in devices if i - distance in devices]
    return lax.ppermute(block, axis, route)


def product(left, right):
    return jnp.dot(left, right, preferred_element_type=F32)


def product_t(left, right):
    return lax.dot_general(
        left, right, (((1,), (1,)), ((), ())), preferred_element_type=F32
    )


def product_tl(left, right):
    return lax.dot_general(
        left, right, (((0,), (0,)), ((), ())), preferred_element_type=F32
    )


def norm_forward(values, gain_vec):
    inv_rms = lax.rsqrt(jnp.mean(values * values, axis=-1, keepdims=True) + epsilon)
    return values * inv_rms * gain_vec


def silu_slope(values):
    sigmoid_val = jax.nn.sigmoid(values)
    return sigmoid_val * (1.0 + values * (1.0 - sigmoid_val))


def join(*matrices):
    rows = matrices[0].shape[0]
    return jnp.concatenate([matrix.reshape(rows, -1) for matrix in matrices], axis=1)


def gather_joined(joined):
    return lax.all_gather(joined, ("dp", "seq"), axis=0, tiled=True)


def tensor_forward_sum(partial_sum):
    rows, width = partial_sum.shape
    low = partial_sum.astype(BF16)
    if width % 128:
        padded = jnp.pad(low, ((0, 0), (0, -width % 128)))
        return tensor_sum(padded, 11, 1)[:, :width].astype(F32)
    return tensor_sum(low, 33, 0).astype(F32)


tensor_backward_sum = tensor_forward_sum


def nt(a, b):
    return lax.dot_general(a, b, (((1,), (1,)), ((), ())), preferred_element_type=F32)

def nn(a, b):
    return lax.dot_general(a, b, (((1,), (0,)), ((), ())), preferred_element_type=F32)

def tn(a, b):
    return lax.dot_general(a, b, (((0,), (0,)), ((), ())), preferred_element_type=F32)

def head_lanes(shape, head):
    lane = lax.broadcasted_iota(jnp.int32, shape, 1)
    return (lane >= HD) if head else (lane < HD)

def seen(shape, hop, rows, query_axis):
    if hop * rows - (rows - 1) >= 0 and hop * rows + rows - 1 < WINDOW:
        return None
    distance = hop * rows + lax.broadcasted_iota(jnp.int32, shape, query_axis) - lax.broadcasted_iota(jnp.int32, shape, 1 - query_axis)
    return (distance >= 0) & (distance < WINDOW)

def seq_greet(place, count):
    barrier = pltpu.get_barrier_semaphore()
    for step in range(1, count):
        pl.semaphore_signal(
            barrier, inc=1, device_id={"seq": lax.rem(place + step, count)}, device_id_type=MESH
        )
    pl.semaphore_wait(barrier, count - 1)


def attend_kernel(
    q_ref, kv_ref, acc_ref, low_ref, top_ref, far_ref, total_ref, send, recv, *, count, hop_count
):
    rows = q_ref.shape[0]
    pairs = top_ref.shape[0]
    place = lax.axis_index("seq")
    scale = LOG2E * HD**-0.5
    seq_greet(place, count)

    def move(hop, device):
        return pltpu.make_async_remote_copy(
            kv_ref,
            far_ref.at[hop - 1],
            send.at[hop - 1],
            recv.at[hop - 1],
            device_id={"seq": device},
            device_id_type=MESH,
        )

    for hop in range(1, hop_count + 1):

        @pl.when(place + hop < count)
        def _(hop=hop):
            move(hop, place + hop).start()

    low = head_lanes((rows, 128), 0)

    def one_block(hop, pair):
        cols = pl.ds(pl.multiple_of(pair * 128, 128), 128)
        q = q_ref[:, cols]
        keys = kv_ref[0, :, cols] if hop == 0 else far_ref[hop - 1, 0, :, cols]
        values = kv_ref[1, :, cols] if hop == 0 else far_ref[hop - 1, 1, :, cols]
        mask = seen((rows, rows), hop, rows, 0)
        outs = []
        tops = []
        for head in range(2):
            mine = low if head == 0 else jnp.logical_not(low)
            s = nt(jnp.where(mine, q, jnp.zeros_like(q)), keys)
            if mask is not None:
                s = jnp.where(mask, s, -1e30)
            top = jnp.max(s, axis=1, keepdims=True)
            if hop > 0:
                top = jnp.maximum(top, top_ref[pair, :, pl.ds(head * HD, 1)])
            p = jnp.exp2((s - top) * scale).astype(BF16)
            outs.append(nn(p, jnp.where(mine, values, jnp.ones_like(values))))
            tops.append(top)
        top = jnp.where(low, tops[0], tops[1])
        acc = jnp.where(low, outs[0], outs[1])
        total = pltpu.roll(jnp.where(low, outs[1], outs[0]), HD, 1)
        if hop > 0:
            fade = jnp.exp2((top_ref[pair] - top) * scale)
            acc = acc + acc_ref[:, cols] * fade
            total = total + total_ref[pair] * fade
        acc_ref[:, cols] = acc
        top_ref[pair] = top
        total_ref[pair] = total

    def all_pairs(hop):
        def one(pair, carry):
            one_block(hop, pair)
            return carry

        lax.fori_loop(0, pairs, one, 0)

    all_pairs(0)
    for hop in range(1, hop_count + 1):

        @pl.when(place >= hop)
        def _(hop=hop):
            move(hop, place - hop).wait_recv()
            all_pairs(hop)

    def finish(pair, carry):
        cols = pl.ds(pl.multiple_of(pair * 128, 128), 128)
        total = total_ref[pair]
        acc = acc_ref[:, cols] / total
        acc_ref[:, cols] = acc
        low_ref[:, cols] = acc.astype(BF16)
        top_ref[pair] = top_ref[pair] * scale + jnp.log2(total)
        return carry

    lax.fori_loop(0, pairs, finish, 0)
    for hop in range(1, hop_count + 1):

        @pl.when(place + hop < count)
        def _(hop=hop):
            move(hop, place + hop).wait_send()


def attend(q, kv, hop_count, identifier):
    rows, width = q.shape
    pairs = width // 128
    whole = pl.BlockSpec(memory_space=pltpu.VMEM)
    return pl.pallas_call(
        functools.partial(attend_kernel, count=lax.axis_size("seq"), hop_count=hop_count),
        in_specs=[whole] * 2,
        out_specs=[whole] * 4,
        out_shape=[
            jax.ShapeDtypeStruct((rows, width), F32),
            jax.ShapeDtypeStruct((rows, width), BF16),
            jax.ShapeDtypeStruct((pairs, rows, 128), F32),
            jax.ShapeDtypeStruct((hop_count, 2, rows, width), BF16),
        ],
        scratch_shapes=[
            pltpu.VMEM((pairs, rows, 128), F32),
            pltpu.SemaphoreType.DMA((hop_count,)),
            pltpu.SemaphoreType.DMA((hop_count,)),
        ],
        compiler_params=pltpu.CompilerParams(
            collective_id=identifier, has_side_effects=True, vmem_limit_bytes=48 * 2**20
        ),
        cost_estimate=lasting(55),
        name="attend",
    )(q, kv)


def attend_back_kernel(
    q_ref,
    g_ref,
    o_ref,
    lse_ref,
    kv_ref,
    far_ref,
    cosine_ref,
    sine_ref,
    out_ref,
    lines,
    dq_ref,
    dkv_ref,
    leaving,
    landed,
    send,
    recv,
    *,
    count,
    hop_count,
):
    rows, width = q_ref.shape
    pairs = width // 128
    place = lax.axis_index("seq")
    scale = HD**-0.5
    seq_greet(place, count)

    def columns(pair):
        return pl.ds(pl.multiple_of(pair * 128, 128), 128)

    def move(hop, pair, device):
        return pltpu.make_async_remote_copy(
            leaving.at[hop - 1, :, :, columns(pair)],
            landed.at[hop - 1, :, :, columns(pair)],
            send.at[hop - 1, pair],
            recv.at[hop - 1, pair],
            device_id={"seq": device},
            device_id_type=MESH,
        )

    def prepare(pair, carry):
        cols = columns(pair)
        turned = jnp.transpose(lse_ref[pair])
        dots = jnp.transpose(o_ref[:, cols] * g_ref[:, cols].astype(F32))
        lines[pair, 0:1] = turned[0:1]
        lines[pair, 1:2] = turned[HD : HD + 1]
        lines[pair, 2:3] = jnp.sum(dots[:HD], axis=0, keepdims=True)
        lines[pair, 3:4] = jnp.sum(dots[HD:], axis=0, keepdims=True)
        dq_ref[:, cols] = jnp.zeros((rows, 128), F32)
        return carry

    lax.fori_loop(0, pairs, prepare, 0)

    def one_block(hop, pair):
        cols = columns(pair)
        q = q_ref[:, cols]
        g = g_ref[:, cols]
        k = kv_ref[0, :, cols] if hop == 0 else far_ref[hop - 1, 0, :, cols]
        v = kv_ref[1, :, cols] if hop == 0 else far_ref[hop - 1, 1, :, cols]
        mask = seen((rows, rows), hop, rows, 1)
        dk = jnp.zeros((rows, 128), F32)
        dv = jnp.zeros((rows, 128), F32)
        dq = dq_ref[:, cols]
        for head in range(2):
            mine = head_lanes((rows, 128), head)
            qm = jnp.where(mine, q, jnp.zeros_like(q))
            gm = jnp.where(mine, g, jnp.zeros_like(g))
            km = jnp.where(mine, k, jnp.zeros_like(k))
            s = nt(k, qm) * (LOG2E * scale)
            p = jnp.exp2(s - lines[pair, head : head + 1])
            if mask is not None:
                p = jnp.where(mask, p, 0.0)
            dv = dv + nn(p.astype(BF16), gm)
            dp = nt(v, gm)
            ds = (p * (dp - lines[pair, head + 2 : head + 3])).astype(BF16)
            dk = dk + nn(ds, qm)
            dq = dq + tn(ds, km) * scale
        dq_ref[:, cols] = dq
        return dk * scale, dv

    for hop in reversed(range(1, hop_count + 1)):

        @pl.when(place >= hop)
        def _(hop=hop):
            def one(pair, carry):
                dk, dv = one_block(hop, pair)
                leaving[hop - 1, 0, :, columns(pair)] = dk.astype(BF16)
                leaving[hop - 1, 1, :, columns(pair)] = dv.astype(BF16)
                move(hop, pair, place - hop).start()
                return carry

            lax.fori_loop(0, pairs, one, 0)

    def own(pair, carry):
        dk, dv = one_block(0, pair)
        dkv_ref[0, :, columns(pair)] = dk
        dkv_ref[1, :, columns(pair)] = dv
        return carry

    lax.fori_loop(0, pairs, own, 0)

    for hop in range(1, hop_count + 1):

        @pl.when(place + hop < count)
        def _(hop=hop):
            def one(pair, carry):
                cols = columns(pair)
                move(hop, pair, place + hop).wait_recv()
                for which in range(2):
                    dkv_ref[which, :, cols] += landed[hop - 1, which, :, cols].astype(F32)
                return carry

            lax.fori_loop(0, pairs, one, 0)

    def finish(pair, carry):
        cols = columns(pair)
        cosine, sine = cosine_ref[...], sine_ref[...]

        def turned(values):
            return turn(values.astype(BF16).astype(F32), cosine, sine, -1.0).astype(BF16)

        def later(part):
            return pl.ds(pl.multiple_of(part * width + pair * 128, 128), 128)

        out_ref[:, cols] = turned(dq_ref[:, cols])
        out_ref[:, later(1)] = turned(dkv_ref[0, :, cols])
        out_ref[:, later(2)] = dkv_ref[1, :, cols].astype(BF16)
        return carry

    lax.fori_loop(0, pairs, finish, 0)
    for hop in range(1, hop_count + 1):

        @pl.when(place >= hop)
        def _(hop=hop):
            def one(pair, carry):
                move(hop, pair, place - hop).wait_send()
                return carry

            lax.fori_loop(0, pairs, one, 0)


def attend_back(q, g, o, lse, kv, far, cosine, sine, identifier):
    rows, width = q.shape
    pairs = width // 128
    hop_count = far.shape[0]
    whole = pl.BlockSpec(memory_space=pltpu.VMEM)
    return pl.pallas_call(
        functools.partial(attend_back_kernel, count=lax.axis_size("seq"), hop_count=hop_count),
        in_specs=[whole] * 8,
        out_specs=whole,
        out_shape=jax.ShapeDtypeStruct((rows, 3 * width), BF16),
        scratch_shapes=[
            pltpu.VMEM((pairs, 8, rows), F32),
            pltpu.VMEM((rows, width), F32),
            pltpu.VMEM((2, rows, width), F32),
            pltpu.VMEM((hop_count, 2, rows, width), BF16),
            pltpu.VMEM((hop_count, 2, rows, width), BF16),
            pltpu.SemaphoreType.DMA((hop_count, pairs)),
            pltpu.SemaphoreType.DMA((hop_count, pairs)),
        ],
        compiler_params=pltpu.CompilerParams(
            collective_id=identifier, has_side_effects=True, vmem_limit_bytes=48 * 2**20
        ),
        cost_estimate=lasting(55),
        name="attend_back",
    )(q, g, o, lse, kv, far, cosine, sine)


def partners(values):
    lane = lax.broadcasted_iota(jnp.int32, values.shape, 1)
    half = HD // 2
    return jnp.where(
        lax.rem(lane, HD) < half, pltpu.roll(values, 128 - half, 1), pltpu.roll(values, half, 1)
    )


def turn(values, cosine, sine, sign):
    parts = []
    for first in range(0, values.shape[1], 128):
        piece = values[:, first : first + 128]
        parts.append(piece * cosine + partners(piece) * (sine * sign))
    return jnp.concatenate(parts, axis=1) if len(parts) > 1 else parts[0]


def rope_tables(positions):
    half = HD // 2
    frequency = 10000.0 ** (-jnp.arange(half, dtype=F32) / half)
    angles = positions.astype(F32)[:, None] * frequency[None, :]
    cosine, sine = jnp.cos(angles), jnp.sin(angles)
    return jnp.tile(cosine, (1, 4)), jnp.tile(jnp.concatenate([-sine, sine], axis=1), (1, 2))


def qkv_kernel(x_ref, w_ref, cosine_ref, sine_ref, q_ref, kv_ref, *, tiles):
    step = pl.program_id(0)
    result = nn(x_ref[...], w_ref[...])
    turned = turn(result, cosine_ref[...], sine_ref[...], 1.0)

    @pl.when(step < tiles)
    def _():
        q_ref[...] = turned.astype(BF16)

    @pl.when(step >= tiles)
    def _():
        kv_ref[0] = jnp.where(step < 2 * tiles, turned, result).astype(BF16)


def qkv_rows(x, w, first_column, width, cosine, sine):
    rows, depth = x.shape
    tile = 256
    tiles = width // tile
    skip = first_column // tile
    table = pl.BlockSpec((rows, 128), lambda j: (0, 0))

    def kv_at(j):
        later = jnp.maximum(j - tiles, 0)
        return later // tiles, 0, lax.rem(later, tiles)

    return pl.pallas_call(
        functools.partial(qkv_kernel, tiles=tiles),
        grid=(3 * tiles,),
        in_specs=[
            pl.BlockSpec((rows, depth), lambda j: (0, 0)),
            pl.BlockSpec((depth, tile), lambda j: (0, j + skip)),
            table,
            table,
        ],
        out_specs=[
            pl.BlockSpec((rows, tile), lambda j: (0, jnp.minimum(j, tiles - 1))),
            pl.BlockSpec((1, rows, tile), kv_at),
        ],
        out_shape=[
            jax.ShapeDtypeStruct((rows, width), BF16),
            jax.ShapeDtypeStruct((2, rows, width), BF16),
        ],
        compiler_params=pltpu.CompilerParams(vmem_limit_bytes=32 * 2**20),
        cost_estimate=lasting(8),
        name="qkv_rows",
    )(x, w, cosine, sine)


def sigmoid(v):
    return 1.0 / (1.0 + jnp.exp(-v))

def gate_up_kernel(x_ref, wg_ref, wu_ref, gate_ref, up_ref, hid_ref):
    x = x_ref[...]
    gate = nn(x, wg_ref[...])
    up = nn(x, wu_ref[...])
    gate_ref[...] = gate.astype(BF16)
    up_ref[...] = up.astype(BF16)
    hid_ref[...] = (gate * sigmoid(gate) * up).astype(BF16)

def gate_up(x, w, tile):
    rows, depth = x.shape
    units = w.shape[1] // 3
    steps = units // tile
    col = pl.BlockSpec((rows, tile), lambda j: (0, j))
    out = jax.ShapeDtypeStruct((rows, units), BF16)
    return pl.pallas_call(gate_up_kernel, grid=(steps,),
        in_specs=[pl.BlockSpec((rows, depth), lambda j: (0, 0)), pl.BlockSpec((depth, tile), lambda j: (0, j)), pl.BlockSpec((depth, tile), lambda j: (0, j + steps))],
        out_specs=[col] * 3, out_shape=[out] * 3, compiler_params=pltpu.CompilerParams(vmem_limit_bytes=40 * 2**20),
        cost_estimate=lasting(14), name="gate_up")(x, w, w)

def hidden_back_kernel(g_ref, w_ref, gate_ref, up_ref, gg_ref, gu_ref):
    gh = nn(g_ref[...], w_ref[...])
    gate = gate_ref[...].astype(F32)
    up = up_ref[...].astype(F32)
    sig = sigmoid(gate)
    gg_ref[...] = (gh * up * (sig * (1.0 + gate * (1.0 - sig)))).astype(BF16)
    gu_ref[...] = (gh * (gate * sig)).astype(BF16)

def hidden_back(g, w, gate, up, tile):
    rows, depth = g.shape
    units = w.shape[1] // 3
    steps = units // tile
    col = pl.BlockSpec((rows, tile), lambda j: (0, j))
    out = jax.ShapeDtypeStruct((rows, units), BF16)
    return pl.pallas_call(hidden_back_kernel, grid=(steps,),
        in_specs=[pl.BlockSpec((rows, depth), lambda j: (0, 0)), pl.BlockSpec((depth, tile), lambda j: (0, j + 2 * steps)), col, col],
        out_specs=[col] * 2, out_shape=[out] * 2, compiler_params=pltpu.CompilerParams(vmem_limit_bytes=40 * 2**20),
        cost_estimate=lasting(10), name="hidden_back")(g, w, gate, up)

def weight_grads_kernel(*refs, counts):
    n = len(counts)
    lhs, rhs, out_ref, turned = refs[:n], refs[n:2 * n], refs[2 * n], refs[2 * n + 1]
    step = pl.program_id(0)
    first = 0
    for which in range(n):
        @pl.when(step == first)
        def _():
            turned[...] = jnp.transpose(lhs[which][...])
        @pl.when((step >= first) & (step < first + counts[which]))
        def _():
            out_ref[...] = nn(turned[...], rhs[which][...]).astype(BF16)
        first += counts[which]

def weight_grads(pairs, tile):
    rows, depth = pairs[0][0].shape
    counts = [right.shape[1] // tile for _, right in pairs]
    total = sum(counts)
    starts = [sum(counts[:i]) for i in range(len(counts))]
    whole = pl.BlockSpec((rows, depth), lambda j: (0, 0))
    def spec(start, count):
        return pl.BlockSpec((rows, tile), lambda j: (0, jnp.clip(j - start, 0, count - 1)))
    return pl.pallas_call(functools.partial(weight_grads_kernel, counts=counts), grid=(total,),
        in_specs=[whole] * len(pairs) + [spec(s, c) for s, c in zip(starts, counts)],
        out_specs=pl.BlockSpec((depth, tile), lambda j: (0, j)),
        out_shape=jax.ShapeDtypeStruct((depth, total * tile), BF16),
        scratch_shapes=[pltpu.VMEM((depth, rows), BF16)],
        compiler_params=pltpu.CompilerParams(vmem_limit_bytes=40 * 2**20),
        cost_estimate=lasting(1.25 * total), name="weight_grads")(
        *[left for left, _ in pairs], *[right for _, right in pairs])

def group_place(axes):
    me = lax.axis_index(axes[0])
    for a in axes[1:]:
        me = me * lax.axis_size(a) + lax.axis_index(a)
    return me


def group_device(axes, index):
    found = {}
    for a in reversed(axes):
        found[a] = lax.rem(index, lax.axis_size(a))
        index = index // lax.axis_size(a)
    return found


class SmallSum:
    axes = ("dp", "seq")

    def __init__(self, x_ref, out_ref, arrived, total, send, recv, send_out, recv_out):
        self.x_ref, self.out_ref, self.arrived, self.total = x_ref, out_ref, arrived, total
        self.sems = (send, recv, send_out, recv_out)
        self.count = x_ref.shape[0]
        self.me = group_place(self.axes)

    def to(self, step):
        return lax.rem(self.me + step, self.count)

    def back(self, step):
        return lax.rem(self.me - step + self.count, self.count)

    def greet(self, barrier):
        for step in range(1, self.count):
            pl.semaphore_signal(
                barrier,
                inc=1,
                device_id=group_device(self.axes, self.to(step)),
                device_id_type=MESH,
            )
        return self.count - 1

    def part(self, step, device):
        return pltpu.make_async_remote_copy(
            self.x_ref.at[device],
            self.arrived.at[step],
            self.sems[0].at[step],
            self.sems[1].at[step],
            device_id=group_device(self.axes, device),
            device_id_type=MESH,
        )

    def whole(self, step, slot, device):
        return pltpu.make_async_remote_copy(
            self.total,
            self.out_ref.at[slot],
            self.sems[2].at[step],
            self.sems[3].at[step],
            device_id=group_device(self.axes, device),
            device_id_type=MESH,
        )

    def begin(self):
        for step in range(1, self.count):
            self.part(step, self.to(step)).start()

    def middle(self):
        result = self.x_ref[self.me].astype(F32)
        for step in range(1, self.count):
            self.part(step, self.back(step)).wait_recv()
            result = result + self.arrived[step].astype(F32)
        self.total[...] = result.astype(BF16)
        self.out_ref[self.me] = result.astype(BF16)
        for step in range(1, self.count):
            self.whole(step, self.me, self.to(step)).start()

    def end(self):
        for step in range(1, self.count):
            self.whole(step, self.back(step), self.back(step)).wait_recv()
        for step in range(1, self.count):
            self.part(step, self.to(step)).wait_send()
            self.whole(step, self.me, self.to(step)).wait_send()


class OwnGrads:
    lag = 0

    def __init__(self, lefts, rights, uses, counts, tile, out_ref, scratch):
        self.lefts, self.rights, self.uses, self.counts, self.tile = lefts, rights, uses, counts, tile
        self.out_ref = out_ref
        self.turned, self.staged, self.out_sem = scratch
        self.total = sum(counts)

    @staticmethod
    def scratch(rows, depth, total, tile):
        return [
            pltpu.VMEM((depth, rows), BF16),
            pltpu.VMEM((2, depth, tile), BF16),
            pltpu.SemaphoreType.DMA((2,)),
        ]

    def put(self, t):
        slot = lax.rem(t, 2)
        return pltpu.make_async_copy(
            self.staged.at[slot],
            self.out_ref.at[:, pl.ds(pl.multiple_of(t * self.tile, self.tile), self.tile)],
            self.out_sem.at[slot],
        )

    def turn(self, which):
        self.turned[...] = jnp.transpose(self.lefts[self.uses[which]][...])

    def step(self, t):
        first = 0
        for which, count in enumerate(self.counts):
            if which == 0 or self.uses[which] != self.uses[which - 1]:

                @pl.when(t == first)
                def _(which=which):
                    self.turn(which)

            @pl.when((t >= first) & (t < first + count))
            def _(which=which, first=first):
                self.multiply(which, t - first, t)

            first += count

    def greet(self, barrier):
        return 0

    def multiply(self, which, index, t):
        slot = lax.rem(t, 2)
        block = self.rights[which][:, pl.ds(pl.multiple_of(index * self.tile, self.tile), self.tile)]

        @pl.when(t >= 2)
        def _():
            self.put(t - 2).wait()

        self.staged[slot] = nn(self.turned[...], block).astype(BF16)
        self.put(t).start()

    def end(self):
        for t in (self.total - 2, self.total - 1):
            self.put(t).wait()


class ScatterGrads(OwnGrads):
    lags = (1, 3, 5)
    lag = 5

    def __init__(self, lefts, rights, uses, counts, tile, out_ref, scratch):
        self.lefts, self.rights, self.uses, self.counts, self.tile = lefts, rights, uses, counts, tile
        self.out_ref = out_ref
        self.turned, self.sent, self.kept, self.landed, self.crossed, self.last = scratch[:6]
        self.sems = scratch[6:]
        self.total = sum(counts)
        self.dp = lax.axis_index("dp")
        place = lax.axis_index("seq")
        self.low, self.high = lax.rem(place, 2), place // 2
        self.beside = self.high * 2 + 1 - self.low
        self.across = (1 - self.high) * 2 + self.low
        self.half = self.turned.shape[0] // 2
        self.block = self.half // 4

    @staticmethod
    def scratch(rows, depth, total, tile):
        half = depth // 2
        return [
            pltpu.VMEM((depth, rows), BF16),
            pltpu.VMEM((2, half, tile), BF16),
            pltpu.VMEM((3, half, tile), F32),
            pltpu.VMEM((total, half, tile), BF16),
            pltpu.VMEM((total, 2, half // 4, tile), BF16),
            pltpu.VMEM((total, half // 4, tile), BF16),
            pltpu.SemaphoreType.DMA((2, total)),
            pltpu.SemaphoreType.DMA((total, 2)),
            pltpu.SemaphoreType.DMA((total, 2)),
            pltpu.SemaphoreType.DMA((total,)),
            pltpu.SemaphoreType.DMA((total,)),
        ]

    def greet(self, barrier):
        for device in ({"dp": 1 - self.dp}, {"seq": self.beside}, {"seq": self.across}):
            pl.semaphore_signal(barrier, inc=1, device_id=device, device_id_type=MESH)
        return 3

    def part(self, which):
        return self.turned[pl.ds(pl.multiple_of(which * self.half, self.half), self.half)]

    def to_core(self, t):
        return pltpu.make_async_remote_copy(
            self.sent.at[lax.rem(t, 2)],
            self.landed.at[t],
            self.sems[0].at[0, t],
            self.sems[0].at[1, t],
            device_id={"dp": 1 - self.dp},
            device_id_type=MESH,
        )

    def rows(self, index):
        return pl.ds(pl.multiple_of(index * self.block, self.block), self.block)

    def even(self, t, if_even, if_odd):
        return jnp.where(lax.rem(t, 2) == 0, if_even, if_odd)

    def to_first(self, t, k):
        index = self.even(t, 2 * k + 1 - self.low, (1 - self.high) * 2 + k)
        return pltpu.make_async_remote_copy(
            self.landed.at[t, self.rows(index)],
            self.crossed.at[t, k],
            self.sems[1].at[t, k],
            self.sems[2].at[t, k],
            device_id={"seq": self.even(t, self.beside, self.across)},
            device_id_type=MESH,
        )

    def to_second(self, t):
        return pltpu.make_async_remote_copy(
            self.crossed.at[t, self.even(t, 1 - self.high, 1 - self.low)],
            self.last.at[t],
            self.sems[3].at[t],
            self.sems[4].at[t],
            device_id={"seq": self.even(t, self.across, self.beside)},
            device_id_type=MESH,
        )

    def multiply(self, which, index, t):
        slot = lax.rem(t, 2)
        block = self.rights[which][:, pl.ds(pl.multiple_of(index * self.tile, self.tile), self.tile)]

        @pl.when(t >= 2)
        def _():
            self.to_core(t - 2).wait_send()

        self.sent[slot] = nn(self.part(1 - self.dp), block).astype(BF16)
        self.to_core(t).start()
        self.kept[lax.rem(t, 3)] = nn(self.part(self.dp), block)

    def core_sum(self, t):
        self.to_core(t).wait_recv()
        self.landed[t] = (self.kept[lax.rem(t, 3)] + self.landed[t].astype(F32)).astype(BF16)
        for k in range(2):
            self.to_first(t, k).start()

    def first_chip_sum(self, t):
        for k in range(2):
            self.to_first(t, k).wait_recv()
            index = self.even(t, 2 * k + self.low, self.high * 2 + k)
            own = self.landed[t, self.rows(index)].astype(F32)
            self.crossed[t, k] = (own + self.crossed[t, k].astype(F32)).astype(BF16)
        self.to_second(t).start()

    def second_chip_sum(self, t):
        self.to_second(t).wait_recv()
        own = self.crossed[t, self.even(t, self.high, self.low)].astype(F32)
        self.out_ref[:, pl.ds(pl.multiple_of(t * self.tile, self.tile), self.tile)] = (
            own + self.last[t].astype(F32)
        ).astype(BF16)

    def step(self, t):
        super().step(t)
        works = (self.core_sum, self.first_chip_sum, self.second_chip_sum)
        for late, work in zip(self.lags, works):

            @pl.when((t >= late) & (t < self.total + late))
            def _(late=late, work=work):
                work(t - late)

    def end(self):
        for t in (self.total - 2, self.total - 1):
            self.to_core(t).wait_send()

        def finish(t, carry):
            for k in range(2):
                self.to_first(t, k).wait_send()
            self.to_second(t).wait_send()
            return carry

        lax.fori_loop(0, self.total, finish, 0)


def grad_operands(pairs, xs):
    lefts, uses = [], []
    for left, _ in pairs:
        known = [i for i, other in enumerate(lefts) if other is left]
        uses.append(known[0] if known else len(lefts))
        if not known:
            lefts.append(left)
    shared = []
    rights = []
    for _, right in pairs:
        same = [i for i, x in enumerate(xs) if x is right]
        shared.append(same[0] if same else -1)
        if not same:
            rights.append(right)
    return lefts, rights, uses, shared


def matmul_sum_kernel(
    *refs, columns, first_column, tile, splits, with_small, uses, shared, counts, job_kind
):
    refs = list(refs)

    def take(count):
        taken = refs[:count]
        del refs[:count]
        return taken

    xs = take(len(columns))
    (w_ref,) = take(1)
    small_in = take(1 if with_small else 0)
    lefts = take(max(uses) + 1 if uses else 0)
    others = take(sum(which < 0 for which in shared))
    rights = [xs[which] if which >= 0 else others.pop(0) for which in shared]
    (out_ref,) = take(1)
    small_out = take(1 if with_small else 0)
    grads_out = take(1 if uses else 0)
    w_buf, part, a_buf, b_buf, w_sem, a_send, a_recv, b_send, b_recv, c_send, c_recv = take(11)
    small = SmallSum(*small_in, *small_out, *take(6)) if with_small else None
    job = None
    if uses:
        job = job_kind(lefts, rights, uses, counts, tile, *grads_out, refs)
    rows, depth = out_ref.shape
    tiles = depth // tile
    short = rows // splits
    wide = sum(columns)
    z = lax.axis_index("tensor")
    half = lax.axis_size("tensor") // 2
    inner = (z == half - 1) | (z == half)
    low = z < half
    outer_dev = jnp.where(low, half - 2, half + 1)
    inner_dev = jnp.where(low, half - 1, half)
    other = jnp.where(low, half, half - 1)
    barrier = pltpu.get_barrier_semaphore()

    def weights(j, slot):
        return pltpu.make_async_copy(
            w_ref.at[pl.ds(pl.multiple_of(j * tile, tile), tile), pl.ds(first_column, wide)],
            w_buf.at[slot],
            w_sem.at[slot],
        )

    def cells(ref, j, r):
        return ref.at[pl.ds(r * short, short), pl.ds(pl.multiple_of(j * tile, tile), tile)]

    def send(src, dst, sems, j, r, device):
        return pltpu.make_async_remote_copy(
            cells(src, j, r),
            cells(dst, j, r),
            sems[0].at[j, r],
            sems[1].at[j, r],
            device_id={"tensor": device},
            device_id_type=MESH,
        )

    def send_a(j, r):
        return send(part, a_buf, (a_send, a_recv), j, r, inner_dev)

    def send_b(j, r):
        return send(part, b_buf, (b_send, b_recv), j, r, other)

    def send_c(j, r):
        return send(out_ref, out_ref, (c_send, c_recv), j, r, outer_dev)

    weights(0, 0).start()
    greeted = (small.greet(barrier) if with_small else 0) + (job.greet(barrier) if uses else 0)

    @pl.when(jnp.logical_not(inner))
    def _():
        pl.semaphore_signal(barrier, inc=1, device_id={"tensor": inner_dev}, device_id_type=MESH)
        pl.semaphore_wait(barrier, 1 + greeted)

    @pl.when(inner)
    def _():
        pl.semaphore_signal(barrier, inc=1, device_id={"tensor": outer_dev}, device_id_type=MESH)
        pl.semaphore_signal(barrier, inc=1, device_id={"tensor": other}, device_id_type=MESH)
        pl.semaphore_wait(barrier, 2 + greeted)

    if with_small:
        small.begin()

    def first_sum(j, r):
        send_a(j, r).wait_recv()
        mine = cells(part, j, r)
        mine[...] = (mine[...].astype(F32) + cells(a_buf, j, r)[...].astype(F32)).astype(BF16)
        send_b(j, r).start()

    def second_sum(j, r):
        send_b(j, r).wait_recv()
        cells(out_ref, j, r)[...] = (
            cells(part, j, r)[...].astype(F32) + cells(b_buf, j, r)[...].astype(F32)
        ).astype(BF16)
        send_c(j, r).start()

    lag = splits - 1

    def one_tile(j, carry):
        slot = lax.rem(j, 2)
        weights(j, slot).wait()

        @pl.when(j + 1 < tiles)
        def _():
            weights(j + 1, 1 - slot).start()

        total = None
        first = 0
        for x_ref, count in zip(xs, columns):
            term = nt(x_ref[...], w_buf[slot, :, pl.ds(first, count)])
            total = term if total is None else total + term
            first += count
        part[:, pl.ds(pl.multiple_of(j * tile, tile), tile)] = total.astype(BF16)

        @pl.when(jnp.logical_not(inner))
        def _():
            for r in range(splits):
                send_a(j, r).start()

        each = (job.total + job.lag) // tiles if uses else 0
        for r in range(max(splits, each)):
            if r < splits:

                @pl.when(inner)
                def _(r=r):
                    first_sum(j, r)
                    if r >= lag:
                        second_sum(j, r - lag)
                    else:

                        @pl.when(j > 0)
                        def _():
                            second_sum(j - 1, r + splits - lag)

            if r < each:
                job.step(j * each + r)

        return carry

    if with_small:
        lax.fori_loop(0, tiles // 2, one_tile, 0)
        small.middle()
        lax.fori_loop(tiles // 2, tiles, one_tile, 0)
    else:
        lax.fori_loop(0, tiles, one_tile, 0)

    @pl.when(inner)
    def _():
        for r in range(splits - lag, splits):
            second_sum(tiles - 1, r)

    if uses:
        for t in range((job.total + job.lag) // tiles * tiles, job.total + job.lag):
            job.step(t)

    @pl.when(inner)
    def _():

        def finish(j, carry):
            for r in range(splits):
                send_b(j, r).wait_send()
                send_c(j, r).wait_send()
            return carry

        lax.fori_loop(0, tiles, finish, 0)

    @pl.when(jnp.logical_not(inner))
    def _():
        def finish(j, carry):
            for r in range(splits):
                send_c(j, r).wait_recv()
                send_a(j, r).wait_send()
            return carry

        lax.fori_loop(0, tiles, finish, 0)

    if with_small:
        small.end()
    if uses:
        job.end()


def matmul_sum(
    xs, w, first_column, identifier, small=None, pairs=None, scatter=False, tile=256, splits=3
):
    rows = xs[0].shape[0]
    depth = w.shape[0]
    columns = [x.shape[1] for x in xs]
    wide = sum(columns)
    whole = pl.BlockSpec(memory_space=pltpu.VMEM)
    far = pl.BlockSpec(memory_space=pltpu.HBM)
    tiles = depth // tile
    out_shape = [jax.ShapeDtypeStruct((rows, depth), BF16)]
    out_specs = [whole]
    scratch = (
        [pltpu.VMEM((2, tile, wide), BF16)]
        + [pltpu.VMEM((rows, depth), BF16)] * 3
        + [pltpu.SemaphoreType.DMA((2,))]
        + [pltpu.SemaphoreType.DMA((tiles, splits))] * 6
    )
    extra = ()
    if small is not None:
        extra = (small,)
        out_shape.append(jax.ShapeDtypeStruct(small.shape, BF16))
        out_specs.append(whole)
        scratch += [pltpu.VMEM(small.shape, BF16), pltpu.VMEM(small.shape[1:], BF16)]
        scratch += [pltpu.SemaphoreType.DMA((small.shape[0],))] * 4
    uses, shared, counts, job_kind = (), (), (), None
    if pairs is not None:
        job_kind = ScatterGrads if scatter else OwnGrads
        lefts, rights, uses, shared = grad_operands(pairs, xs)
        counts = [right.shape[1] // tile for _, right in pairs]
        extra = (*extra, *lefts, *rights)
        height = depth // 8 if scatter else depth
        out_shape.append(jax.ShapeDtypeStruct((height, sum(counts) * tile), BF16))
        out_specs.append(whole if scatter else far)
        scratch += job_kind.scratch(rows, depth, sum(counts), tile)
    results = pl.pallas_call(
        functools.partial(
            matmul_sum_kernel,
            columns=columns,
            first_column=first_column,
            tile=tile,
            splits=splits,
            with_small=small is not None,
            uses=uses,
            shared=shared,
            counts=counts,
            job_kind=job_kind,
        ),
        out_shape=out_shape,
        in_specs=[whole] * len(xs) + [far] + [whole] * len(extra),
        out_specs=out_specs,
        scratch_shapes=scratch,
        compiler_params=pltpu.CompilerParams(
            collective_id=identifier, has_side_effects=True, vmem_limit_bytes=(40 if pairs is None else 44) * 2**20
        ),
        cost_estimate=lasting(58 if pairs is None else 67),
        name="matmul_sum" + ("_small" if small is not None else "_grads" if uses else ""),
    )(*xs, w, *extra)
    return results if extra else results[0]


def norm_back_kernel(v_ref, gain_ref, normed_ref, out_ref, total_ref, low_ref, gain_out):
    @pl.when(pl.program_id(0) == 0)
    def _():
        gain_out[...] = jnp.zeros_like(gain_out)

    v = v_ref[...].astype(F32)
    grad = normed_ref[...].astype(F32)
    inv_rms = lax.rsqrt(jnp.mean(v * v, axis=1, keepdims=True) + epsilon)
    weighted = grad * gain_ref[...]
    mean_term = jnp.mean(weighted * v, axis=1, keepdims=True)
    total = out_ref[...] + inv_rms * weighted - v * (inv_rms * inv_rms * inv_rms * mean_term)
    total_ref[...] = total
    low_ref[...] = total.astype(BF16)
    gain_out[...] += jnp.sum(grad * (v * inv_rms), axis=0, keepdims=True)


def norm_back(v, gain, grad_normed, grad_out):
    rows, depth = v.shape
    chunk = rows // 11 if rows % 176 == 0 else rows
    block = pl.BlockSpec((chunk, depth), lambda i: (i, 0))
    line = pl.BlockSpec((1, depth), lambda i: (0, 0))
    return pl.pallas_call(
        norm_back_kernel,
        grid=(rows // chunk,),
        in_specs=[block, line, block, block],
        out_specs=[block, block, line],
        out_shape=[
            jax.ShapeDtypeStruct((rows, depth), F32),
            jax.ShapeDtypeStruct((rows, depth), BF16),
            jax.ShapeDtypeStruct((1, depth), F32),
        ],
        compiler_params=pltpu.CompilerParams(vmem_limit_bytes=24 * 2**20),
        cost_estimate=lasting(4),
        name="norm_back",
    )(v, gain.reshape(1, depth), grad_normed, grad_out)


def scattered(grads, axes):
    return lax.optimization_barrier(
        lax.psum_scatter(grads, axes, scatter_dimension=0, tiled=True)
    )


def first_gather_kernel(
    rows_ref, gains_ref, w_ref, full_ref, gains_out, acting_ref, own_sem, gain_sems, sems
):
    dp = lax.axis_index("dp")
    seq = lax.axis_index("seq")
    low, high = lax.rem(seq, 2), seq // 2
    beside = high * 2 + 1 - low
    across = (1 - high) * 2 + low
    far = (1 - high) * 2 + 1 - low
    count = 8
    me = dp * 4 + seq
    height = w_ref.shape[0]
    pieces = 4
    wide = w_ref.shape[1] // pieces
    axes = ("dp", "seq")
    barrier = pltpu.get_barrier_semaphore()
    for step in range(1, count):
        pl.semaphore_signal(
            barrier,
            inc=1,
            device_id=group_device(axes, lax.rem(me + step, count)),
            device_id_type=MESH,
        )
    pl.semaphore_wait(barrier, count - 1)

    def cells(ref, owner_dp, owner_seq, p):
        first = pl.multiple_of((owner_dp * 4 + owner_seq) * height, height)
        return ref.at[pl.ds(first, height), pl.ds(p * wide, wide)]

    def copy(kind, p, owner_dp, owner_seq, device, own=False):
        here = w_ref.at[:, pl.ds(p * wide, wide)] if own else cells(full_ref, owner_dp, owner_seq, p)
        return pltpu.make_async_remote_copy(
            here,
            cells(full_ref, owner_dp, owner_seq, p),
            sems.at[0, kind, p],
            sems.at[1, kind, p],
            device_id=device,
            device_id_type=MESH,
        )

    to_beside, to_across, to_core = {"seq": beside}, {"seq": across}, {"dp": 1 - dp}
    keep = pltpu.make_async_copy(
        w_ref, full_ref.at[pl.ds(pl.multiple_of(me * height, height), height)], own_sem
    )

    def gain_copy(step, slot, device):
        return pltpu.make_async_remote_copy(
            gains_ref,
            gains_out.at[slot],
            gain_sems.at[0, step],
            gain_sems.at[1, step],
            device_id=group_device(axes, device),
            device_id_type=MESH,
        )

    for step in range(1, count):
        gain_copy(step, me, lax.rem(me + step, count)).start()
    for p in range(pieces):
        copy(0, p, dp, seq, to_beside, True).start()
        copy(1, (p + 2) % pieces, dp, seq, to_across, True).start()
    keep.start()
    for p in range(pieces):
        copy(3, p, dp, seq, to_core, True).start()
    gains_out[me] = gains_ref[...]
    for step in range(1, count):
        source = lax.rem(me - step + count, count)
        gain_copy(step, source, source).wait_recv()
    values = rows_ref[...].astype(F32)
    inv_rms = lax.rsqrt(jnp.mean(values * values, axis=1, keepdims=True) + epsilon)
    part = values.shape[1] // count
    for i in range(count):
        at = pl.ds(i * part, part)
        acting_ref[:, at] = (
            values[:, i * part : (i + 1) * part] * inv_rms * gains_out[i, 0:1, :]
        ).astype(BF16)
    for turn_index in range(pieces):
        p = turn_index
        copy(0, p, dp, beside, to_beside).wait_recv()
        if p < pieces // 2:
            copy(2, p, dp, beside, to_across).start()
        copy(4, p, dp, beside, to_core).start()
        p = (turn_index + 2) % pieces
        copy(1, p, dp, across, to_across).wait_recv()
        if p >= pieces // 2:
            copy(2, p, dp, across, to_beside).start()
        copy(5, p, dp, across, to_core).start()
    for p in (0, 2, 1, 3):
        copy(2, p, dp, far, to_across).wait_recv()
        copy(6, p, dp, far, to_core).start()
    for p in range(pieces):
        for kind, owner in ((3, seq), (4, beside), (5, across), (6, far)):
            copy(kind, p, 1 - dp, owner, to_core).wait_recv()
    keep.wait()
    for step in range(1, count):
        gain_copy(step, me, lax.rem(me + step, count)).wait_send()
    for p in range(pieces):
        copy(0, p, dp, seq, to_beside, True).wait_send()
        copy(1, p, dp, seq, to_across, True).wait_send()
        copy(3, p, dp, seq, to_core, True).wait_send()
        if p < pieces // 2:
            copy(2, p, dp, beside, to_across).wait_send()
        else:
            copy(2, p, dp, across, to_beside).wait_send()
        copy(4, p, dp, beside, to_core).wait_send()
        copy(5, p, dp, across, to_core).wait_send()
        copy(6, p, dp, far, to_core).wait_send()


def first_gather(rows, gains, w, identifier):
    whole = pl.BlockSpec(memory_space=pltpu.VMEM)
    far = pl.BlockSpec(memory_space=pltpu.HBM)
    return pl.pallas_call(
        first_gather_kernel,
        in_specs=[whole, whole, far],
        out_specs=[far, whole, whole],
        out_shape=[
            jax.ShapeDtypeStruct((8 * w.shape[0], w.shape[1]), BF16),
            jax.ShapeDtypeStruct((8,) + gains.shape, F32),
            jax.ShapeDtypeStruct(rows.shape, BF16),
        ],
        scratch_shapes=[
            pltpu.SemaphoreType.DMA,
            pltpu.SemaphoreType.DMA((2, 8)),
            pltpu.SemaphoreType.DMA((2, 7, 4)),
        ],
        compiler_params=pltpu.CompilerParams(
            collective_id=identifier, has_side_effects=True, vmem_limit_bytes=32 * 2**20
        ),
        name="first_gather",
        cost_estimate=lasting(42),
    )(rows, gains, w)


def gate_back_kernel(g_ref, w_ref, gate_ref, scanned_ref, input_ref, scan_ref, gate_out, skip_ref):
    grad = nn(g_ref[...], w_ref[...])
    gate = gate_ref[...].astype(F32)
    sig = sigmoid(gate)
    scan = grad * (gate * sig)
    scan_ref[...] = scan
    gate_out[...] = (grad * scanned_ref[...] * (sig * (1.0 + gate * (1.0 - sig)))).astype(BF16)
    skip_ref[...] = jnp.sum(scan * input_ref[...].astype(F32), axis=0, keepdims=True)


def gate_back(g, w, gate, gate_column, scanned, inputs, tile=256):
    rows, depth = g.shape
    width = scanned.shape[1]
    skip = gate_column // tile
    column = pl.BlockSpec((rows, tile), lambda j: (0, j))
    return pl.pallas_call(
        gate_back_kernel,
        grid=(width // tile,),
        in_specs=[
            pl.BlockSpec((rows, depth), lambda j: (0, 0)),
            pl.BlockSpec((depth, tile), lambda j: (0, j)),
            pl.BlockSpec((rows, tile), lambda j: (0, j + skip)),
            column,
            column,
        ],
        out_specs=[column, column, pl.BlockSpec((1, tile), lambda j: (0, j))],
        out_shape=[
            jax.ShapeDtypeStruct((rows, width), F32),
            jax.ShapeDtypeStruct((rows, width), BF16),
            jax.ShapeDtypeStruct((1, width), F32),
        ],
        compiler_params=pltpu.CompilerParams(vmem_limit_bytes=32 * 2**20),
        cost_estimate=lasting(6),
        name="gate_back",
    )(g, w, gate, scanned, inputs)


def ffn_forward(stream, gain, weights, identifier):
    acting = norm_forward(stream, gain).astype(BF16)
    gate, up, hidden_low = gate_up(acting, weights, 256)
    branch = matmul_sum([hidden_low], weights, 2 * hidden_low.shape[1], identifier)
    return (stream + branch.astype(F32), (acting, gate, up, hidden_low))


def shards(
    hidden,
    teacher,
    valid_length,
    mamba_norm,
    mamba_in,
    conv_kernel,
    conv_bias,
    select_weight,
    step_weight,
    step_bias,
    decay_log,
    skip_gain,
    mamba_out,
    attn_norm,
    attn_qkv,
    attn_out,
    first_norm,
    first_gate_up,
    first_down,
    second_norm,
    second_gate_up,
    second_down,
):
    def split(rows, *like):
        parts = []
        first = 0
        for shard in like:
            if len(shard.shape) == 3:
                height, groups, columns = shard.shape
                pieces = [
                    rows[:, first + columns * g : first + columns * (g + 1)] for g in range(groups)
                ]
                parts.append(jnp.stack(pieces).transpose(1, 0, 2).astype(F32))
                columns = columns * groups
            else:
                columns = shard.shape[1]
                parts.append(rows[:, first : first + columns].astype(F32))
            first += columns
        return parts

    rows_here = hidden.shape[1]
    model_width = hidden.shape[2]
    seq_count = lax.axis_size("seq")
    seq_place = lax.axis_index("seq")
    my_length = valid_length[lax.axis_index("dp")]
    positions = seq_place * rows_here + jnp.arange(rows_here, dtype=jnp.int32)
    valid_rows = (positions < my_length).astype(F32)[:, None]
    total_valid = jnp.sum(valid_length).astype(F32)
    total_slots = valid_length.shape[0] * rows_here * seq_count
    stream_zero = hidden[0].astype(F32)
    gains = jnp.stack([mamba_norm, attn_norm, first_norm, second_norm]).astype(F32)
    gains = jnp.pad(gains, ((0, 4), (0, 0)))
    split_four = lax.axis_size("dp") == 2 and seq_count == 4
    mixed = join(mamba_out, attn_qkv, attn_out)
    if split_four:
        gains, mixed = lax.optimization_barrier((gains, mixed))
        in_full, gains, acting_mamba = first_gather(hidden[0], gains, join(mamba_in), 2)
    else:
        gains = direct_gather(gains, ("dp", "seq"), 2)
        in_full = gather_joined(join(mamba_in))
    gain_mamba, gain_attn, gain_first, gain_second = (
        gains[:, which].reshape(model_width) for which in range(4)
    )
    mixed, in_full = lax.optimization_barrier((mixed, in_full))
    mixed_full = gather_joined(mixed)
    channels = mamba_out.shape[1]
    heads_width = attn_out.shape[1]
    qkv_column = channels
    attn_column = channels + 3 * heads_width
    if not split_four:
        acting_mamba = norm_forward(stream_zero, gain_mamba).astype(BF16)
    projected = product(acting_mamba, in_full).astype(BF16)
    ffn_shards = (first_gate_up, first_down, second_gate_up, second_down)
    ffn_shards, projected = lax.optimization_barrier((ffn_shards, projected))
    first_weights = gather_joined(join(*ffn_shards[:2]))
    second_weights = gather_joined(join(*ffn_shards[2:]))
    conv_input = projected[:, :channels]
    gate_input = projected[:, channels:].astype(F32)
    tap_count = conv_kernel.shape[0]
    edge_rows = shifted(conv_input[rows_here - (tap_count - 1) :], "seq", 1)
    padded = jnp.concatenate([edge_rows, conv_input], axis=0).astype(F32)
    conv_pre = conv_bias
    for tap_index in range(tap_count):
        conv_pre = conv_pre + conv_kernel[tap_index] * padded[tap_index : tap_index + rows_here]
    inputs_low = jax.nn.silu(conv_pre).astype(BF16)
    inputs = inputs_low.astype(F32)
    selected = tensor_forward_sum(product(inputs_low, select_weight))
    step_rank = step_weight.shape[0]
    states = decay_log.shape[0]
    step_in = selected[:, :step_rank].astype(BF16)
    input_map = selected[:, step_rank : step_rank + states]
    output_map = selected[:, step_rank + states :]
    step_pre = product(step_in, step_weight) + step_bias
    step_size = jax.nn.softplus(step_pre)
    decay_rate = -jnp.exp(decay_log)
    width = inputs.shape[1]
    run_state, run_scan, run_back_state, run_back = scan_calls(rows_here, width, states)
    rate_two = decay_rate * LOG2E
    in_wide = jnp.broadcast_to(input_map[:, :, None], (rows_here, states, 128))
    out_wide = jnp.broadcast_to(output_map[:, :, None], (rows_here, states, 128))
    moved = step_size * inputs
    end_state = run_state(step_size, moved, in_wide, rate_two)
    step_total = jnp.sum(step_size, axis=0, keepdims=True)
    ends = direct_gather(
        jnp.concatenate([end_state, step_total, jnp.zeros((7, width), F32)], axis=0), ("seq",), 3
    )
    decays = [jnp.exp2(rate_two * ends[place, states][None]) for place in range(seq_count)]
    start_state = jnp.zeros_like(end_state)
    for place in range(seq_count - 1):
        start_state = jnp.where(
            place < seq_place, decays[place] * start_state + ends[place, :states], start_state
        )
    scanned, kept_states = run_scan(step_size, moved, in_wide, out_wide, rate_two, start_state)
    scanned = scanned + skip_gain * inputs
    gate_silu = jax.nn.silu(gate_input)
    gated_low = (scanned * gate_silu).astype(BF16)
    stream_one = stream_zero + matmul_sum([gated_low], mixed_full, 0, 6).astype(F32)
    normed_attn = norm_forward(stream_one, gain_attn)
    acting_attn = normed_attn.astype(BF16)
    cosine, sine = rope_tables(positions)
    queries, own_kv = qkv_rows(acting_attn, mixed_full, qkv_column, heads_width, cosine, sine)
    hop_count = min(seq_count - 1, (WINDOW - 2) // rows_here + 1)
    attended, attended_low, log_sums, far_kv = attend(queries, own_kv, hop_count, 13)
    stream_two = stream_one + matmul_sum([attended_low], mixed_full, attn_column, 7).astype(F32)
    stream_three, first_saved = ffn_forward(stream_two, gain_first, first_weights, 8)
    stream_four, second_saved = ffn_forward(stream_three, gain_second, second_weights, 8)
    residue = (stream_four - teacher[0].astype(F32)) * valid_rows
    local_loss = jnp.sum(residue * residue) / (model_width * total_valid)
    grad_four = residue * (total_slots / total_valid)
    acting, gate, up, hidden_low = second_saved
    grad_low = grad_four.astype(BF16)
    grad_gate, grad_up = hidden_back(grad_low, second_weights, gate, up, 256)
    second_parts = [(acting, grad_gate), (acting, grad_up), (grad_low, hidden_low)]
    second_grads = weight_grads(second_parts, 256)
    grad_gate, grad_up, second_grads = lax.optimization_barrier((grad_gate, grad_up, second_grads))
    second_grads = scattered(second_grads, ("dp", "seq"))
    grad_normed = matmul_sum([grad_gate, grad_up], second_weights, 0, 9)
    grad_three, grad_low, grad_gain_second = norm_back(
        stream_three, gain_second, grad_normed, grad_four
    )
    acting, gate, up, hidden_low = first_saved
    grad_gate, grad_up = hidden_back(grad_low, first_weights, gate, up, 256)
    first_parts = [(acting, grad_gate), (acting, grad_up), (grad_low, hidden_low)]
    grad_normed, first_grads = matmul_sum(
        [grad_gate, grad_up], first_weights, 0, 16, pairs=first_parts
    )
    grad_two, grad_low_attn, grad_gain_first = norm_back(
        stream_two, gain_first, grad_normed, grad_three
    )
    grad_attended = product(grad_low_attn, mixed_full[:, attn_column:]).astype(BF16)
    grad_projected_attn = attend_back(
        queries, grad_attended, attended, log_sums, own_kv, far_kv, cosine, sine, 14
    )
    grad_projected_attn, second_grads, first_grads = lax.optimization_barrier(
        (grad_projected_attn, second_grads, first_grads)
    )
    first_grads = scattered(first_grads, ("dp", "seq"))
    second_both, second_down_grad = split(second_grads, second_gate_up, second_down)
    attn_pairs = [(acting_attn, grad_projected_attn), (grad_low_attn, attended_low)]
    grad_normed_attn, attn_grads = matmul_sum(
        [grad_projected_attn], mixed_full, qkv_column, 10, pairs=attn_pairs
    )
    grad_one, grad_low_mamba, grad_gain_attn = norm_back(
        stream_one, gain_attn, grad_normed_attn, grad_two
    )
    grad_scanned, grad_gate_low, grad_skip = gate_back(
        grad_low_mamba, mixed_full, projected, channels, scanned, inputs_low
    )
    incoming = run_back_state(step_size, grad_scanned, out_wide, rate_two)
    incomings = direct_gather(incoming, ("seq",), 4)
    arriving_grad = jnp.zeros_like(incoming)
    for place in reversed(range(1, seq_count)):
        arriving_grad = jnp.where(
            place > seq_place, incomings[place] + decays[place] * arriving_grad, arriving_grad
        )
    grad_sizes, grad_inputs_scan, grad_in_map, grad_out_map, grad_rates = run_back(
        step_size, inputs, grad_scanned, in_wide, out_wide, rate_two, kept_states, arriving_grad
    )
    grad_decay_log = grad_rates * decay_rate
    grad_inputs = grad_inputs_scan + grad_scanned * skip_gain
    grad_step_pre = grad_sizes * jax.nn.sigmoid(step_pre)
    grad_step_bias = jnp.sum(grad_step_pre, axis=0)
    grad_step_low = grad_step_pre.astype(BF16)
    grad_step_weight = product_tl(step_in, grad_step_low)
    grad_step_in = product_t(grad_step_low, step_weight)
    grad_selected = tensor_backward_sum(
        jnp.concatenate([grad_step_in, grad_in_map, grad_out_map], axis=1)
    ).astype(BF16)
    early_grads = weight_grads(
        [(grad_low_mamba, gated_low), (acting_mamba, grad_gate_low)], 256
    )
    grad_selected, first_grads, attn_grads, early_grads, second_both, second_down_grad = (
        lax.optimization_barrier(
            (grad_selected, first_grads, attn_grads, early_grads, second_both, second_down_grad)
        )
    )
    attn_grads = scattered(attn_grads, ("dp", "seq"))
    early_grads = scattered(early_grads, ("dp", "seq"))
    grad_select = product_tl(grad_selected, inputs_low)
    grad_inputs = grad_inputs + product_t(grad_selected, select_weight)
    grad_conv_pre = grad_inputs * silu_slope(conv_pre)
    grad_conv_bias = jnp.sum(grad_conv_pre, axis=0)
    grad_kernel = jnp.stack(
        [
            jnp.sum(padded[tap_index : tap_index + rows_here] * grad_conv_pre, axis=0)
            for tap_index in range(tap_count)
        ]
    )
    grad_padded = sum(
        (
            jnp.pad(
                conv_kernel[tap_index] * grad_conv_pre,
                ((tap_index, tap_count - 1 - tap_index), (0, 0)),
            )
            for tap_index in range(tap_count)
        )
    )
    back_edge = shifted(grad_padded[: tap_count - 1], "seq", -1)
    grad_conv_input = grad_padded[tap_count - 1 :] + jnp.pad(
        back_edge, ((rows_here - (tap_count - 1), 0), (0, 0))
    )
    grad_conv_low = grad_conv_input.astype(BF16)
    late_pairs = [(acting_mamba, grad_conv_low)]
    loose = (
        grad_kernel,
        grad_conv_bias[None],
        grad_step_bias[None],
        grad_skip,
        jnp.broadcast_to(local_loss, (1, width)),
        grad_gain_attn.reshape(-1, width),
        grad_gain_first.reshape(-1, width),
        grad_gain_second.reshape(-1, width),
    )
    loose_rows = sum(part.shape[0] for part in loose)
    loose_block = jnp.concatenate(
        loose + (jnp.zeros((-loose_rows % 16, width), F32),), axis=0
    ).astype(BF16)
    packed = (grad_select, grad_step_weight, grad_decay_log, loose_block)
    devices = lax.axis_size("dp") * seq_count
    packed_rows = sum(part.shape[0] for part in packed)
    each = -(-packed_rows // (16 * devices)) * 16
    blocks = jnp.concatenate(
        [part.astype(BF16) for part in packed]
        + [jnp.zeros((each * devices - packed_rows, width), BF16)],
        axis=0,
    ).reshape(devices, each, width)
    if split_four:
        grad_normed_mamba, summed, late_grads = matmul_sum(
            [grad_conv_low, grad_gate_low],
            in_full,
            0,
            11,
            small=blocks,
            pairs=late_pairs,
            scatter=True,
        )
    else:
        grad_normed_mamba, summed = matmul_sum(
            [grad_conv_low, grad_gate_low], in_full, 0, 11, small=blocks
        )
        late_grads = scattered(weight_grads(late_pairs, 256), ("dp", "seq"))
    input_grad, _, grad_gain_mamba = norm_back(stream_zero, gain_mamba, grad_normed_mamba, grad_one)
    summed = summed.reshape(devices * each, width).astype(F32)

    def unpack(rows, shapes):
        parts = []
        first = 0
        for part in shapes:
            parts.append(rows[first : first + part.shape[0]])
            first += part.shape[0]
        return parts

    sum_select, sum_step_weight, sum_decay_log, loose_sums = unpack(summed, packed)
    (
        sum_kernel,
        sum_conv_bias,
        sum_step_bias,
        sum_skip,
        sum_loss,
        sum_attn,
        sum_first,
        sum_second,
    ) = unpack(loose_sums, loose)
    loss_total = sum_loss[0, 0]
    sum_mamba = jnp.sum(direct_gather(grad_gain_mamba.reshape(8, -1), ("dp", "seq"), 5), axis=0)
    gain_rows = mamba_norm.shape[0]
    place = lax.axis_index("dp") * seq_count + seq_place
    grad_qkv, grad_attn_out = split(attn_grads, attn_qkv, attn_out)
    grad_out, gate_half = split(early_grads, mamba_out, mamba_in[:, 1])
    (conv_half,) = split(late_grads, mamba_in[:, 0])
    grad_in = jnp.stack([conv_half, gate_half], axis=1)
    grad_first_both, grad_first_down = split(first_grads, first_gate_up, first_down)

    def own(whole_gain):
        return lax.dynamic_slice_in_dim(whole_gain.reshape(-1), place * gain_rows, gain_rows)

    return (
        loss_total,
        stream_four.astype(BF16)[None],
        input_grad[None],
        own(sum_mamba),
        grad_in,
        sum_kernel,
        sum_conv_bias[0],
        sum_select.T,
        sum_step_weight,
        sum_step_bias[0],
        sum_decay_log,
        sum_skip[0],
        grad_out,
        own(sum_attn),
        grad_qkv,
        grad_attn_out,
        own(sum_first),
        grad_first_both,
        grad_first_down,
        own(sum_second),
        second_both,
        second_down_grad,
    )


def solution(mesh):
    placed = (
        P("dp", "seq", None),
        P("dp", "seq", None),
        P(),
        P(("dp", "seq")),
        P(("dp", "seq"), None, "tensor"),
        P(None, "tensor"),
        P("tensor"),
        P("tensor", None),
        P(None, "tensor"),
        P("tensor"),
        P(None, "tensor"),
        P("tensor"),
        P(("dp", "seq"), "tensor"),
        P(("dp", "seq")),
        P(("dp", "seq"), None, "tensor"),
        P(("dp", "seq"), "tensor"),
        P(("dp", "seq")),
        P(("dp", "seq"), None, "tensor"),
        P(("dp", "seq"), "tensor"),
        P(("dp", "seq")),
        P(("dp", "seq"), None, "tensor"),
        P(("dp", "seq"), "tensor"),
    )
    return jax.shard_map(
        shards,
        mesh=mesh,
        in_specs=placed,
        out_specs=(
            P(),
            P("dp", "seq", None),
            P("dp", "seq", None),
            P(("dp", "seq")),
            P(("dp", "seq"), None, "tensor"),
            P(None, "tensor"),
            P("tensor"),
            P("tensor", None),
            P(None, "tensor"),
            P("tensor"),
            P(None, "tensor"),
            P("tensor"),
            P(("dp", "seq"), "tensor"),
            P(("dp", "seq")),
            P(("dp", "seq"), None, "tensor"),
            P(("dp", "seq"), "tensor"),
            P(("dp", "seq")),
            P(("dp", "seq"), None, "tensor"),
            P(("dp", "seq"), "tensor"),
            P(("dp", "seq")),
            P(("dp", "seq"), None, "tensor"),
            P(("dp", "seq"), "tensor"),
        ),
        check_vma=False,
    )
```
